32 devices in a mesh: scen: 2 (over x), tm: 16 (over z, y, core).
Axes of the slice: x: 2, y: 2, z: 4, core: 2. Of those that a mesh axis runs over, the one named last changes fastest.
Arguments:
- base_injection: bfloat16 [32, 36864], P(('scen', 'tm')), parts along dimension 0, may hold values from -6 to 6
- ptdf_tiles: bfloat16 [128, 80, 128, 128], P(None, 'tm'), may hold values from -0.0625 to 0.0625
- tile_block: int32 [128, 80], P(None, 'tm'), may hold values from 0 to 17
- limits: float32 [16384], replicated, may hold values from 0.5 to 2
- stor_bus: int32 [2048], replicated, may hold values from 0 to 36863
- stor_gain: float32 [2048], replicated, may hold values from 0.5 to 4
- soc_init: float32 [32, 2048], P(('scen', 'tm')), parts along dimension 0, may hold values from 0 to 1
Outputs:
- injection: float32 [32, 36864], P(('scen', 'tm')), parts along dimension 0
- line_dual: float32 [32, 16384], P(('scen', 'tm')), parts along dimension 0
- level: float32 [32, 2048], P(('scen', 'tm')), parts along dimension 0
The draws below stay inside these ranges and needn't reach their ends.
There are 2 independent parts, one for each index of `scen`. The reference program is written for one: setup_inputs(seed, part) draws one part's arguments, and reference() takes and returns one part's arrays. A program takes and returns all parts, laid end to end along the dimension named above; an argument that names none is the same for every part. Nothing has to cross between parts.
All inputs are finite; a program needn't handle non-finite values.
Results may differ from the reference program's by a relative error of at most 0.012.
The reference program's roundings to bfloat16 on the way count: a program that leaves them out, or rounds other values in their place, can miss the bound.
Values may be sent and summed in bfloat16 or wider, within the bound.
No kernel may reach another device: no remote copies, remote signals or barrier semaphores. Data moves between devices by JAX's collectives and lax.ppermute only.
A program may use at most 128 MiB of HBM per device.

```python
import math
import jax
import jax.numpy as jnp
from jax import lax

TILE = 128
LG = 128
BB_DEV = 18
KD = 5
STOR = 2048
ITERS = 2
HOURS = 16
LINES = 16384
BUSES = 36864
N_TM = 16


def with_ends(values, own_key, least, high):
    index_at = [jax.random.randint(jax.random.fold_in(own_key, axis), (), 0, length) for axis, length in enumerate(values.shape)]
    longest = values.shape.index(max(values.shape))
    next_to = index_at[:longest] + [(index_at[longest] + 1) % values.shape[longest]] + index_at[longest + 1:]
    return values.at[tuple(index_at)].set(least).at[tuple(next_to)].set(high)


def block_levels(own_key, extent, pieces, low, largest):
    def one(dim, parts):
        draws = jax.random.uniform(jax.random.fold_in(jax.random.fold_in(own_key, 6), dim), (parts,), jnp.float32, low / len(pieces), largest / len(pieces))
        return jnp.repeat(jnp.exp(draws), extent[dim] // parts).reshape((-1,) + (1,) * (len(extent) - dim - 1))

    level = one(*pieces[0])
    for cut in pieces[1:]:
        level = level * one(*cut)
    return level


def centred(stream_key, dims, scale, reach, shards=(), kind=jnp.bfloat16):
    entries = jax.random.normal(stream_key, dims, jnp.float32) * scale
    if len(shards) > 0:
        entries = block_levels(stream_key, dims, shards, -0.22, 0.18) * entries
    return jnp.clip(entries, min=-reach, max=reach).astype(kind)


def setup_inputs(seed: int = 0, part: int = 0) -> dict:
    splits = jax.random.split(jax.random.key(seed), 8)
    own_keys = jax.random.split(jax.random.fold_in(splits[7], part), 8)
    return {
        "base_injection": centred(own_keys[0], (HOURS, BUSES), 1.0, 6.0, ((0, 16),)),
        "ptdf_tiles": centred(splits[1], (LG, KD * N_TM, TILE, TILE), (KD * N_TM * TILE) ** -0.5, 0.0625, ((1, 16),)),
        "tile_block": with_ends(jax.random.randint(splits[2], (LG, KD * N_TM), 0, BB_DEV), jax.random.fold_in(splits[2], 1), 0, BB_DEV - 1).astype(jnp.int32),
        "limits": jnp.clip(jax.random.uniform(splits[3], (LINES,), jnp.float32, 0.5, 2.0), 0.5, 2.0),
        "stor_bus": with_ends(jax.random.randint(splits[4], (STOR,), 0, BUSES), jax.random.fold_in(splits[4], 1), 0, BUSES - 1).astype(jnp.int32),
        "stor_gain": jnp.clip(jnp.exp(jax.random.uniform(splits[5], (STOR,), jnp.float32, math.log(0.5), math.log(4.0))), 0.5, 4.0),
        "soc_init": jnp.clip(1.0 * jax.random.uniform(own_keys[6], (HOURS, STOR), jnp.float32) ** block_levels(own_keys[6], (HOURS, STOR), ((0, 16),), -0.2, 0.2), 0.0, 1.0),
    }


step_size = 0.5
penalty = 4.0
ramp_weight = 0.5


def flow_product(sent, ptdf_tiles, tile_block):
    grid = sent.astype(jnp.float32).reshape(HOURS, N_TM, BB_DEV, TILE)
    tiles = ptdf_tiles.reshape(LG, N_TM, KD, TILE, TILE)
    blocks = tile_block.reshape(LG, N_TM, KD)
    device_ids = jnp.arange(N_TM, dtype=jnp.int32)[:, None]

    def one_group(pair):
        tiles_g, blocks_g = pair
        picked = grid[:, device_ids, blocks_g]
        return jnp.einsum("hnkb,nklb->hl", picked, tiles_g.astype(jnp.float32), precision=lax.Precision.HIGHEST)

    result = lax.map(one_group, (tiles, blocks))
    return jnp.transpose(result, (1, 0, 2)).reshape(HOURS, LG * TILE)


def price_product(dual_b, ptdf_tiles, tile_block):
    folded = jnp.transpose(dual_b.astype(jnp.float32).reshape(HOURS, LG, TILE), (1, 0, 2))
    tiles = ptdf_tiles.reshape(LG, N_TM, KD, TILE, TILE)
    blocks = tile_block.reshape(LG, N_TM, KD)
    device_ids = jnp.arange(N_TM, dtype=jnp.int32)[:, None]

    def add_group(total, triple):
        rows_g, tiles_g, blocks_g = triple
        contrib = jnp.einsum("hl,nklb->hnkb", rows_g, tiles_g.astype(jnp.float32), precision=lax.Precision.HIGHEST)
        return total.at[:, device_ids, blocks_g].add(contrib), None

    start_total = jnp.zeros((HOURS, N_TM, BB_DEV, TILE), jnp.float32)
    total, unused = lax.scan(add_group, start_total, (folded, tiles, blocks))
    return total.reshape(HOURS, BB_DEV * TILE * N_TM)


def reference(base_injection, ptdf_tiles, tile_block, limits, stor_bus, stor_gain, soc_init):
    base_full = base_injection.astype(jnp.float32)
    inject = base_full
    line_dual = jnp.zeros((HOURS, LG * TILE), jnp.float32)
    level = soc_init
    for iteration in range(ITERS):
        prev_inj = jnp.roll(inject, 1, axis=0)
        next_inj = jnp.roll(inject, -1, axis=0)
        prev_level = jnp.roll(level, 1, axis=0)
        line_flows = flow_product(inject.astype(jnp.bfloat16), ptdf_tiles, tile_block)
        shifted = line_flows + line_dual
        clipped = jnp.clip(shifted, -limits, limits)
        line_dual = shifted - clipped
        bus_price = price_product(line_dual.astype(jnp.bfloat16), ptdf_tiles, tile_block)
        store_price = bus_price[:, stor_bus]
        charge = level - prev_level
        updated = inject - step_size * ((inject - base_full) + penalty * bus_price
                                        + ramp_weight * (2.0 * inject - prev_inj - next_inj))
        updated = updated.at[:, stor_bus].add(-step_size * charge)
        level = 0.5 * (level + prev_level) - stor_gain * store_price
        inject = updated
    return inject, line_dual, level
```

```python
import functools

import jax
import jax.numpy as jnp
from jax import lax
from jax.experimental import pallas as pl
from jax.experimental.pallas import tpu as pltpu
from jax.sharding import PartitionSpec as P

ITERS = 2


step_size = 0.5
penalty = 4.0
ramp_weight = 0.5

NT = (((1,), (1,)), ((), ()))
VMEM = pl.BlockSpec(memory_space=pltpu.VMEM)
SMEM = pl.BlockSpec(memory_space=pltpu.SMEM)
HBM = pl.BlockSpec(memory_space=pl.ANY)
UNROLL = 4
CHUNKS = 16


def fetch(tiles_hbm, tiles, sems, chunk):
    size = tiles.shape[0] // sems.shape[0]
    part = pl.ds(chunk * size, size)
    return pltpu.make_async_copy(tiles_hbm.at[part], tiles.at[part], sems.at[chunk])


def fetch_all(tiles_hbm, tiles, sems):
    for chunk in range(sems.shape[0]):
        fetch(tiles_hbm, tiles, sems, chunk).start()


def flow_pass(picked, blocks, tiles, flows, ready):
    groups, depth = tiles.shape[0], tiles.shape[1]
    size = groups // CHUNKS

    def chunk_body(chunk, carry):
        ready(chunk)

        def body(step, inner):
            for u in range(UNROLL):
                g = chunk * size + step * UNROLL + u
                total = None
                for k in range(depth):
                    rows = picked[blocks[g * depth + k]]
                    part = lax.dot_general(rows, tiles[g, k], NT, preferred_element_type=jnp.float32)
                    total = part if total is None else total + part
                flows[g] = total.astype(flows.dtype)
            return inner

        return lax.fori_loop(0, size // UNROLL, body, carry)

    lax.fori_loop(0, CHUNKS, chunk_body, 0)


def price_pass(dual, blocks, tiles, sums, ready):
    groups, depth = tiles.shape[0], tiles.shape[1]
    size = groups // CHUNKS
    for ref in sums:
        ref[...] = jnp.zeros_like(ref)

    def chunk_body(chunk, carry):
        ready(chunk)

        def body(step, inner):
            for u in range(UNROLL):
                g = chunk * size + step * UNROLL + u
                rows = dual[g]
                for k in range(depth):
                    part = jnp.dot(rows, tiles[g, k], preferred_element_type=jnp.float32)
                    at = blocks[g * depth + k]
                    sums[k][at] = sums[k][at] + part
            return inner

        return lax.fori_loop(0, size // UNROLL, body, carry)

    lax.fori_loop(0, CHUNKS, chunk_body, 0)


def earlier(values):
    return jnp.concatenate([values[-1:], values[:-1]], axis=0)


def later(values):
    return jnp.concatenate([values[1:], values[:1]], axis=0)


def update_pass(sums, inject, base, delta, out, sent):
    for block in range(sums[0].shape[0]):
        price = sums[0][block]
        for ref in sums[1:]:
            price = price + ref[block]
        sums[0][block] = price
        now = inject(block)
        new = now - step_size * (
            (now - base(block))
            + penalty * price
            + ramp_weight * (2.0 * now - earlier(now) - later(now))
        )
        new = new - delta[block]
        out(block, new)
        if sent is not None:
            sent[block] = new.astype(jnp.bfloat16)


def level_pass(price, level, unit_block, unit_lane, gain, out, mine):
    count, hours, width = price.shape

    def body(c, carry):
        cols = pl.ds(pl.multiple_of(c * width, width), width)
        block = jnp.broadcast_to(unit_block[:, cols], (hours, width))
        lane = jnp.broadcast_to(unit_lane[:, cols], (hours, width))
        found = jnp.zeros((hours, width), jnp.float32)
        for b in range(count):
            found = jnp.where(block == b, jnp.take_along_axis(price[b], lane, axis=1), found)
        now = level[:, cols]
        new = 0.5 * (now + earlier(now)) - gain[:, cols] * found
        if mine:
            new = jnp.where((block >= 0) & (block < count), new, 0.0)
        out[:, cols] = new
        return carry

    lax.fori_loop(0, level.shape[1] // width, body, 0)


def first_flow_kernel(blocks, base, tiles_hbm, flows, tiles, picked, sems):
    fetch_all(tiles_hbm, tiles, sems)
    width = tiles.shape[3]
    for b in range(picked.shape[0]):
        picked[b] = base[:, b * width : (b + 1) * width]
    flow_pass(picked, blocks, tiles, flows, lambda c: fetch(tiles_hbm, tiles, sems, c).wait())


def middle_kernel(
    blocks, dual, base, delta, level, unit_block, unit_lane, gain, tiles_hbm,
    inject_out, level_out, flows, tiles, picked, sems, *sums
):
    fetch_all(tiles_hbm, tiles, sems)
    width = tiles.shape[3]
    price_pass(dual, blocks, tiles, sums, lambda c: fetch(tiles_hbm, tiles, sems, c).wait())

    def start(b):
        return base[:, b * width : (b + 1) * width].astype(jnp.float32)

    def write(b, new):
        inject_out[b] = new

    update_pass(sums, start, start, delta, write, picked)
    flow_pass(picked, blocks, tiles, flows, lambda c: None)
    level_pass(sums[0], level, unit_block, unit_lane, gain, level_out, False)


def last_kernel(
    blocks, dual, base, inject, delta, level, unit_block, unit_lane, gain, tiles_hbm,
    inject_out, level_out, tiles, sems, *sums
):
    fetch_all(tiles_hbm, tiles, sems)
    width = tiles.shape[3]
    price_pass(dual, blocks, tiles, sums, lambda c: fetch(tiles_hbm, tiles, sems, c).wait())

    def start(b):
        return base[:, b * width : (b + 1) * width].astype(jnp.float32)

    def write(b, new):
        inject_out[:, b * width : (b + 1) * width] = new

    update_pass(sums, lambda b: inject[b], start, delta, write, None)
    level_pass(sums[0], level, unit_block, unit_lane, gain, level_out, True)


def storage_kernel(level, unit_block, unit_lane, delta):
    count, hours, width = delta.shape
    units = level.shape[1]
    span = 2 * width
    delta[...] = jnp.zeros_like(delta)

    def body(c, carry):
        cols = pl.ds(pl.multiple_of(c * span, span), span)
        now = level[:, cols]
        charge = step_size * (now - earlier(now))
        high = charge.astype(jnp.bfloat16).astype(jnp.float32)
        low = charge - high
        lane = jnp.broadcast_to(unit_lane[:, cols], (width, span))
        hot = (lane == lax.broadcasted_iota(jnp.int32, (width, span), 0)).astype(jnp.bfloat16)
        block = jnp.broadcast_to(unit_block[:, cols], (hours, span))
        for b in range(count):
            held = block == b
            both = jnp.concatenate([jnp.where(held, high, 0.0), jnp.where(held, low, 0.0)], axis=0)
            part = lax.dot_general(both.astype(jnp.bfloat16), hot, NT, preferred_element_type=jnp.float32)
            delta[b] = delta[b] + (part[:hours] + part[hours:])
        return carry

    lax.fori_loop(0, units // span, body, 0)


def shards(base_injection, ptdf_tiles, tile_block, limits, stor_bus, stor_gain, soc_init):
    hour_rows = base_injection.shape[0]
    bus_count = base_injection.shape[1]
    line_count = limits.shape[0]
    groups, depth, lines, width = ptdf_tiles.shape
    units = stor_bus.shape[0]
    devices = lax.axis_size("tm")
    me = lax.axis_index("tm")
    buses = bus_count // devices
    bus_blocks = buses // width
    hours = hour_rows * devices
    own_groups = groups // devices
    blocks = tile_block.reshape(groups * depth)
    unit_block = (stor_bus // width - me * bus_blocks).reshape(1, units)
    unit_lane = (stor_bus % width).reshape(1, units)
    gain = stor_gain.reshape(1, units)
    own_limits = lax.dynamic_slice_in_dim(limits.reshape(groups, 1, lines), me * own_groups, own_groups, 0)

    tile_bytes = ptdf_tiles.size * 2
    held = [
        pltpu.VMEM(ptdf_tiles.shape, ptdf_tiles.dtype),
        pltpu.VMEM((bus_blocks, hours, width), jnp.bfloat16),
        pltpu.SemaphoreType.DMA((CHUNKS,)),
    ]
    sums = [pltpu.VMEM((bus_blocks, hours, width), jnp.float32)] * depth
    params = pltpu.CompilerParams(vmem_limit_bytes=tile_bytes + (16 << 20))
    pass_flops = 2 * hours * ptdf_tiles.size
    flow_shape = jax.ShapeDtypeStruct((groups, hours, lines), jnp.bfloat16)
    block_shape = jax.ShapeDtypeStruct((bus_blocks, hours, width), jnp.float32)
    level_shape = jax.ShapeDtypeStruct((hours, units), jnp.float32)

    level = lax.all_gather(soc_init, "tm", axis=0, tiled=True)
    base = lax.all_to_all(base_injection, "tm", split_axis=1, concat_axis=0, tiled=True)

    flows = pl.pallas_call(
        first_flow_kernel,
        out_shape=flow_shape,
        in_specs=[SMEM, VMEM, HBM],
        out_specs=VMEM,
        scratch_shapes=held,
        compiler_params=params,
        cost_estimate=pl.CostEstimate(flops=pass_flops, bytes_accessed=tile_bytes, transcendentals=0),
        name="first_flow",
    )(blocks, base, ptdf_tiles)

    line_dual = jnp.zeros((own_groups, hours, lines), jnp.float32)
    inject = None
    for iteration in range(ITERS):
        delta = pl.pallas_call(
            storage_kernel,
            out_shape=block_shape,
            in_specs=[VMEM] * 3,
            out_specs=VMEM,
            cost_estimate=pl.CostEstimate(flops=pass_flops, bytes_accessed=units * hours * 4, transcendentals=0),
            name="storage",
        )(level, unit_block, unit_lane)
        parts = lax.all_to_all(
            flows.reshape(devices, own_groups, hours, lines), "tm", split_axis=0, concat_axis=0, tiled=True
        )
        shifted = jnp.sum(parts.astype(jnp.float32), axis=0) + line_dual
        clipped = jnp.clip(shifted, -own_limits, own_limits)
        line_dual = shifted - clipped
        dual = lax.all_gather(line_dual.astype(jnp.bfloat16), "tm", axis=0, tiled=True)
        if iteration < ITERS - 1:
            inject, level, flows = pl.pallas_call(
                middle_kernel,
                out_shape=[block_shape, level_shape, flow_shape],
                in_specs=[SMEM] + [VMEM] * 7 + [HBM],
                out_specs=[VMEM] * 3,
                scratch_shapes=held + sums,
                compiler_params=params,
                cost_estimate=pl.CostEstimate(
                    flops=2 * pass_flops, bytes_accessed=tile_bytes, transcendentals=0
                ),
                name="price_then_flow",
            )(blocks, dual, base, delta, level, unit_block, unit_lane, gain, ptdf_tiles)
        else:
            inject, level = pl.pallas_call(
                last_kernel,
                out_shape=[jax.ShapeDtypeStruct((hours, buses), jnp.float32), level_shape],
                in_specs=[SMEM] + [VMEM] * 8 + [HBM],
                out_specs=[VMEM] * 2,
                scratch_shapes=[held[0], held[2]] + sums,
                compiler_params=params,
                cost_estimate=pl.CostEstimate(flops=pass_flops, bytes_accessed=tile_bytes, transcendentals=0),
                name="last_price",
            )(blocks, dual, base, inject, delta, level, unit_block, unit_lane, gain, ptdf_tiles)

    own_dual = lax.all_to_all(
        jnp.swapaxes(line_dual, 0, 1).reshape(hours, own_groups * lines), "tm", split_axis=0, concat_axis=1, tiled=True
    )
    joined = jnp.concatenate([inject, level], axis=1)
    back = lax.all_to_all(
        joined.reshape(devices, hour_rows, buses + units), "tm", split_axis=0, concat_axis=0, tiled=True
    )
    inject = jnp.swapaxes(back[:, :, :buses], 0, 1).reshape(hour_rows, bus_count)
    level = jnp.sum(back[:, :, buses:], axis=0)
    return (inject, own_dual, level)


def solution(mesh):
    in_specs = (
        P(("scen", "tm"), None),
        P(None, "tm", None, None),
        P(None, "tm"),
        P(),
        P(),
        P(),
        P(("scen", "tm"), None),
    )
    out_specs = (P(("scen", "tm"), None), P(("scen", "tm"), None), P(("scen", "tm"), None))
    return jax.shard_map(shards, mesh=mesh, in_specs=in_specs, out_specs=out_specs, check_vma=False)
```

```python
import functools

import jax
import jax.numpy as jnp
from jax import lax
from jax.experimental import pallas as pl
from jax.experimental.pallas import tpu as pltpu
from jax.sharding import PartitionSpec as P

ITERS = 2


step_size = 0.5
penalty = 4.0
ramp_weight = 0.5

NT = (((1,), (1,)), ((), ()))
VMEM = pl.BlockSpec(memory_space=pltpu.VMEM)
SMEM = pl.BlockSpec(memory_space=pltpu.SMEM)
PARAMS = pltpu.CompilerParams(vmem_limit_bytes=12 << 20)


def flow_pass(picked, blocks, tiles, flows):
    groups, depth, lines = tiles.shape[0], tiles.shape[1], tiles.shape[2]
    hours = picked.shape[1]

    def body(step, carry):
        base = step * 4
        rows = [[picked[blocks[(base + u) * depth + k]] for k in range(depth)] for u in range(4)]
        zero = jnp.zeros_like(rows[0][0])
        totals = [None] * 4

        def add(u, part):
            totals[u] = part if totals[u] is None else totals[u] + part

        for first in (0, 2):
            for k in range(0, depth - 1, 2):
                left = wide([[rows[first][k], rows[first][k + 1]], [rows[first + 1][k], rows[first + 1][k + 1]]])
                g = base + first
                right = wide([[tiles[g, k], tiles[g, k + 1]], [tiles[g + 1, k], tiles[g + 1, k + 1]]])
                part = lax.dot_general(left, right, NT, preferred_element_type=jnp.float32)
                add(first, part[:hours, :lines])
                add(first + 1, part[hours:, lines:])
        if depth % 2:
            k = depth - 1
            left = wide([[rows[0][k], zero], [rows[1][k], zero], [zero, rows[2][k]], [zero, rows[3][k]]])
            right = wide([[tiles[base, k], tiles[base + 2, k]], [tiles[base + 1, k], tiles[base + 3, k]]])
            part = lax.dot_general(left, right, NT, preferred_element_type=jnp.float32)
            for u in range(4):
                at = (u % 2) * lines
                add(u, part[u * hours : (u + 1) * hours, at : at + lines])
        for u in range(4):
            flows[base + u] = totals[u].astype(flows.dtype)
        return carry

    lax.fori_loop(0, groups // 4, body, 0)


def wide(parts):
    return jnp.concatenate([jnp.concatenate(row, axis=1) for row in parts], axis=0)


def price_pass(dual, blocks, tiles, sums):
    groups, depth, width = tiles.shape[0], tiles.shape[1], tiles.shape[3]
    hours = dual.shape[1]
    for ref in sums:
        ref[...] = jnp.zeros_like(ref)

    def body(step, carry):
        base = step * 4
        rows = [dual[base + u] for u in range(4)]
        zero = jnp.zeros_like(rows[0])
        parts = []
        for first in (0, 2):
            left = wide([[rows[first], zero], [zero, rows[first + 1]]])
            for k in range(0, depth - 1, 2):
                g = base + first
                right = wide([[tiles[g, k], tiles[g, k + 1]], [tiles[g + 1, k], tiles[g + 1, k + 1]]])
                part = jnp.dot(left, right, preferred_element_type=jnp.float32)
                for u in range(2):
                    for j in range(2):
                        block = part[u * hours : (u + 1) * hours, j * width : (j + 1) * width]
                        parts.append((first + u, k + j, block))
        if depth % 2:
            k = depth - 1
            left = wide([[rows[0], zero], [zero, rows[1]], [rows[2], zero], [zero, rows[3]]])
            right = wide([[tiles[base, k], tiles[base + 2, k]], [tiles[base + 1, k], tiles[base + 3, k]]])
            part = jnp.dot(left, right, preferred_element_type=jnp.float32)
            for u in range(4):
                at = (u // 2) * width
                parts.append((u, k, part[u * hours : (u + 1) * hours, at : at + width]))
        for u, k, part in parts:
            at = blocks[(base + u) * depth + k]
            sums[k][at] = sums[k][at] + part
        return carry

    lax.fori_loop(0, groups // 4, body, 0)


def earlier(values):
    return jnp.concatenate([values[-1:], values[:-1]], axis=0)


def later(values):
    return jnp.concatenate([values[1:], values[:1]], axis=0)


def update_pass(sums, inject, base, delta, out, sent):
    for block in range(sums[0].shape[0]):
        price = sums[0][block]
        for ref in sums[1:]:
            price = price + ref[block]
        sums[0][block] = price
        now = inject(block)
        new = now - step_size * (
            (now - base(block))
            + penalty * price
            + ramp_weight * (2.0 * now - earlier(now) - later(now))
        )
        new = new - delta[block]
        out(block, new)
        if sent is not None:
            sent[block] = new.astype(jnp.bfloat16)


def level_pass(price, level, unit_block, unit_lane, gain, out, mine):
    count, hours, width = price.shape

    def body(c, carry):
        cols = pl.ds(pl.multiple_of(c * width, width), width)
        block = jnp.broadcast_to(unit_block[:, cols], (hours, width))
        lane = jnp.broadcast_to(unit_lane[:, cols], (hours, width))
        found = jnp.zeros((hours, width), jnp.float32)
        for b in range(count):
            found = jnp.where(block == b, jnp.take_along_axis(price[b], lane, axis=1), found)
        now = level[:, cols]
        new = 0.5 * (now + earlier(now)) - gain[:, cols] * found
        if mine:
            new = jnp.where((block >= 0) & (block < count), new, 0.0)
        out[:, cols] = new
        return carry

    lax.fori_loop(0, level.shape[1] // width, body, 0)


def hold_kernel(tiles_hbm, tiles, sems):
    size = tiles.shape[0] // sems.shape[0]
    copies = []
    for chunk in range(sems.shape[0]):
        part = pl.ds(chunk * size, size)
        copies.append(pltpu.make_async_copy(tiles_hbm.at[part], tiles.at[part], sems.at[chunk]))
        copies[-1].start()
    for copy in copies:
        copy.wait()


def first_flow_kernel(blocks, base, tiles, flows, picked):
    width = tiles.shape[3]
    for b in range(picked.shape[0]):
        picked[b] = base[:, b * width : (b + 1) * width]
    flow_pass(picked, blocks, tiles, flows)


def middle_kernel(
    blocks, dual, base, delta, level, unit_block, unit_lane, gain, tiles,
    inject_out, level_out, flows, picked, *sums
):
    width = tiles.shape[3]
    price_pass(dual, blocks, tiles, sums)

    def start(b):
        return base[:, b * width : (b + 1) * width].astype(jnp.float32)

    def write(b, new):
        inject_out[b] = new

    update_pass(sums, start, start, delta, write, picked)
    flow_pass(picked, blocks, tiles, flows)
    level_pass(sums[0], level, unit_block, unit_lane, gain, level_out, False)


def last_kernel(
    blocks, dual, base, inject, delta, level, unit_block, unit_lane, gain, tiles,
    inject_out, level_out, *sums
):
    width = tiles.shape[3]
    price_pass(dual, blocks, tiles, sums)

    def start(b):
        return base[:, b * width : (b + 1) * width].astype(jnp.float32)

    def write(b, new):
        inject_out[:, b * width : (b + 1) * width] = new

    update_pass(sums, lambda b: inject[b], start, delta, write, None)
    level_pass(sums[0], level, unit_block, unit_lane, gain, level_out, True)


def storage_kernel(level, unit_block, unit_lane, delta):
    count, hours, width = delta.shape
    units = level.shape[1]
    span = 2 * width
    delta[...] = jnp.zeros_like(delta)

    def body(c, carry):
        cols = pl.ds(pl.multiple_of(c * span, span), span)
        now = level[:, cols]
        charge = step_size * (now - earlier(now))
        high = charge.astype(jnp.bfloat16).astype(jnp.float32)
        low = charge - high
        lane = jnp.broadcast_to(unit_lane[:, cols], (width, span))
        hot = (lane == lax.broadcasted_iota(jnp.int32, (width, span), 0)).astype(jnp.bfloat16)
        block = jnp.broadcast_to(unit_block[:, cols], (hours, span))
        for b in range(count):
            held = block == b
            both = jnp.concatenate([jnp.where(held, high, 0.0), jnp.where(held, low, 0.0)], axis=0)
            part = lax.dot_general(both.astype(jnp.bfloat16), hot, NT, preferred_element_type=jnp.float32)
            delta[b] = delta[b] + (part[:hours] + part[hours:])
        return carry

    lax.fori_loop(0, units // span, body, 0)


def shards(base_injection, ptdf_tiles, tile_block, limits, stor_bus, stor_gain, soc_init):
    hour_rows = base_injection.shape[0]
    bus_count = base_injection.shape[1]
    line_count = limits.shape[0]
    groups, depth, lines, width = ptdf_tiles.shape
    units = stor_bus.shape[0]
    devices = lax.axis_size("tm")
    me = lax.axis_index("tm")
    buses = bus_count // devices
    bus_blocks = buses // width
    hours = hour_rows * devices
    own_groups = groups // devices
    blocks = tile_block.reshape(groups * depth)
    unit_block = (stor_bus // width - me * bus_blocks).reshape(1, units)
    unit_lane = (stor_bus % width).reshape(1, units)
    gain = stor_gain.reshape(1, units)
    own_limits = lax.dynamic_slice_in_dim(limits.reshape(groups, 1, lines), me * own_groups, own_groups, 0)

    tile_bytes = ptdf_tiles.size * 2
    held = [pltpu.VMEM((bus_blocks, hours, width), jnp.bfloat16)]
    sums = [pltpu.VMEM((bus_blocks, hours, width), jnp.float32)] * depth
    pass_flops = 2 * hours * ptdf_tiles.size
    flow_shape = jax.ShapeDtypeStruct((groups, hours, lines), jnp.bfloat16)
    block_shape = jax.ShapeDtypeStruct((bus_blocks, hours, width), jnp.float32)
    level_shape = jax.ShapeDtypeStruct((hours, units), jnp.float32)

    high = soc_init.astype(jnp.bfloat16)
    low = (soc_init - high.astype(jnp.float32)).astype(jnp.bfloat16)
    own = jnp.concatenate([high, low], axis=1)[:, None, :]
    sent = jnp.concatenate(
        [base_injection.reshape(hour_rows, devices, buses), jnp.broadcast_to(own, (hour_rows, devices, 2 * units))], axis=2
    )
    came = lax.all_to_all(jnp.swapaxes(sent, 0, 1), "tm", split_axis=0, concat_axis=0, tiled=True)
    came = came.reshape(hours, buses + 2 * units)
    base = came[:, :buses]
    level = came[:, buses : buses + units].astype(jnp.float32) + came[:, buses + units :].astype(jnp.float32)

    tiles = pl.pallas_call(
        hold_kernel,
        out_shape=jax.ShapeDtypeStruct(ptdf_tiles.shape, ptdf_tiles.dtype),
        in_specs=[pl.BlockSpec(memory_space=pltpu.HBM)],
        out_specs=VMEM,
        scratch_shapes=[pltpu.SemaphoreType.DMA((16,))],
        compiler_params=PARAMS,
        cost_estimate=pl.CostEstimate(flops=0, bytes_accessed=2 * tile_bytes, transcendentals=0),
        name="hold_tiles",
    )(ptdf_tiles)
    flows = pl.pallas_call(
        first_flow_kernel,
        out_shape=flow_shape,
        in_specs=[SMEM, VMEM, VMEM],
        out_specs=VMEM,
        scratch_shapes=held,
        compiler_params=PARAMS,
        cost_estimate=pl.CostEstimate(flops=pass_flops, bytes_accessed=tile_bytes, transcendentals=0),
        name="first_flow",
    )(blocks, base, tiles)

    line_dual = jnp.zeros((own_groups, hours, lines), jnp.float32)
    inject = None
    for iteration in range(ITERS):
        delta = pl.pallas_call(
            storage_kernel,
            out_shape=block_shape,
            in_specs=[VMEM] * 3,
            out_specs=VMEM,
            compiler_params=PARAMS,
            cost_estimate=pl.CostEstimate(flops=pass_flops, bytes_accessed=units * hours * 4, transcendentals=0),
            name="storage",
        )(level, unit_block, unit_lane)
        parts = lax.all_to_all(
            flows.reshape(devices, own_groups, hours, lines), "tm", split_axis=0, concat_axis=0, tiled=True
        )
        shifted = jnp.sum(parts.astype(jnp.float32), axis=0) + line_dual
        clipped = jnp.clip(shifted, -own_limits, own_limits)
        line_dual = shifted - clipped
        dual = lax.all_gather(line_dual.astype(jnp.bfloat16), "tm", axis=0, tiled=True)
        if iteration < ITERS - 1:
            inject, level, flows = pl.pallas_call(
                middle_kernel,
                out_shape=[block_shape, level_shape, flow_shape],
                in_specs=[SMEM] + [VMEM] * 8,
                out_specs=[VMEM] * 3,
                scratch_shapes=held + sums,
                compiler_params=PARAMS,
                cost_estimate=pl.CostEstimate(
                    flops=2 * pass_flops, bytes_accessed=tile_bytes, transcendentals=0
                ),
                name="price_then_flow",
            )(blocks, dual, base, delta, level, unit_block, unit_lane, gain, tiles)
        else:
            inject, level = pl.pallas_call(
                last_kernel,
                out_shape=[jax.ShapeDtypeStruct((hours, buses), jnp.float32), level_shape],
                in_specs=[SMEM] + [VMEM] * 9,
                out_specs=[VMEM] * 2,
                scratch_shapes=sums,
                compiler_params=PARAMS,
                cost_estimate=pl.CostEstimate(flops=pass_flops, bytes_accessed=tile_bytes, transcendentals=0),
                name="last_price",
            )(blocks, dual, base, inject, delta, level, unit_block, unit_lane, gain, tiles)

    own_dual = lax.all_to_all(
        jnp.swapaxes(line_dual, 0, 1).reshape(hours, own_groups * lines), "tm", split_axis=0, concat_axis=1, tiled=True
    )
    joined = jnp.concatenate([inject, level], axis=1)
    back = lax.all_to_all(
        joined.reshape(devices, hour_rows, buses + units), "tm", split_axis=0, concat_axis=0, tiled=True
    )
    inject = jnp.swapaxes(back[:, :, :buses], 0, 1).reshape(hour_rows, bus_count)
    level = jnp.sum(back[:, :, buses:], axis=0)
    return (inject, own_dual, level)


def solution(mesh):
    in_specs = (
        P(("scen", "tm"), None),
        P(None, "tm", None, None),
        P(None, "tm"),
        P(),
        P(),
        P(),
        P(("scen", "tm"), None),
    )
    out_specs = (P(("scen", "tm"), None), P(("scen", "tm"), None), P(("scen", "tm"), None))
    return jax.shard_map(shards, mesh=mesh, in_specs=in_specs, out_specs=out_specs, check_vma=False)
```

```python
import functools

import jax
import jax.numpy as jnp
from jax import lax
from jax.experimental import pallas as pl
from jax.experimental.pallas import tpu as pltpu
from jax.sharding import PartitionSpec as P

ITERS = 2


step_size = 0.5
penalty = 4.0
ramp_weight = 0.5

NT = (((1,), (1,)), ((), ()))
VMEM = pl.BlockSpec(memory_space=pltpu.VMEM)
SMEM = pl.BlockSpec(memory_space=pltpu.SMEM)
HBM = pl.BlockSpec(memory_space=pl.ANY)
SMALL = pltpu.CompilerParams(vmem_limit_bytes=12 << 20)
CHUNKS = 8


def fetch(tiles_hbm, tiles, sems, chunk):
    size = tiles.shape[0] // sems.shape[0]
    part = pl.ds(chunk * size, size)
    return pltpu.make_async_copy(tiles_hbm.at[part], tiles.at[part], sems.at[chunk])


def fetch_all(tiles_hbm, tiles, sems):
    for chunk in range(sems.shape[0]):
        fetch(tiles_hbm, tiles, sems, chunk).start()


def over_groups(groups, ready, four):
    size = groups // CHUNKS

    def body(chunk, carry):
        ready(chunk)
        for sub in range(0, size, 4):
            four(chunk * size + sub)
        return carry

    lax.fori_loop(0, CHUNKS, body, 0)


def flow_pass(picked, blocks, tiles, flows, ready):
    groups, depth, lines = tiles.shape[0], tiles.shape[1], tiles.shape[2]
    hours = picked.shape[1]

    def four(base):
        rows = [[picked[blocks[(base + u) * depth + k]] for k in range(depth)] for u in range(4)]
        zero = jnp.zeros_like(rows[0][0])
        totals = [None] * 4

        def add(u, part):
            totals[u] = part if totals[u] is None else totals[u] + part

        for first in (0, 2):
            for k in range(0, depth - 1, 2):
                left = wide([[rows[first][k], rows[first][k + 1]], [rows[first + 1][k], rows[first + 1][k + 1]]])
                g = base + first
                right = wide([[tiles[g, k], tiles[g, k + 1]], [tiles[g + 1, k], tiles[g + 1, k + 1]]])
                part = lax.dot_general(left, right, NT, preferred_element_type=jnp.float32)
                add(first, part[:hours, :lines])
                add(first + 1, part[hours:, lines:])
        if depth % 2:
            k = depth - 1
            left = wide([[rows[0][k], zero], [rows[1][k], zero], [zero, rows[2][k]], [zero, rows[3][k]]])
            right = wide([[tiles[base, k], tiles[base + 2, k]], [tiles[base + 1, k], tiles[base + 3, k]]])
            part = lax.dot_general(left, right, NT, preferred_element_type=jnp.float32)
            for u in range(4):
                at = (u % 2) * lines
                add(u, part[u * hours : (u + 1) * hours, at : at + lines])
        for u in range(4):
            flows[base + u] = totals[u].astype(flows.dtype)

    over_groups(groups, ready, four)


def wide(parts):
    return jnp.concatenate([jnp.concatenate(row, axis=1) for row in parts], axis=0)


def price_pass(dual, blocks, tiles, sums, ready):
    groups, depth, width = tiles.shape[0], tiles.shape[1], tiles.shape[3]
    hours = dual.shape[1]
    for ref in sums:
        ref[...] = jnp.zeros_like(ref)

    def four(base):
        rows = [dual[base + u] for u in range(4)]
        zero = jnp.zeros_like(rows[0])
        parts = []
        for first in (0, 2):
            left = wide([[rows[first], zero], [zero, rows[first + 1]]])
            for k in range(0, depth - 1, 2):
                g = base + first
                right = wide([[tiles[g, k], tiles[g, k + 1]], [tiles[g + 1, k], tiles[g + 1, k + 1]]])
                part = jnp.dot(left, right, preferred_element_type=jnp.float32)
                for u in range(2):
                    for j in range(2):
                        block = part[u * hours : (u + 1) * hours, j * width : (j + 1) * width]
                        parts.append((first + u, k + j, block))
        if depth % 2:
            k = depth - 1
            left = wide([[rows[0], zero], [zero, rows[1]], [rows[2], zero], [zero, rows[3]]])
            right = wide([[tiles[base, k], tiles[base + 2, k]], [tiles[base + 1, k], tiles[base + 3, k]]])
            part = jnp.dot(left, right, preferred_element_type=jnp.float32)
            for u in range(4):
                at = (u // 2) * width
                parts.append((u, k, part[u * hours : (u + 1) * hours, at : at + width]))
        for u, k, part in parts:
            at = blocks[(base + u) * depth + k]
            sums[k][at] = sums[k][at] + part

    over_groups(groups, ready, four)


def earlier(values):
    return jnp.concatenate([values[-1:], values[:-1]], axis=0)


def later(values):
    return jnp.concatenate([values[1:], values[:1]], axis=0)


def update_pass(sums, inject, base, delta, out, sent):
    for block in range(sums[0].shape[0]):
        price = sums[0][block]
        for ref in sums[1:]:
            price = price + ref[block]
        sums[0][block] = price
        now = inject(block)
        new = now - step_size * (
            (now - base(block))
            + penalty * price
            + ramp_weight * (2.0 * now - earlier(now) - later(now))
        )
        new = new - delta[block]
        out(block, new)
        if sent is not None:
            sent[block] = new.astype(jnp.bfloat16)


def level_pass(price, level, unit_block, unit_lane, gain, out, mine):
    count, hours, width = price.shape

    def body(c, carry):
        cols = pl.ds(pl.multiple_of(c * width, width), width)
        block = jnp.broadcast_to(unit_block[:, cols], (hours, width))
        lane = jnp.broadcast_to(unit_lane[:, cols], (hours, width))
        found = jnp.zeros((hours, width), jnp.float32)
        for b in range(count):
            found = jnp.where(block == b, jnp.take_along_axis(price[b], lane, axis=1), found)
        now = level[:, cols]
        new = 0.5 * (now + earlier(now)) - gain[:, cols] * found
        if mine:
            new = jnp.where((block >= 0) & (block < count), new, 0.0)
        out[:, cols] = new
        return carry

    lax.fori_loop(0, level.shape[1] // width, body, 0)


def first_flow_kernel(blocks, base, tiles_hbm, flows, tiles, sems, picked):
    fetch_all(tiles_hbm, tiles, sems)
    width = tiles.shape[3]
    for b in range(picked.shape[0]):
        picked[b] = base[:, b * width : (b + 1) * width]
    flow_pass(picked, blocks, tiles, flows, lambda c: fetch(tiles_hbm, tiles, sems, c).wait())


def middle_kernel(
    blocks, dual, base, delta, level, unit_block, unit_lane, gain, tiles_hbm,
    inject_out, level_out, flows, tiles, sems, picked, *sums
):
    fetch_all(tiles_hbm, tiles, sems)
    width = tiles.shape[3]
    price_pass(dual, blocks, tiles, sums, lambda c: fetch(tiles_hbm, tiles, sems, c).wait())

    def start(b):
        return base[:, b * width : (b + 1) * width].astype(jnp.float32)

    def write(b, new):
        inject_out[b] = new

    update_pass(sums, start, start, delta, write, picked)
    flow_pass(picked, blocks, tiles, flows, lambda c: None)
    level_pass(sums[0], level, unit_block, unit_lane, gain, level_out, False)


def last_kernel(
    blocks, dual, base, inject, delta, level, unit_block, unit_lane, gain, tiles_hbm,
    inject_out, level_out, tiles, sems, *sums
):
    fetch_all(tiles_hbm, tiles, sems)
    width = tiles.shape[3]
    price_pass(dual, blocks, tiles, sums, lambda c: fetch(tiles_hbm, tiles, sems, c).wait())

    def start(b):
        return base[:, b * width : (b + 1) * width].astype(jnp.float32)

    def write(b, new):
        inject_out[:, b * width : (b + 1) * width] = new

    update_pass(sums, lambda b: inject[b], start, delta, write, None)
    level_pass(sums[0], level, unit_block, unit_lane, gain, level_out, True)


def storage_kernel(level, unit_block, unit_lane, delta):
    count, hours, width = delta.shape
    units = level.shape[1]
    span = 2 * width
    delta[...] = jnp.zeros_like(delta)

    def body(c, carry):
        cols = pl.ds(pl.multiple_of(c * span, span), span)
        now = level[:, cols]
        charge = step_size * (now - earlier(now))
        high = charge.astype(jnp.bfloat16).astype(jnp.float32)
        low = charge - high
        lane = jnp.broadcast_to(unit_lane[:, cols], (width, span))
        hot = (lane == lax.broadcasted_iota(jnp.int32, (width, span), 0)).astype(jnp.bfloat16)
        block = jnp.broadcast_to(unit_block[:, cols], (hours, span))
        for b in range(count):
            held = block == b
            both = jnp.concatenate([jnp.where(held, high, 0.0), jnp.where(held, low, 0.0)], axis=0)
            part = lax.dot_general(both.astype(jnp.bfloat16), hot, NT, preferred_element_type=jnp.float32)
            delta[b] = delta[b] + (part[:hours] + part[hours:])
        return carry

    lax.fori_loop(0, units // span, body, 0)


def shards(base_injection, ptdf_tiles, tile_block, limits, stor_bus, stor_gain, soc_init):
    hour_rows = base_injection.shape[0]
    bus_count = base_injection.shape[1]
    line_count = limits.shape[0]
    groups, depth, lines, width = ptdf_tiles.shape
    units = stor_bus.shape[0]
    devices = lax.axis_size("tm")
    me = lax.axis_index("tm")
    buses = bus_count // devices
    bus_blocks = buses // width
    hours = hour_rows * devices
    own_groups = groups // devices
    blocks = tile_block.reshape(groups * depth)
    unit_block = (stor_bus // width - me * bus_blocks).reshape(1, units)
    unit_lane = (stor_bus % width).reshape(1, units)
    gain = stor_gain.reshape(1, units)
    own_limits = lax.dynamic_slice_in_dim(limits.reshape(groups, 1, lines), me * own_groups, own_groups, 0)

    tile_bytes = ptdf_tiles.size * 2
    stream = [pltpu.VMEM(ptdf_tiles.shape, ptdf_tiles.dtype), pltpu.SemaphoreType.DMA((CHUNKS,))]
    held = stream + [pltpu.VMEM((bus_blocks, hours, width), jnp.bfloat16)]
    large = pltpu.CompilerParams(vmem_limit_bytes=tile_bytes + (16 << 20))
    sums = [pltpu.VMEM((bus_blocks, hours, width), jnp.float32)] * depth
    pass_flops = 2 * hours * ptdf_tiles.size
    flow_shape = jax.ShapeDtypeStruct((groups, hours, lines), jnp.bfloat16)
    block_shape = jax.ShapeDtypeStruct((bus_blocks, hours, width), jnp.float32)
    level_shape = jax.ShapeDtypeStruct((hours, units), jnp.float32)

    high = soc_init.astype(jnp.bfloat16)
    low = (soc_init - high.astype(jnp.float32)).astype(jnp.bfloat16)
    own = jnp.concatenate([high, low], axis=1)[:, None, :]
    sent = jnp.concatenate(
        [base_injection.reshape(hour_rows, devices, buses), jnp.broadcast_to(own, (hour_rows, devices, 2 * units))], axis=2
    )
    came = lax.all_to_all(jnp.swapaxes(sent, 0, 1), "tm", split_axis=0, concat_axis=0, tiled=True)
    came = came.reshape(hours, buses + 2 * units)
    base = came[:, :buses]
    level = came[:, buses : buses + units].astype(jnp.float32) + came[:, buses + units :].astype(jnp.float32)

    flows = pl.pallas_call(
        first_flow_kernel,
        out_shape=flow_shape,
        in_specs=[SMEM, VMEM, HBM],
        out_specs=VMEM,
        scratch_shapes=held,
        compiler_params=large,
        cost_estimate=pl.CostEstimate(flops=pass_flops, bytes_accessed=tile_bytes, transcendentals=0),
        name="first_flow",
    )(blocks, base, ptdf_tiles)

    line_dual = jnp.zeros((own_groups, hours, lines), jnp.float32)
    inject = None
    for iteration in range(ITERS):
        delta = pl.pallas_call(
            storage_kernel,
            out_shape=block_shape,
            in_specs=[VMEM] * 3,
            out_specs=VMEM,
            compiler_params=SMALL,
            cost_estimate=pl.CostEstimate(flops=pass_flops, bytes_accessed=units * hours * 4, transcendentals=0),
            name="storage",
        )(level, unit_block, unit_lane)
        parts = lax.all_to_all(
            flows.reshape(devices, own_groups, hours, lines), "tm", split_axis=0, concat_axis=0, tiled=True
        )
        shifted = jnp.sum(parts.astype(jnp.float32), axis=0) + line_dual
        clipped = jnp.clip(shifted, -own_limits, own_limits)
        line_dual = shifted - clipped
        dual = lax.all_gather(line_dual.astype(jnp.bfloat16), "tm", axis=0, tiled=True)
        if iteration < ITERS - 1:
            inject, level, flows = pl.pallas_call(
                middle_kernel,
                out_shape=[block_shape, level_shape, flow_shape],
                in_specs=[SMEM] + [VMEM] * 7 + [HBM],
                out_specs=[VMEM] * 3,
                scratch_shapes=held + sums,
                compiler_params=large,
                cost_estimate=pl.CostEstimate(
                    flops=2 * pass_flops, bytes_accessed=tile_bytes, transcendentals=0
                ),
                name="price_then_flow",
            )(blocks, dual, base, delta, level, unit_block, unit_lane, gain, ptdf_tiles)
        else:
            inject, level = pl.pallas_call(
                last_kernel,
                out_shape=[jax.ShapeDtypeStruct((hours, buses), jnp.float32), level_shape],
                in_specs=[SMEM] + [VMEM] * 8 + [HBM],
                out_specs=[VMEM] * 2,
                scratch_shapes=stream + sums,
                compiler_params=large,
                cost_estimate=pl.CostEstimate(flops=pass_flops, bytes_accessed=tile_bytes, transcendentals=0),
                name="last_price",
            )(blocks, dual, base, inject, delta, level, unit_block, unit_lane, gain, ptdf_tiles)

    duals = own_groups * lines
    joined = jnp.concatenate([inject, level, jnp.swapaxes(line_dual, 0, 1).reshape(hours, duals)], axis=1)
    back = lax.all_to_all(
        joined.reshape(devices, hour_rows, buses + units + duals), "tm", split_axis=0, concat_axis=0, tiled=True
    )
    inject = jnp.swapaxes(back[:, :, :buses], 0, 1).reshape(hour_rows, bus_count)
    level = jnp.sum(back[:, :, buses : buses + units], axis=0)
    own_dual = jnp.swapaxes(back[:, :, buses + units :], 0, 1).reshape(hour_rows, line_count)
    return (inject, own_dual, level)


def solution(mesh):
    in_specs = (
        P(("scen", "tm"), None),
        P(None, "tm", None, None),
        P(None, "tm"),
        P(),
        P(),
        P(),
        P(("scen", "tm"), None),
    )
    out_specs = (P(("scen", "tm"), None), P(("scen", "tm"), None), P(("scen", "tm"), None))
    return jax.shard_map(shards, mesh=mesh, in_specs=in_specs, out_specs=out_specs, check_vma=False)
```

```python
import functools

import jax
import jax.numpy as jnp
from jax import lax
from jax.experimental import pallas as pl
from jax.experimental.pallas import tpu as pltpu
from jax.sharding import PartitionSpec as P

ITERS = 2


step_size = 0.5
penalty = 4.0
ramp_weight = 0.5

NT = (((1,), (1,)), ((), ()))
VMEM = pl.BlockSpec(memory_space=pltpu.VMEM)
SMEM = pl.BlockSpec(memory_space=pltpu.SMEM)
HBM = pl.BlockSpec(memory_space=pl.ANY)
SMALL = pltpu.CompilerParams(vmem_limit_bytes=12 << 20)
STRAIGHT = 16


class Half:
    def __init__(self, core, blocks, tiles_hbm, tiles, sems):
        self.core, self.blocks, self.tiles_hbm, self.tiles, self.sems = core, blocks, tiles_hbm, tiles, sems
        self.chunks = sems.shape[0]
        self.own = tiles.shape[0] // self.chunks

    def fetch(self, chunk):
        there = pl.ds((2 * chunk + self.core) * self.own, self.own)
        here = pl.ds(chunk * self.own, self.own)
        return pltpu.make_async_copy(self.tiles_hbm.at[there], self.tiles.at[here], self.sems.at[chunk])

    def start(self):
        for chunk in range(self.chunks):
            self.fetch(chunk).start()

    def each_four(self, wait, four):
        depth = self.tiles.shape[1]
        per = max(1, STRAIGHT // self.own)

        def body(step, carry):
            for c in range(per):
                chunk = step * per + c
                if wait:
                    self.fetch(chunk).wait()
                for sub in range(0, self.own, 4):
                    first = ((2 * chunk + self.core) * self.own + sub) * depth
                    four(chunk * self.own + sub, lambda u, k: self.blocks[first + u * depth + k])
            return carry

        lax.fori_loop(0, self.chunks // per, body, 0)


def wide(parts):
    return jnp.concatenate([jnp.concatenate(row, axis=1) for row in parts], axis=0)


def flow_pass(picked, half, flows, wait):
    tiles = half.tiles
    depth, lines = tiles.shape[1], tiles.shape[2]
    hours = picked.shape[1]

    def four(base, block):
        rows = [[picked[block(u, k)] for k in range(depth)] for u in range(4)]
        zero = jnp.zeros_like(rows[0][0])
        totals = [None] * 4

        def add(u, part):
            totals[u] = part if totals[u] is None else totals[u] + part

        for first in (0, 2):
            for k in range(0, depth - 1, 2):
                left = wide([[rows[first][k], rows[first][k + 1]], [rows[first + 1][k], rows[first + 1][k + 1]]])
                g = base + first
                right = wide([[tiles[g, k], tiles[g, k + 1]], [tiles[g + 1, k], tiles[g + 1, k + 1]]])
                part = lax.dot_general(left, right, NT, preferred_element_type=jnp.float32)
                add(first, part[:hours, :lines])
                add(first + 1, part[hours:, lines:])
        if depth % 2:
            k = depth - 1
            left = wide([[rows[0][k], zero], [rows[1][k], zero], [zero, rows[2][k]], [zero, rows[3][k]]])
            right = wide([[tiles[base, k], tiles[base + 2, k]], [tiles[base + 1, k], tiles[base + 3, k]]])
            part = lax.dot_general(left, right, NT, preferred_element_type=jnp.float32)
            for u in range(4):
                at = (u % 2) * lines
                add(u, part[u * hours : (u + 1) * hours, at : at + lines])
        for u in range(4):
            flows[base + u] = totals[u].astype(flows.dtype)

    half.each_four(wait, four)


def price_pass(dual, half, sums, wait):
    tiles = half.tiles
    depth, width = tiles.shape[1], tiles.shape[3]
    hours = dual.shape[1]
    for ref in sums:
        ref[...] = jnp.zeros_like(ref)

    def four(base, block):
        rows = [dual[base + u] for u in range(4)]
        zero = jnp.zeros_like(rows[0])
        parts = []
        for first in (0, 2):
            left = wide([[rows[first], zero], [zero, rows[first + 1]]])
            for k in range(0, depth - 1, 2):
                g = base + first
                right = wide([[tiles[g, k], tiles[g, k + 1]], [tiles[g + 1, k], tiles[g + 1, k + 1]]])
                part = jnp.dot(left, right, preferred_element_type=jnp.float32)
                for u in range(2):
                    for j in range(2):
                        piece = part[u * hours : (u + 1) * hours, j * width : (j + 1) * width]
                        parts.append((first + u, k + j, piece))
        if depth % 2:
            k = depth - 1
            left = wide([[rows[0], zero], [zero, rows[1]], [rows[2], zero], [zero, rows[3]]])
            right = wide([[tiles[base, k], tiles[base + 2, k]], [tiles[base + 1, k], tiles[base + 3, k]]])
            part = jnp.dot(left, right, preferred_element_type=jnp.float32)
            for u in range(4):
                at = (u // 2) * width
                parts.append((u, k, part[u * hours : (u + 1) * hours, at : at + width]))
        for u, k, part in parts:
            at = block(u, k)
            sums[k][at] = sums[k][at] + part

    half.each_four(wait, four)


def earlier(values):
    return jnp.concatenate([values[-1:], values[:-1]], axis=0)


def later(values):
    return jnp.concatenate([values[1:], values[:1]], axis=0)


def total(sums, block):
    price = sums[0][block]
    for ref in sums[1:]:
        price = price + ref[block]
    return price


def update_pass(sums, before, inject, base, delta, price_out, out):
    for block in range(sums[0].shape[0]):
        price = before[block] + total(sums, block)
        price_out[block] = price
        now = inject(block)
        new = now - step_size * (
            (now - base(block))
            + penalty * price
            + ramp_weight * (2.0 * now - earlier(now) - later(now))
        )
        out(block, new - delta[block])


def level_pass(price, level, unit_block, unit_lane, gain, out, mine):
    count, hours, width = price.shape

    def body(c, carry):
        cols = pl.ds(pl.multiple_of(c * width, width), width)
        block = jnp.broadcast_to(unit_block[:, cols], (hours, width))
        lane = jnp.broadcast_to(unit_lane[:, cols], (hours, width))
        found = jnp.zeros((hours, width), jnp.float32)
        for b in range(count):
            found = jnp.where(block == b, jnp.take_along_axis(price[b], lane, axis=1), found)
        now = level[:, cols]
        new = 0.5 * (now + earlier(now)) - gain[:, cols] * found
        if mine:
            new = jnp.where((block >= 0) & (block < count), new, 0.0)
        out[:, cols] = new
        return carry

    lax.fori_loop(0, level.shape[1] // width, body, 0)


def first_flow_kernel(core, blocks, base, tiles_hbm, flows, picked, tiles, sems):
    half = Half(1 - core[0], blocks, tiles_hbm, tiles, sems)
    half.start()
    width = tiles.shape[3]
    for b in range(picked.shape[0]):
        picked[b] = base[:, b * width : (b + 1) * width]
    flow_pass(picked, half, flows, True)


def own_flow_kernel(core, blocks, picked, tiles_hbm, flows, tiles, sems):
    half = Half(core[0], blocks, tiles_hbm, tiles, sems)
    half.start()
    flow_pass(picked, half, flows, True)


def own_price_kernel(core, blocks, dual, tiles_hbm, price, tiles, sems, *sums):
    half = Half(core[0], blocks, tiles_hbm, tiles, sems)
    half.start()
    price_pass(dual, half, sums, True)
    for b in range(price.shape[0]):
        price[b] = total(sums, b)


def middle_kernel(
    core, blocks, dual, before, base, delta, tiles_hbm,
    price, inject_out, picked, flows, tiles, sems, *sums
):
    half = Half(1 - core[0], blocks, tiles_hbm, tiles, sems)
    half.start()
    width = tiles.shape[3]
    price_pass(dual, half, sums, True)

    def start(b):
        return base[:, b * width : (b + 1) * width].astype(jnp.float32)

    def write(b, new):
        inject_out[b] = new
        picked[b] = new.astype(picked.dtype)

    update_pass(sums, before, start, start, delta, price, write)
    flow_pass(picked, half, flows, False)


def last_kernel(
    core, blocks, dual, before, base, inject, delta, level, unit_block, unit_lane, gain, tiles_hbm,
    inject_out, level_out, tiles, sems, price, *sums
):
    half = Half(1 - core[0], blocks, tiles_hbm, tiles, sems)
    half.start()
    width = tiles.shape[3]
    price_pass(dual, half, sums, True)

    def start(b):
        return base[:, b * width : (b + 1) * width].astype(jnp.float32)

    def write(b, new):
        inject_out[:, b * width : (b + 1) * width] = new

    update_pass(sums, before, lambda b: inject[b], start, delta, price, write)
    level_pass(price, level, unit_block, unit_lane, gain, level_out, True)


def storage_pass(level, unit_block, unit_lane, delta):
    count, hours, width = delta.shape
    units = level.shape[1]
    span = 2 * width
    delta[...] = jnp.zeros_like(delta)

    def body(c, carry):
        cols = pl.ds(pl.multiple_of(c * span, span), span)
        now = level[:, cols]
        charge = step_size * (now - earlier(now))
        high = charge.astype(jnp.bfloat16).astype(jnp.float32)
        low = charge - high
        lane = jnp.broadcast_to(unit_lane[:, cols], (width, span))
        hot = (lane == lax.broadcasted_iota(jnp.int32, (width, span), 0)).astype(jnp.bfloat16)
        block = jnp.broadcast_to(unit_block[:, cols], (hours, span))
        for b in range(count):
            held = block == b
            both = jnp.concatenate([jnp.where(held, high, 0.0), jnp.where(held, low, 0.0)], axis=0)
            part = lax.dot_general(both.astype(jnp.bfloat16), hot, NT, preferred_element_type=jnp.float32)
            delta[b] = delta[b] + (part[:hours] + part[hours:])
        return carry

    lax.fori_loop(0, units // span, body, 0)


def storage_kernel(level, unit_block, unit_lane, delta):
    storage_pass(level, unit_block, unit_lane, delta)


def level_kernel(price, level, unit_block, unit_lane, gain, level_out, delta):
    level_pass(price, level, unit_block, unit_lane, gain, level_out, False)
    storage_pass(level_out, unit_block, unit_lane, delta)


def shards(base_injection, ptdf_tiles, tile_block, limits, stor_bus, stor_gain, soc_init):
    hour_rows = base_injection.shape[0]
    bus_count = base_injection.shape[1]
    line_count = limits.shape[0]
    groups, depth, lines, width = ptdf_tiles.shape
    units = stor_bus.shape[0]
    devices = lax.axis_size("tm")
    me = lax.axis_index("tm")
    buses = bus_count // devices
    bus_blocks = buses // width
    hours = hour_rows * devices
    own_groups = groups // devices
    blocks = tile_block.reshape(groups * depth)
    unit_block = (stor_bus // width - me * bus_blocks).reshape(1, units)
    unit_lane = (stor_bus % width).reshape(1, units)
    gain = stor_gain.reshape(1, units)
    own_limits = lax.dynamic_slice_in_dim(limits.reshape(groups, 1, lines), me * own_groups, own_groups, 0)

    chips = devices // 2
    half_groups = chips * own_groups
    core = (me % 2).reshape(1)
    same_core = [[2 * chip + c for chip in range(chips)] for c in range(2)]
    sibling = [(d, d + 1 - 2 * (d % 2)) for d in range(devices)]

    half_bytes = ptdf_tiles.size
    half_flops = hours * ptdf_tiles.size
    stream = [pltpu.VMEM((half_groups, *ptdf_tiles.shape[1:]), ptdf_tiles.dtype), pltpu.SemaphoreType.DMA((chips,))]
    sums = [pltpu.VMEM((bus_blocks, hours, width), jnp.float32)] * depth
    large = pltpu.CompilerParams(vmem_limit_bytes=half_bytes + (16 << 20))
    picked_shape = jax.ShapeDtypeStruct((bus_blocks, hours, width), jnp.bfloat16)
    block_shape = jax.ShapeDtypeStruct((bus_blocks, hours, width), jnp.float32)
    level_shape = jax.ShapeDtypeStruct((hours, units), jnp.float32)
    flow_shape = jax.ShapeDtypeStruct((half_groups, hours, lines), jnp.float32)

    def product(kernel, name, outs, operands, scratch, passes=1):
        return pl.pallas_call(
            kernel,
            out_shape=outs,
            in_specs=[SMEM] * 2 + [VMEM] * len(operands) + [HBM],
            out_specs=[VMEM] * len(outs),
            scratch_shapes=stream + scratch,
            compiler_params=large,
            cost_estimate=pl.CostEstimate(
                flops=passes * half_flops, bytes_accessed=passes * half_bytes, transcendentals=0
            ),
            name=name,
        )(core, blocks, *operands, ptdf_tiles)

    def small(kernel, name, outs, operands):
        return pl.pallas_call(
            kernel,
            out_shape=outs,
            in_specs=[VMEM] * len(operands),
            out_specs=[VMEM] * len(outs),
            compiler_params=SMALL,
            cost_estimate=pl.CostEstimate(flops=half_flops, bytes_accessed=4 << 20, transcendentals=0),
            name=name,
        )(*operands)

    high = soc_init.astype(jnp.bfloat16)
    low = (soc_init - high.astype(jnp.float32)).astype(jnp.bfloat16)
    own = jnp.concatenate([high, low], axis=1)[:, None, :]
    sent = jnp.concatenate(
        [base_injection.reshape(hour_rows, devices, buses), jnp.broadcast_to(own, (hour_rows, devices, 2 * units))], axis=2
    )
    came = lax.all_to_all(jnp.swapaxes(sent, 0, 1), "tm", split_axis=0, concat_axis=0, tiled=True)
    came = came.reshape(hours, buses + 2 * units)
    base = came[:, :buses]
    level = came[:, buses : buses + units].astype(jnp.float32) + came[:, buses + units :].astype(jnp.float32)

    away, picked = product(first_flow_kernel, "first_flow", [flow_shape, picked_shape], [base], [])
    (delta,) = small(storage_kernel, "storage", [block_shape], [level, unit_block, unit_lane])
    line_dual = jnp.zeros((own_groups, hours, lines), jnp.float32)
    inject = None
    for iteration in range(ITERS):
        arrived = lax.ppermute(away, "tm", sibling)
        (flows,) = product(own_flow_kernel, "own_flow", [flow_shape], [picked], [])
        pair = (flows + arrived).astype(jnp.bfloat16).reshape(chips, own_groups, hours, lines)
        parts = lax.all_to_all(pair, "tm", split_axis=0, concat_axis=0, axis_index_groups=same_core, tiled=True)
        shifted = jnp.sum(parts.astype(jnp.float32), axis=0) + line_dual
        clipped = jnp.clip(shifted, -own_limits, own_limits)
        line_dual = shifted - clipped
        dual = jnp.broadcast_to(line_dual.astype(jnp.bfloat16)[None], (chips, own_groups, hours, lines))
        dual = lax.all_to_all(dual, "tm", split_axis=0, concat_axis=0, axis_index_groups=same_core, tiled=True)
        dual = dual.reshape(half_groups, hours, lines)
        other = lax.ppermute(dual, "tm", sibling)
        (before,) = product(own_price_kernel, "own_price", [block_shape], [dual], sums)
        if iteration < ITERS - 1:
            price, inject, picked, away = product(
                middle_kernel,
                "price_then_flow",
                [block_shape, block_shape, picked_shape, flow_shape],
                [other, before, base, delta],
                sums,
                2,
            )
            level, delta = small(
                level_kernel, "storage", [level_shape, block_shape], [price, level, unit_block, unit_lane, gain]
            )
        else:
            inject, level = product(
                last_kernel,
                "last_price",
                [jax.ShapeDtypeStruct((hours, buses), jnp.float32), level_shape],
                [other, before, base, inject, delta, level, unit_block, unit_lane, gain],
                [pltpu.VMEM(block_shape.shape, block_shape.dtype)] + sums,
            )

    duals = own_groups * lines
    joined = jnp.concatenate([inject, level, jnp.swapaxes(line_dual, 0, 1).reshape(hours, duals)], axis=1)
    back = lax.all_to_all(
        joined.reshape(devices, hour_rows, buses + units + duals), "tm", split_axis=0, concat_axis=0, tiled=True
    )
    inject = jnp.swapaxes(back[:, :, :buses], 0, 1).reshape(hour_rows, bus_count)
    level = jnp.sum(back[:, :, buses : buses + units], axis=0)
    own_dual = jnp.swapaxes(back[:, :, buses + units :], 0, 1).reshape(hour_rows, line_count)
    return (inject, own_dual, level)


def solution(mesh):
    in_specs = (
        P(("scen", "tm"), None),
        P(None, "tm", None, None),
        P(None, "tm"),
        P(),
        P(),
        P(),
        P(("scen", "tm"), None),
    )
    out_specs = (P(("scen", "tm"), None), P(("scen", "tm"), None), P(("scen", "tm"), None))
    return jax.shard_map(shards, mesh=mesh, in_specs=in_specs, out_specs=out_specs, check_vma=False)
```

```python
import functools

import jax
import jax.numpy as jnp
from jax import lax
from jax.experimental import pallas as pl
from jax.experimental.pallas import tpu as pltpu
from jax.sharding import PartitionSpec as P

ITERS = 2


step_size = 0.5
penalty = 4.0
ramp_weight = 0.5

NT = (((1,), (1,)), ((), ()))
VMEM = pl.BlockSpec(memory_space=pltpu.VMEM)
SMEM = pl.BlockSpec(memory_space=pltpu.SMEM)
HBM = pl.BlockSpec(memory_space=pl.ANY)
SMALL = pltpu.CompilerParams(vmem_limit_bytes=12 << 20)
STRAIGHT = 16


def partner(chip, slot, chips):
    if chips & (chips - 1) == 0:
        return chip ^ slot
    return (chip + slot) % chips


class Half:
    def __init__(self, chip, core, blocks, tiles_hbm, tiles, sems):
        self.chip, self.core = chip, core
        self.blocks, self.tiles_hbm, self.tiles, self.sems = blocks, tiles_hbm, tiles, sems
        self.chunks = sems.shape[0]
        self.own = tiles.shape[0] // self.chunks

    def first_group(self, chunk):
        return (2 * partner(self.chip, chunk, self.chunks) + self.core) * self.own

    def fetch(self, chunk):
        there = pl.ds(self.first_group(chunk), self.own)
        here = pl.ds(chunk * self.own, self.own)
        return pltpu.make_async_copy(self.tiles_hbm.at[there], self.tiles.at[here], self.sems.at[chunk])

    def start(self):
        for chunk in range(self.chunks):
            self.fetch(chunk).start()

    def each_four(self, wait, four):
        depth = self.tiles.shape[1]
        per = max(1, STRAIGHT // self.own)

        def body(step, carry):
            for c in range(per):
                chunk = step * per + c
                if wait:
                    self.fetch(chunk).wait()
                for sub in range(0, self.own, 4):
                    first = (self.first_group(chunk) + sub) * depth
                    four(chunk * self.own + sub, lambda u, k: self.blocks[first + u * depth + k])
            return carry

        lax.fori_loop(0, self.chunks // per, body, 0)


def wide(parts):
    return jnp.concatenate([jnp.concatenate(row, axis=1) for row in parts], axis=0)


def flow_pass(picked, half, flows, wait):
    tiles = half.tiles
    depth, lines = tiles.shape[1], tiles.shape[2]
    hours = picked.shape[1]

    def four(base, block):
        rows = [[picked[block(u, k)] for k in range(depth)] for u in range(4)]
        zero = jnp.zeros_like(rows[0][0])
        totals = [None] * 4

        def add(u, part):
            totals[u] = part if totals[u] is None else totals[u] + part

        for first in (0, 2):
            for k in range(0, depth - 1, 2):
                left = wide([[rows[first][k], rows[first][k + 1]], [rows[first + 1][k], rows[first + 1][k + 1]]])
                g = base + first
                right = wide([[tiles[g, k], tiles[g, k + 1]], [tiles[g + 1, k], tiles[g + 1, k + 1]]])
                part = lax.dot_general(left, right, NT, preferred_element_type=jnp.float32)
                add(first, part[:hours, :lines])
                add(first + 1, part[hours:, lines:])
        if depth % 2:
            k = depth - 1
            left = wide([[rows[0][k], zero], [rows[1][k], zero], [zero, rows[2][k]], [zero, rows[3][k]]])
            right = wide([[tiles[base, k], tiles[base + 2, k]], [tiles[base + 1, k], tiles[base + 3, k]]])
            part = lax.dot_general(left, right, NT, preferred_element_type=jnp.float32)
            for u in range(4):
                at = (u % 2) * lines
                add(u, part[u * hours : (u + 1) * hours, at : at + lines])
        for u in range(4):
            flows[base + u] = totals[u].astype(flows.dtype)

    half.each_four(wait, four)


def price_pass(dual, half, sums, wait):
    tiles = half.tiles
    depth, width = tiles.shape[1], tiles.shape[3]
    hours = dual.shape[1]
    for ref in sums:
        ref[...] = jnp.zeros_like(ref)

    def four(base, block):
        rows = [dual[base + u] for u in range(4)]
        zero = jnp.zeros_like(rows[0])
        parts = []
        for first in (0, 2):
            left = wide([[rows[first], zero], [zero, rows[first + 1]]])
            for k in range(0, depth - 1, 2):
                g = base + first
                right = wide([[tiles[g, k], tiles[g, k + 1]], [tiles[g + 1, k], tiles[g + 1, k + 1]]])
                part = jnp.dot(left, right, preferred_element_type=jnp.float32)
                for u in range(2):
                    for j in range(2):
                        piece = part[u * hours : (u + 1) * hours, j * width : (j + 1) * width]
                        parts.append((first + u, k + j, piece))
        if depth % 2:
            k = depth - 1
            left = wide([[rows[0], zero], [zero, rows[1]], [rows[2], zero], [zero, rows[3]]])
            right = wide([[tiles[base, k], tiles[base + 2, k]], [tiles[base + 1, k], tiles[base + 3, k]]])
            part = jnp.dot(left, right, preferred_element_type=jnp.float32)
            for u in range(4):
                at = (u // 2) * width
                parts.append((u, k, part[u * hours : (u + 1) * hours, at : at + width]))
        for u, k, part in parts:
            at = block(u, k)
            sums[k][at] = sums[k][at] + part

    half.each_four(wait, four)


def earlier(values):
    return jnp.concatenate([values[-1:], values[:-1]], axis=0)


def later(values):
    return jnp.concatenate([values[1:], values[:1]], axis=0)


def total(sums, block):
    price = sums[0][block]
    for ref in sums[1:]:
        price = price + ref[block]
    return price


def update_pass(sums, before, inject, base, delta, price_out, out):
    for block in range(sums[0].shape[0]):
        price = before[block] + total(sums, block)
        price_out[block] = price
        now = inject(block)
        new = now - step_size * (
            (now - base(block))
            + penalty * price
            + ramp_weight * (2.0 * now - earlier(now) - later(now))
        )
        out(block, new - delta[block])


def level_pass(price, level, unit_block, unit_lane, gain, out, mine):
    count, hours, width = price.shape

    def body(c, carry):
        cols = pl.ds(pl.multiple_of(c * width, width), width)
        block = jnp.broadcast_to(unit_block[:, cols], (hours, width))
        lane = jnp.broadcast_to(unit_lane[:, cols], (hours, width))
        found = jnp.zeros((hours, width), jnp.float32)
        for b in range(count):
            found = jnp.where(block == b, jnp.take_along_axis(price[b], lane, axis=1), found)
        now = level[:, cols]
        new = 0.5 * (now + earlier(now)) - gain[:, cols] * found
        if mine:
            new = jnp.where((block >= 0) & (block < count), new, 0.0)
        out[:, cols] = new
        return carry

    lax.fori_loop(0, level.shape[1] // width, body, 0)


def pack_kernel(base, soc, out):
    devices, rows, width = out.shape
    hour_rows = soc.shape[0]
    count = base.shape[1] // devices
    units = soc.shape[1]
    pad = jnp.zeros((rows // hour_rows - count - units, width), jnp.float32)
    for d in range(devices):
        parts = []
        for r in range(hour_rows):
            parts += [base[r, d * count : (d + 1) * count], soc[r], pad]
        out[d] = jnp.concatenate(parts, axis=0).astype(out.dtype)


def first_flow_kernel(place, blocks, came, tiles_hbm, flows, picked, level, tiles, sems, flat):
    half = Half(place[0], 1 - place[1], blocks, tiles_hbm, tiles, sems)
    half.start()
    count, hours, width = picked.shape
    flat[...] = came[...].astype(jnp.float32)
    rows = flat.shape[0] // hours
    for b in range(count):
        picked[b] = flat[pl.ds(b, hours, stride=rows), :].astype(picked.dtype)
    for c in range(level.shape[1] // width):
        level[:, c * width : (c + 1) * width] = flat[pl.ds(count + c, hours, stride=rows), :]
    flow_pass(picked, half, flows, True)


def own_flow_kernel(place, blocks, picked, tiles_hbm, flows, tiles, sems):
    half = Half(place[0], place[1], blocks, tiles_hbm, tiles, sems)
    half.start()
    flow_pass(picked, half, flows, True)


def own_price_kernel(place, blocks, dual, tiles_hbm, price, tiles, sems, *sums):
    half = Half(place[0], place[1], blocks, tiles_hbm, tiles, sems)
    half.start()
    price_pass(dual, half, sums, True)
    for b in range(price.shape[0]):
        price[b] = total(sums, b)


def middle_kernel(
    place, blocks, dual, before, base, delta, tiles_hbm,
    price, inject_out, picked, flows, tiles, sems, *sums
):
    half = Half(place[0], 1 - place[1], blocks, tiles_hbm, tiles, sems)
    half.start()
    price_pass(dual, half, sums, True)

    def start(b):
        return base[b].astype(jnp.float32)

    def write(b, new):
        inject_out[b] = new
        picked[b] = new.astype(picked.dtype)

    update_pass(sums, before, start, start, delta, price, write)
    flow_pass(picked, half, flows, False)


def last_kernel(
    place, blocks, dual, before, base, inject, delta, level, line_dual, unit_block, unit_lane, gain, tiles_hbm,
    out, tiles, sems, price, level_out, flat, *sums
):
    half = Half(place[0], 1 - place[1], blocks, tiles_hbm, tiles, sems)
    half.start()
    count, hours, width = price.shape
    rows = flat.shape[0] // hours
    flat[...] = jnp.zeros_like(flat)
    units = level.shape[1] // width
    for g in range(line_dual.shape[0]):
        flat[pl.ds(count + units + g, hours, stride=rows), :] = line_dual[g]
    price_pass(dual, half, sums, True)

    def start(b):
        return base[b].astype(jnp.float32)

    def write(b, new):
        flat[pl.ds(b, hours, stride=rows), :] = new

    update_pass(sums, before, lambda b: inject[b], start, delta, price, write)
    level_pass(price, level, unit_block, unit_lane, gain, level_out, True)
    for c in range(units):
        flat[pl.ds(count + c, hours, stride=rows), :] = level_out[:, c * width : (c + 1) * width]
    out[...] = flat[...].astype(out.dtype)


def unpack_kernel(back, inject, line_dual, level):
    devices = back.shape[0]
    hour_rows, units = level.shape[0], level.shape[1]
    count, own = inject.shape[1] // devices, line_dual.shape[1] // devices
    rows = back.shape[1] // hour_rows
    for r in range(hour_rows):
        sum_levels = None
        for d in range(devices):
            came = back[d, r * rows : (r + 1) * rows].astype(jnp.float32)
            inject[r, d * count : (d + 1) * count] = came[:count]
            line_dual[r, d * own : (d + 1) * own] = came[count + units : count + units + own]
            part = came[count : count + units]
            sum_levels = part if sum_levels is None else sum_levels + part
        level[r] = sum_levels


def storage_pass(level, unit_block, unit_lane, delta):
    count, hours, width = delta.shape
    units = level.shape[1]
    span = 2 * width
    delta[...] = jnp.zeros_like(delta)

    def body(c, carry):
        cols = pl.ds(pl.multiple_of(c * span, span), span)
        now = level[:, cols]
        charge = step_size * (now - earlier(now))
        high = charge.astype(jnp.bfloat16).astype(jnp.float32)
        low = charge - high
        lane = jnp.broadcast_to(unit_lane[:, cols], (width, span))
        hot = (lane == lax.broadcasted_iota(jnp.int32, (width, span), 0)).astype(jnp.bfloat16)
        block = jnp.broadcast_to(unit_block[:, cols], (hours, span))
        for b in range(count):
            held = block == b
            both = jnp.concatenate([jnp.where(held, high, 0.0), jnp.where(held, low, 0.0)], axis=0)
            part = lax.dot_general(both.astype(jnp.bfloat16), hot, NT, preferred_element_type=jnp.float32)
            delta[b] = delta[b] + (part[:hours] + part[hours:])
        return carry

    lax.fori_loop(0, units // span, body, 0)


def storage_kernel(level, unit_block, unit_lane, delta):
    storage_pass(level, unit_block, unit_lane, delta)


def level_kernel(price, level, unit_block, unit_lane, gain, level_out, delta):
    level_pass(price, level, unit_block, unit_lane, gain, level_out, False)
    storage_pass(level_out, unit_block, unit_lane, delta)


def shards(base_injection, ptdf_tiles, tile_block, limits, stor_bus, stor_gain, soc_init):
    hour_rows = base_injection.shape[0]
    bus_count = base_injection.shape[1]
    line_count = limits.shape[0]
    groups, depth, lines, width = ptdf_tiles.shape
    units = stor_bus.shape[0]
    devices = lax.axis_size("tm")
    me = lax.axis_index("tm")
    buses = bus_count // devices
    bus_blocks = buses // width
    hours = hour_rows * devices
    own_groups = groups // devices
    blocks = tile_block.reshape(groups * depth)
    unit_block = (stor_bus // width - me * bus_blocks).reshape(1, units)
    unit_lane = (stor_bus % width).reshape(1, units)
    gain = stor_gain.reshape(1, units)
    own_limits = lax.dynamic_slice_in_dim(limits.reshape(groups, 1, lines), me * own_groups, own_groups, 0)

    chips = devices // 2
    half_groups = chips * own_groups
    place = jnp.stack([me // 2, me % 2])
    sibling = [(d, d + 1 - 2 * (d % 2)) for d in range(devices)]

    def to_partner(slot):
        return [(d, 2 * partner(d // 2, slot, chips) + d % 2) for d in range(devices)]

    def from_partner(slot):
        return [(target, source) for source, target in to_partner(slot)]

    half_bytes = ptdf_tiles.size
    half_flops = hours * ptdf_tiles.size
    stream = [pltpu.VMEM((half_groups, *ptdf_tiles.shape[1:]), ptdf_tiles.dtype), pltpu.SemaphoreType.DMA((chips,))]
    sums = [pltpu.VMEM((bus_blocks, hours, width), jnp.float32)] * depth
    large = pltpu.CompilerParams(vmem_limit_bytes=48 << 20)
    picked_shape = jax.ShapeDtypeStruct((bus_blocks, hours, width), jnp.bfloat16)
    block_shape = jax.ShapeDtypeStruct((bus_blocks, hours, width), jnp.float32)
    level_shape = jax.ShapeDtypeStruct((hours, units), jnp.float32)
    flow_shape = jax.ShapeDtypeStruct((half_groups, hours, lines), jnp.float32)

    def product(kernel, name, outs, operands, scratch, passes=1):
        return pl.pallas_call(
            kernel,
            out_shape=outs,
            in_specs=[SMEM] * 2 + [VMEM] * len(operands) + [HBM],
            out_specs=[VMEM] * len(outs),
            scratch_shapes=stream + scratch,
            compiler_params=large,
            cost_estimate=pl.CostEstimate(
                flops=passes * half_flops, bytes_accessed=passes * half_bytes, transcendentals=0
            ),
            name=name,
        )(place, blocks, *operands, ptdf_tiles)

    def small(kernel, name, outs, operands):
        return pl.pallas_call(
            kernel,
            out_shape=outs,
            in_specs=[VMEM] * len(operands),
            out_specs=[VMEM] * len(outs),
            compiler_params=SMALL,
            cost_estimate=pl.CostEstimate(flops=half_flops, bytes_accessed=4 << 20, transcendentals=0),
            name=name,
        )(*operands)

    unit_rows = units // width

    def whole_tiles(rows):
        return -(-rows // 16) * 16

    rows_in = whole_tiles(bus_blocks + unit_rows)
    rows_out = whole_tiles(bus_blocks + unit_rows + own_groups)
    (sent,) = small(
        pack_kernel,
        "pack",
        [jax.ShapeDtypeStruct((devices, hour_rows * rows_in, width), jnp.bfloat16)],
        [
            base_injection.astype(jnp.float32).reshape(hour_rows, bus_count // width, width),
            soc_init.reshape(hour_rows, unit_rows, width),
        ],
    )
    came = lax.all_to_all(sent, "tm", split_axis=0, concat_axis=0, tiled=True)
    away, base, level = product(
        first_flow_kernel,
        "first_flow",
        [flow_shape, picked_shape, level_shape],
        [came.reshape(hours * rows_in, width)],
        [pltpu.VMEM((hours * rows_in, width), jnp.float32)],
    )
    picked = base
    price = None
    line_dual = jnp.zeros((own_groups, hours, lines), jnp.float32)
    for iteration in range(ITERS):
        arrived = lax.ppermute(away, "tm", sibling).reshape(chips, own_groups, hours, lines)
        (flows,) = product(own_flow_kernel, "own_flow", [flow_shape], [picked], [])
        flows = flows.reshape(chips, own_groups, hours, lines)
        parts = [
            lax.ppermute((flows[slot] + arrived[slot]).astype(jnp.bfloat16), "tm", to_partner(slot))
            for slot in range(1, chips)
        ]
        if iteration == 0:
            (delta,) = small(storage_kernel, "storage", [block_shape], [level, unit_block, unit_lane])
        else:
            level, delta = small(
                level_kernel, "storage", [level_shape, block_shape], [price, level, unit_block, unit_lane, gain]
            )
        parts, level, delta = lax.optimization_barrier((parts, level, delta))
        shifted = flows[0] + arrived[0] + line_dual
        for part in parts:
            shifted = shifted + part.astype(jnp.float32)
        clipped = jnp.clip(shifted, -own_limits, own_limits)
        line_dual = shifted - clipped
        dual = line_dual.astype(jnp.bfloat16)
        dual = jnp.concatenate(
            [dual] + [lax.ppermute(dual, "tm", from_partner(slot)) for slot in range(1, chips)], axis=0
        )
        other = lax.ppermute(dual, "tm", sibling)
        (before,) = product(own_price_kernel, "own_price", [block_shape], [dual], sums)
        if iteration < ITERS - 1:
            price, inject, picked, away = product(
                middle_kernel,
                "price_then_flow",
                [block_shape, block_shape, picked_shape, flow_shape],
                [other, before, base, delta],
                sums,
                2,
            )
        else:
            (out,) = product(
                last_kernel,
                "last_price",
                [jax.ShapeDtypeStruct((hours * rows_out, width), jnp.bfloat16)],
                [other, before, base, inject, delta, level, line_dual, unit_block, unit_lane, gain],
                [
                    pltpu.VMEM(block_shape.shape, jnp.float32),
                    pltpu.VMEM(level_shape.shape, jnp.float32),
                    pltpu.VMEM((hours * rows_out, width), jnp.float32),
                ]
                + sums,
            )

    back = lax.all_to_all(
        out.reshape(devices, hour_rows * rows_out, width), "tm", split_axis=0, concat_axis=0, tiled=True
    )
    inject, own_dual, level = small(
        unpack_kernel,
        "unpack",
        [
            jax.ShapeDtypeStruct((hour_rows, bus_count // width, width), jnp.float32),
            jax.ShapeDtypeStruct((hour_rows, line_count // width, width), jnp.float32),
            jax.ShapeDtypeStruct((hour_rows, unit_rows, width), jnp.float32),
        ],
        [back],
    )
    inject = inject.reshape(hour_rows, bus_count)
    own_dual = own_dual.reshape(hour_rows, line_count)
    level = level.reshape(hour_rows, units)
    return (inject, own_dual, level)


def solution(mesh):
    in_specs = (
        P(("scen", "tm"), None),
        P(None, "tm", None, None),
        P(None, "tm"),
        P(),
        P(),
        P(),
        P(("scen", "tm"), None),
    )
    out_specs = (P(("scen", "tm"), None), P(("scen", "tm"), None), P(("scen", "tm"), None))
    return jax.shard_map(shards, mesh=mesh, in_specs=in_specs, out_specs=out_specs, check_vma=False)
```

```python
import functools

import jax
import jax.numpy as jnp
from jax import lax
from jax.experimental import pallas as pl
from jax.experimental.pallas import tpu as pltpu
from jax.sharding import PartitionSpec as P

ITERS = 2


step_size = 0.5
penalty = 4.0
ramp_weight = 0.5

NT = (((1,), (1,)), ((), ()))
VMEM = pl.BlockSpec(memory_space=pltpu.VMEM)
HBM = pl.BlockSpec(memory_space=pl.ANY)
SMALL = pltpu.CompilerParams(vmem_limit_bytes=12 << 20)
STRAIGHT = 16


class Half:
    def __init__(self, sibling, blocks_hbm, tiles_hbm, tiles, sems, blocks, block_sem):
        me = lax.axis_index("tm")
        self.core = 1 - me % 2 if sibling else me % 2
        self.blocks, self.tiles_hbm, self.tiles, self.sems = blocks, tiles_hbm, tiles, sems
        self.chunks = sems.shape[0]
        self.own = tiles.shape[0] // self.chunks
        for chunk in range(self.chunks):
            self.fetch(chunk).start()
        self.block_copy = pltpu.make_async_copy(blocks_hbm, blocks, block_sem)
        self.block_copy.start()

    def first_group(self, chunk):
        return (2 * chunk + self.core) * self.own

    def fetch(self, chunk):
        there = pl.ds(self.first_group(chunk), self.own)
        here = pl.ds(chunk * self.own, self.own)
        return pltpu.make_async_copy(self.tiles_hbm.at[there], self.tiles.at[here], self.sems.at[chunk])

    def each_four(self, wait, four):
        depth = self.tiles.shape[1]
        if wait:
            self.block_copy.wait()
        per = max(1, STRAIGHT // self.own)

        def body(step, carry):
            for c in range(per):
                chunk = step * per + c
                if wait:
                    self.fetch(chunk).wait()
                for sub in range(0, self.own, 4):
                    first = (self.first_group(chunk) + sub) * depth
                    four(chunk * self.own + sub, lambda u, k: self.blocks[first + u * depth + k])
            return carry

        lax.fori_loop(0, self.chunks // per, body, 0)


def wide(parts):
    return jnp.concatenate([jnp.concatenate(row, axis=1) for row in parts], axis=0)


def flow_pass(picked, half, flows, wait):
    tiles = half.tiles
    depth, lines = tiles.shape[1], tiles.shape[2]
    hours = picked.shape[1]

    def four(base, block):
        rows = [[picked[block(u, k)] for k in range(depth)] for u in range(4)]
        zero = jnp.zeros_like(rows[0][0])
        totals = [None] * 4

        def add(u, part):
            totals[u] = part if totals[u] is None else totals[u] + part

        for first in (0, 2):
            for k in range(0, depth - 1, 2):
                left = wide([[rows[first][k], rows[first][k + 1]], [rows[first + 1][k], rows[first + 1][k + 1]]])
                g = base + first
                right = wide([[tiles[g, k], tiles[g, k + 1]], [tiles[g + 1, k], tiles[g + 1, k + 1]]])
                part = lax.dot_general(left, right, NT, preferred_element_type=jnp.float32)
                add(first, part[:hours, :lines])
                add(first + 1, part[hours:, lines:])
        if depth % 2:
            k = depth - 1
            left = wide([[rows[0][k], zero], [rows[1][k], zero], [zero, rows[2][k]], [zero, rows[3][k]]])
            right = wide([[tiles[base, k], tiles[base + 2, k]], [tiles[base + 1, k], tiles[base + 3, k]]])
            part = lax.dot_general(left, right, NT, preferred_element_type=jnp.float32)
            for u in range(4):
                at = (u % 2) * lines
                add(u, part[u * hours : (u + 1) * hours, at : at + lines])
        for u in range(4):
            flows[base + u] = totals[u].astype(flows.dtype)

    half.each_four(wait, four)


def price_pass(dual, half, sums, wait):
    tiles = half.tiles
    depth, width = tiles.shape[1], tiles.shape[3]
    hours = dual.shape[1]
    for ref in sums:
        ref[...] = jnp.zeros_like(ref)

    def four(base, block):
        rows = [dual[base + u] for u in range(4)]
        zero = jnp.zeros_like(rows[0])
        parts = []
        for first in (0, 2):
            left = wide([[rows[first], zero], [zero, rows[first + 1]]])
            for k in range(0, depth - 1, 2):
                g = base + first
                right = wide([[tiles[g, k], tiles[g, k + 1]], [tiles[g + 1, k], tiles[g + 1, k + 1]]])
                part = jnp.dot(left, right, preferred_element_type=jnp.float32)
                for u in range(2):
                    for j in range(2):
                        piece = part[u * hours : (u + 1) * hours, j * width : (j + 1) * width]
                        parts.append((first + u, k + j, piece))
        if depth % 2:
            k = depth - 1
            left = wide([[rows[0], zero], [zero, rows[1]], [rows[2], zero], [zero, rows[3]]])
            right = wide([[tiles[base, k], tiles[base + 2, k]], [tiles[base + 1, k], tiles[base + 3, k]]])
            part = jnp.dot(left, right, preferred_element_type=jnp.float32)
            for u in range(4):
                at = (u // 2) * width
                parts.append((u, k, part[u * hours : (u + 1) * hours, at : at + width]))
        for u, k, part in parts:
            at = block(u, k)
            sums[k][at] = sums[k][at] + part

    half.each_four(wait, four)


def earlier(values):
    return jnp.concatenate([values[-1:], values[:-1]], axis=0)


def later(values):
    return jnp.concatenate([values[1:], values[:1]], axis=0)


def total(sums, block):
    price = sums[0][block]
    for ref in sums[1:]:
        price = price + ref[block]
    return price


def update_pass(sums, before, inject, base, delta, price_out, out):
    for block in range(sums[0].shape[0]):
        price = before[block] + total(sums, block)
        price_out[block] = price
        now = inject(block)
        new = now - step_size * (
            (now - base(block))
            + penalty * price
            + ramp_weight * (2.0 * now - earlier(now) - later(now))
        )
        out(block, new - delta[block])


def level_pass(price, level, unit_block, unit_lane, gain, out, mine):
    count, hours, width = price.shape

    def body(c, carry):
        cols = pl.ds(pl.multiple_of(c * width, width), width)
        block = jnp.broadcast_to(unit_block[:, cols], (hours, width))
        lane = jnp.broadcast_to(unit_lane[:, cols], (hours, width))
        found = jnp.zeros((hours, width), jnp.float32)
        for b in range(count):
            found = jnp.where(block == b, jnp.take_along_axis(price[b], lane, axis=1), found)
        now = level[:, cols]
        new = 0.5 * (now + earlier(now)) - gain[:, cols] * found
        if mine:
            new = jnp.where((block >= 0) & (block < count), new, 0.0)
        out[:, cols] = new
        return carry

    lax.fori_loop(0, level.shape[1] // width, body, 0)


def pack_kernel(base, soc, out):
    devices, rows, width = out.shape
    hour_rows = soc.shape[0]
    count = base.shape[1] // devices
    units = soc.shape[1]
    pad = jnp.zeros((rows // hour_rows - count - units, width), jnp.float32)
    for d in range(devices):
        parts = []
        for r in range(hour_rows):
            parts += [base[r, d * count : (d + 1) * count], soc[r], pad]
        out[d] = jnp.concatenate(parts, axis=0).astype(out.dtype)


def first_flow_kernel(blocks_hbm, tiles_hbm, came, flows, picked, level, *scratch):
    stream, (flat,) = (blocks_hbm, tiles_hbm, *scratch[:4]), scratch[4:]
    half = Half(True, *stream)
    count, hours, width = picked.shape
    flat[...] = came[...].astype(jnp.float32)
    rows = flat.shape[0] // hours
    for b in range(count):
        picked[b] = flat[pl.ds(b, hours, stride=rows), :].astype(picked.dtype)
    for c in range(level.shape[1] // width):
        level[:, c * width : (c + 1) * width] = flat[pl.ds(count + c, hours, stride=rows), :]
    flow_pass(picked, half, flows, True)


def own_flow_kernel(blocks_hbm, tiles_hbm, picked, flows, *scratch):
    stream = (blocks_hbm, tiles_hbm, *scratch)
    half = Half(False, *stream)
    flow_pass(picked, half, flows, True)


def own_price_kernel(blocks_hbm, tiles_hbm, dual, price, *scratch):
    stream, sums = (blocks_hbm, tiles_hbm, *scratch[:4]), scratch[4:]
    half = Half(False, *stream)
    price_pass(dual, half, sums, True)
    for b in range(price.shape[0]):
        price[b] = total(sums, b)


def middle_kernel(
    blocks_hbm, tiles_hbm, dual, before, base, delta, price, inject_out, picked, flows, *scratch
):
    stream, sums = (blocks_hbm, tiles_hbm, *scratch[:4]), scratch[4:]
    half = Half(True, *stream)
    price_pass(dual, half, sums, True)

    def start(b):
        return base[b].astype(jnp.float32)

    def write(b, new):
        inject_out[b] = new
        picked[b] = new.astype(picked.dtype)

    update_pass(sums, before, start, start, delta, price, write)
    flow_pass(picked, half, flows, False)


def last_kernel(
    blocks_hbm, tiles_hbm, dual, before, base, inject, delta, level, line_dual, unit_block, unit_lane, gain,
    out, *scratch
):
    stream, (price, level_out, flat, *sums) = (blocks_hbm, tiles_hbm, *scratch[:4]), scratch[4:]
    half = Half(True, *stream)
    count, hours, width = price.shape
    rows = flat.shape[0] // hours
    flat[...] = jnp.zeros_like(flat)
    units = level.shape[1] // width
    for g in range(line_dual.shape[0]):
        flat[pl.ds(count + units + g, hours, stride=rows), :] = line_dual[g]
    price_pass(dual, half, sums, True)

    def start(b):
        return base[b].astype(jnp.float32)

    def write(b, new):
        flat[pl.ds(b, hours, stride=rows), :] = new

    update_pass(sums, before, lambda b: inject[b], start, delta, price, write)
    level_pass(price, level, unit_block, unit_lane, gain, level_out, True)
    for c in range(units):
        flat[pl.ds(count + c, hours, stride=rows), :] = level_out[:, c * width : (c + 1) * width]
    out[...] = flat[...].astype(out.dtype)


def unpack_kernel(back, inject, line_dual, level):
    devices = back.shape[0]
    hour_rows, units = level.shape[0], level.shape[1]
    count, own = inject.shape[1] // devices, line_dual.shape[1] // devices
    rows = back.shape[1] // hour_rows
    for r in range(hour_rows):
        sum_levels = None
        for d in range(devices):
            came = back[d, r * rows : (r + 1) * rows].astype(jnp.float32)
            inject[r, d * count : (d + 1) * count] = came[:count]
            line_dual[r, d * own : (d + 1) * own] = came[count + units : count + units + own]
            part = came[count : count + units]
            sum_levels = part if sum_levels is None else sum_levels + part
        level[r] = sum_levels


def storage_pass(level, unit_block, unit_lane, delta):
    count, hours, width = delta.shape
    units = level.shape[1]
    span = 2 * width
    delta[...] = jnp.zeros_like(delta)

    def body(c, carry):
        cols = pl.ds(pl.multiple_of(c * span, span), span)
        now = level[:, cols]
        charge = step_size * (now - earlier(now))
        high = charge.astype(jnp.bfloat16).astype(jnp.float32)
        low = charge - high
        lane = jnp.broadcast_to(unit_lane[:, cols], (width, span))
        hot = (lane == lax.broadcasted_iota(jnp.int32, (width, span), 0)).astype(jnp.bfloat16)
        block = jnp.broadcast_to(unit_block[:, cols], (hours, span))
        for b in range(count):
            held = block == b
            both = jnp.concatenate([jnp.where(held, high, 0.0), jnp.where(held, low, 0.0)], axis=0)
            part = lax.dot_general(both.astype(jnp.bfloat16), hot, NT, preferred_element_type=jnp.float32)
            delta[b] = delta[b] + (part[:hours] + part[hours:])
        return carry

    lax.fori_loop(0, units // span, body, 0)


def storage_kernel(level, unit_block, unit_lane, delta):
    storage_pass(level, unit_block, unit_lane, delta)


def level_kernel(price, level, unit_block, unit_lane, gain, level_out, delta):
    level_pass(price, level, unit_block, unit_lane, gain, level_out, False)
    storage_pass(level_out, unit_block, unit_lane, delta)


def shards(base_injection, ptdf_tiles, tile_block, limits, stor_bus, stor_gain, soc_init):
    hour_rows = base_injection.shape[0]
    bus_count = base_injection.shape[1]
    line_count = limits.shape[0]
    groups, depth, lines, width = ptdf_tiles.shape
    units = stor_bus.shape[0]
    devices = lax.axis_size("tm")
    me = lax.axis_index("tm")
    buses = bus_count // devices
    bus_blocks = buses // width
    hours = hour_rows * devices
    own_groups = groups // devices
    blocks = tile_block.reshape(groups * depth)
    unit_block = (stor_bus // width - me * bus_blocks).reshape(1, units)
    unit_lane = (stor_bus % width).reshape(1, units)
    gain = stor_gain.reshape(1, units)
    own_limits = lax.dynamic_slice_in_dim(limits.reshape(groups, 1, lines), me * own_groups, own_groups, 0)

    chips = devices // 2
    half_groups = chips * own_groups
    sibling = [(d, d + 1 - 2 * (d % 2)) for d in range(devices)]

    same_core = [[2 * chip + c for chip in range(chips)] for c in range(2)]

    def exchange(value):
        return lax.all_to_all(value, "tm", split_axis=0, concat_axis=0, axis_index_groups=same_core, tiled=True)

    half_bytes = ptdf_tiles.size
    half_flops = hours * ptdf_tiles.size
    stream = [pltpu.VMEM((half_groups, *ptdf_tiles.shape[1:]), ptdf_tiles.dtype), pltpu.SemaphoreType.DMA((chips,))]
    stream += [pltpu.SMEM(blocks.shape, blocks.dtype), pltpu.SemaphoreType.DMA]
    sums = [pltpu.VMEM((bus_blocks, hours, width), jnp.float32)] * depth
    large = pltpu.CompilerParams(vmem_limit_bytes=48 << 20)
    picked_shape = jax.ShapeDtypeStruct((bus_blocks, hours, width), jnp.bfloat16)
    block_shape = jax.ShapeDtypeStruct((bus_blocks, hours, width), jnp.float32)
    level_shape = jax.ShapeDtypeStruct((hours, units), jnp.float32)
    flow_shape = jax.ShapeDtypeStruct((half_groups, hours, lines), jnp.float32)

    def product(kernel, name, outs, operands, scratch, passes=1):
        return pl.pallas_call(
            kernel,
            out_shape=outs,
            in_specs=[HBM] * 2 + [VMEM] * len(operands),
            out_specs=[VMEM] * len(outs),
            scratch_shapes=stream + scratch,
            compiler_params=large,
            cost_estimate=pl.CostEstimate(
                flops=passes * half_flops, bytes_accessed=passes * half_bytes, transcendentals=0
            ),
            name=name,
        )(blocks, ptdf_tiles, *operands)

    def small(kernel, name, outs, operands):
        return pl.pallas_call(
            kernel,
            out_shape=outs,
            in_specs=[VMEM] * len(operands),
            out_specs=[VMEM] * len(outs),
            compiler_params=SMALL,
            cost_estimate=pl.CostEstimate(flops=half_flops, bytes_accessed=4 << 20, transcendentals=0),
            name=name,
        )(*operands)

    unit_rows = units // width

    def whole_tiles(rows):
        return -(-rows // 16) * 16

    rows_in = whole_tiles(bus_blocks + unit_rows)
    rows_out = whole_tiles(bus_blocks + unit_rows + own_groups)
    (sent,) = small(
        pack_kernel,
        "pack",
        [jax.ShapeDtypeStruct((devices, hour_rows * rows_in, width), jnp.bfloat16)],
        [
            base_injection.astype(jnp.float32).reshape(hour_rows, bus_count // width, width),
            soc_init.reshape(hour_rows, unit_rows, width),
        ],
    )
    came = lax.all_to_all(sent, "tm", split_axis=0, concat_axis=0, tiled=True)
    away, base, level = product(
        first_flow_kernel,
        "first_flow",
        [flow_shape, picked_shape, level_shape],
        [came.reshape(hours * rows_in, width)],
        [pltpu.VMEM((hours * rows_in, width), jnp.float32)],
    )
    picked = base
    price = None
    line_dual = jnp.zeros((own_groups, hours, lines), jnp.float32)
    for iteration in range(ITERS):
        arrived = lax.ppermute(away, "tm", sibling)
        (flows,) = product(own_flow_kernel, "own_flow", [flow_shape], [picked], [])
        pair = (flows + arrived).astype(jnp.bfloat16).reshape(chips, own_groups, hours, lines)
        parts = exchange(pair)
        if iteration == 0:
            (delta,) = small(storage_kernel, "storage", [block_shape], [level, unit_block, unit_lane])
        else:
            level, delta = small(
                level_kernel, "storage", [level_shape, block_shape], [price, level, unit_block, unit_lane, gain]
            )
        parts, level, delta = lax.optimization_barrier((parts, level, delta))
        shifted = jnp.sum(parts.astype(jnp.float32), axis=0) + line_dual
        clipped = jnp.clip(shifted, -own_limits, own_limits)
        line_dual = shifted - clipped
        dual = exchange(jnp.broadcast_to(line_dual.astype(jnp.bfloat16)[None], (chips, own_groups, hours, lines)))
        dual = dual.reshape(half_groups, hours, lines)
        other = lax.ppermute(dual, "tm", sibling)
        (before,) = product(own_price_kernel, "own_price", [block_shape], [dual], sums)
        if iteration < ITERS - 1:
            price, inject, picked, away = product(
                middle_kernel,
                "price_then_flow",
                [block_shape, block_shape, picked_shape, flow_shape],
                [other, before, base, delta],
                sums,
                2,
            )
        else:
            (out,) = product(
                last_kernel,
                "last_price",
                [jax.ShapeDtypeStruct((hours * rows_out, width), jnp.bfloat16)],
                [other, before, base, inject, delta, level, line_dual, unit_block, unit_lane, gain],
                [
                    pltpu.VMEM(block_shape.shape, jnp.float32),
                    pltpu.VMEM(level_shape.shape, jnp.float32),
                    pltpu.VMEM((hours * rows_out, width), jnp.float32),
                ]
                + sums,
            )

    back = lax.all_to_all(
        out.reshape(devices, hour_rows * rows_out, width), "tm", split_axis=0, concat_axis=0, tiled=True
    )
    inject, own_dual, level = small(
        unpack_kernel,
        "unpack",
        [
            jax.ShapeDtypeStruct((hour_rows, bus_count // width, width), jnp.float32),
            jax.ShapeDtypeStruct((hour_rows, line_count // width, width), jnp.float32),
            jax.ShapeDtypeStruct((hour_rows, unit_rows, width), jnp.float32),
        ],
        [back],
    )
    inject = inject.reshape(hour_rows, bus_count)
    own_dual = own_dual.reshape(hour_rows, line_count)
    level = level.reshape(hour_rows, units)
    return (inject, own_dual, level)


def solution(mesh):
    in_specs = (
        P(("scen", "tm"), None),
        P(None, "tm", None, None),
        P(None, "tm"),
        P(),
        P(),
        P(),
        P(("scen", "tm"), None),
    )
    out_specs = (P(("scen", "tm"), None), P(("scen", "tm"), None), P(("scen", "tm"), None))
    return jax.shard_map(shards, mesh=mesh, in_specs=in_specs, out_specs=out_specs, check_vma=False)
```

```python
import functools

import jax
import jax.numpy as jnp
from jax import lax
from jax.experimental import pallas as pl
from jax.experimental.pallas import tpu as pltpu
from jax.sharding import PartitionSpec as P

ITERS = 2


step_size = 0.5
penalty = 4.0
ramp_weight = 0.5

NT = (((1,), (1,)), ((), ()))
VMEM = pl.BlockSpec(memory_space=pltpu.VMEM)
HBM = pl.BlockSpec(memory_space=pl.ANY)
SMALL = pltpu.CompilerParams(vmem_limit_bytes=12 << 20)
STRAIGHT = 32


class Half:
    def __init__(self, sibling, blocks_hbm, tiles_hbm, tiles, sems, blocks, block_sem):
        me = lax.axis_index("tm")
        self.core = 1 - me % 2 if sibling else me % 2
        self.blocks, self.tiles_hbm, self.tiles, self.sems = blocks, tiles_hbm, tiles, sems
        self.chunks = sems.shape[0]
        self.own = tiles.shape[0] // self.chunks
        for chunk in range(self.chunks):
            self.fetch(chunk).start()
        self.block_copy = pltpu.make_async_copy(blocks_hbm, blocks, block_sem)
        self.block_copy.start()

    def first_group(self, chunk):
        return (2 * chunk + self.core) * self.own

    def fetch(self, chunk):
        there = pl.ds(self.first_group(chunk), self.own)
        here = pl.ds(chunk * self.own, self.own)
        return pltpu.make_async_copy(self.tiles_hbm.at[there], self.tiles.at[here], self.sems.at[chunk])

    def each_four(self, wait, four):
        depth = self.tiles.shape[1]
        if wait:
            self.block_copy.wait()
        per = max(1, STRAIGHT // self.own)

        def body(step, carry):
            for c in range(per):
                chunk = step * per + c
                if wait:
                    self.fetch(chunk).wait()
                for sub in range(0, self.own, 4):
                    first = (self.first_group(chunk) + sub) * depth
                    four(chunk * self.own + sub, lambda u, k: self.blocks[first + u * depth + k])
            return carry

        lax.fori_loop(0, self.chunks // per, body, 0)


def wide(parts):
    return jnp.concatenate([jnp.concatenate(row, axis=1) for row in parts], axis=0)


def flow_pass(picked, half, flows, wait):
    tiles = half.tiles
    depth, lines = tiles.shape[1], tiles.shape[2]
    hours = picked.shape[1]

    def four(base, block):
        rows = [[picked[block(u, k)] for k in range(depth)] for u in range(4)]
        zero = jnp.zeros_like(rows[0][0])
        totals = [None] * 4

        def add(u, part):
            totals[u] = part if totals[u] is None else totals[u] + part

        for first in (0, 2):
            for k in range(0, depth - 1, 2):
                left = wide([[rows[first][k], rows[first][k + 1]], [rows[first + 1][k], rows[first + 1][k + 1]]])
                g = base + first
                right = wide([[tiles[g, k], tiles[g, k + 1]], [tiles[g + 1, k], tiles[g + 1, k + 1]]])
                part = lax.dot_general(left, right, NT, preferred_element_type=jnp.float32)
                add(first, part[:hours, :lines])
                add(first + 1, part[hours:, lines:])
        if depth % 2:
            k = depth - 1
            left = wide([[rows[0][k], zero], [rows[1][k], zero], [zero, rows[2][k]], [zero, rows[3][k]]])
            right = wide([[tiles[base, k], tiles[base + 2, k]], [tiles[base + 1, k], tiles[base + 3, k]]])
            part = lax.dot_general(left, right, NT, preferred_element_type=jnp.float32)
            for u in range(4):
                at = (u % 2) * lines
                add(u, part[u * hours : (u + 1) * hours, at : at + lines])
        for u in range(4):
            flows[base + u] = totals[u].astype(flows.dtype)

    half.each_four(wait, four)


def price_pass(dual, half, sums, wait):
    tiles = half.tiles
    depth, width = tiles.shape[1], tiles.shape[3]
    hours = dual.shape[1]
    for ref in sums:
        ref[...] = jnp.zeros_like(ref)

    def four(base, block):
        rows = [dual[base + u] for u in range(4)]
        zero = jnp.zeros_like(rows[0])
        parts = []
        for first in (0, 2):
            left = wide([[rows[first], zero], [zero, rows[first + 1]]])
            for k in range(0, depth - 1, 2):
                g = base + first
                right = wide([[tiles[g, k], tiles[g, k + 1]], [tiles[g + 1, k], tiles[g + 1, k + 1]]])
                part = jnp.dot(left, right, preferred_element_type=jnp.float32)
                for u in range(2):
                    for j in range(2):
                        piece = part[u * hours : (u + 1) * hours, j * width : (j + 1) * width]
                        parts.append((first + u, k + j, piece))
        if depth % 2:
            k = depth - 1
            left = wide([[rows[0], zero], [zero, rows[1]], [rows[2], zero], [zero, rows[3]]])
            right = wide([[tiles[base, k], tiles[base + 2, k]], [tiles[base + 1, k], tiles[base + 3, k]]])
            part = jnp.dot(left, right, preferred_element_type=jnp.float32)
            for u in range(4):
                at = (u // 2) * width
                parts.append((u, k, part[u * hours : (u + 1) * hours, at : at + width]))
        for u, k, part in parts:
            at = block(u, k)
            sums[k][at] = sums[k][at] + part

    half.each_four(wait, four)


def earlier(values):
    return jnp.concatenate([values[-1:], values[:-1]], axis=0)


def later(values):
    return jnp.concatenate([values[1:], values[:1]], axis=0)


def total(sums, block):
    price = sums[0][block]
    for ref in sums[1:]:
        price = price + ref[block]
    return price


def update_pass(sums, before, inject, base, delta, price_out, out):
    for block in range(sums[0].shape[0]):
        price = before[block] + total(sums, block)
        price_out[block] = price
        now = inject(block)
        new = now - step_size * (
            (now - base(block))
            + penalty * price
            + ramp_weight * (2.0 * now - earlier(now) - later(now))
        )
        out(block, new - delta[block])


def one_hot(unit_lane, cols, width):
    lane = jnp.broadcast_to(unit_lane[:, cols], (width, cols.size))
    return (lane == lax.broadcasted_iota(jnp.int32, (width, cols.size), 0)).astype(jnp.bfloat16)


def high_low(values, axis):
    high = values.astype(jnp.bfloat16)
    low = (values - high.astype(jnp.float32)).astype(jnp.bfloat16)
    return jnp.concatenate([high, low], axis=axis)


def level_pass(price, level, unit_block, unit_lane, gain, out, mine):
    count, hours, width = price.shape
    span = 2 * width
    prices = high_low(jnp.concatenate([price[b] for b in range(count)], axis=0), 1)

    def body(c, carry):
        cols = pl.ds(pl.multiple_of(c * span, span), span)
        hot = one_hot(unit_lane, cols, width)
        picked = jnp.dot(prices, jnp.concatenate([hot, hot], axis=0), preferred_element_type=jnp.float32)
        block = jnp.broadcast_to(unit_block[:, cols], (hours, span))
        found = jnp.zeros((hours, span), jnp.float32)
        for b in range(count):
            found = jnp.where(block == b, picked[b * hours : (b + 1) * hours], found)
        now = level[:, cols]
        new = 0.5 * (now + earlier(now)) - gain[:, cols] * found
        if mine:
            new = jnp.where((block >= 0) & (block < count), new, 0.0)
        out[:, cols] = new
        return carry

    lax.fori_loop(0, level.shape[1] // span, body, 0)


def pack_kernel(base, soc_hbm, out, flat, soc, sem):
    devices, rows, width = out.shape
    hour_rows = soc.shape[0]
    rows = rows // hour_rows
    count = base.shape[1] // (devices * width)
    units = soc.shape[1] // width
    copy = pltpu.make_async_copy(soc_hbm, soc, sem)
    copy.start()
    flat[...] = jnp.zeros_like(flat)
    for r in range(hour_rows):
        for d in range(devices):
            at = (d * hour_rows + r) * rows
            for b in range(count):
                first = (d * count + b) * width
                flat[at + b : at + b + 1, :] = base[r : r + 1, first : first + width].astype(jnp.float32)
    copy.wait()
    for r in range(hour_rows):
        levels = jnp.concatenate([soc[r : r + 1, c * width : (c + 1) * width] for c in range(units)], axis=0)
        for d in range(devices):
            at = (d * hour_rows + r) * rows
            flat[at + count : at + count + units, :] = levels
    out[...] = flat[...].reshape(out.shape).astype(out.dtype)


def first_flow_kernel(blocks_hbm, tiles_hbm, came, flows, picked, level, *scratch):
    stream, (flat,) = (blocks_hbm, tiles_hbm, *scratch[:4]), scratch[4:]
    half = Half(True, *stream)
    count, hours, width = picked.shape
    flat[...] = came[...].astype(jnp.float32)
    rows = flat.shape[0] // hours
    for b in range(count):
        picked[b] = flat[pl.ds(b, hours, stride=rows), :].astype(picked.dtype)
    for c in range(level.shape[1] // width):
        level[:, c * width : (c + 1) * width] = flat[pl.ds(count + c, hours, stride=rows), :]
    flow_pass(picked, half, flows, True)


def own_flow_kernel(blocks_hbm, tiles_hbm, picked, flows, *scratch):
    stream = (blocks_hbm, tiles_hbm, *scratch)
    half = Half(False, *stream)
    flow_pass(picked, half, flows, True)


def own_price_kernel(blocks_hbm, tiles_hbm, dual, price, *scratch):
    stream, sums = (blocks_hbm, tiles_hbm, *scratch[:4]), scratch[4:]
    half = Half(False, *stream)
    price_pass(dual, half, sums, True)
    for b in range(price.shape[0]):
        price[b] = total(sums, b)


def middle_kernel(
    blocks_hbm, tiles_hbm, dual, before, base, delta, price, inject_out, picked, flows, *scratch
):
    stream, sums = (blocks_hbm, tiles_hbm, *scratch[:4]), scratch[4:]
    half = Half(True, *stream)
    price_pass(dual, half, sums, True)

    def start(b):
        return base[b].astype(jnp.float32)

    def write(b, new):
        inject_out[b] = new
        picked[b] = new.astype(picked.dtype)

    update_pass(sums, before, start, start, delta, price, write)
    flow_pass(picked, half, flows, False)


def last_kernel(
    blocks_hbm, tiles_hbm, dual, before, base, inject, delta, level, line_dual, unit_block, unit_lane, gain,
    out, *scratch
):
    stream, (price, level_out, flat, *sums) = (blocks_hbm, tiles_hbm, *scratch[:4]), scratch[4:]
    half = Half(True, *stream)
    count, hours, width = price.shape
    rows = flat.shape[0] // hours
    flat[...] = jnp.zeros_like(flat)
    units = level.shape[1] // width
    for g in range(line_dual.shape[0]):
        flat[pl.ds(count + units + g, hours, stride=rows), :] = line_dual[g]
    price_pass(dual, half, sums, True)

    def start(b):
        return base[b].astype(jnp.float32)

    def write(b, new):
        flat[pl.ds(b, hours, stride=rows), :] = new

    update_pass(sums, before, lambda b: inject[b], start, delta, price, write)
    level_pass(price, level, unit_block, unit_lane, gain, level_out, True)
    for c in range(units):
        flat[pl.ds(count + c, hours, stride=rows), :] = level_out[:, c * width : (c + 1) * width]
    out[...] = flat[...].astype(out.dtype)


def unpack_kernel(back, inject, line_dual, level):
    devices = back.shape[0]
    hour_rows, units = level.shape[0], level.shape[1]
    count, own = inject.shape[1] // devices, line_dual.shape[1] // devices
    rows = back.shape[1] // hour_rows
    for r in range(hour_rows):
        sum_levels = None
        for d in range(devices):
            came = back[d, r * rows : (r + 1) * rows].astype(jnp.float32)
            inject[r, d * count : (d + 1) * count] = came[:count]
            line_dual[r, d * own : (d + 1) * own] = came[count + units : count + units + own]
            part = came[count : count + units]
            sum_levels = part if sum_levels is None else sum_levels + part
        level[r] = sum_levels


def storage_pass(level, unit_block, unit_lane, delta):
    count, hours, width = delta.shape
    span = 2 * width
    delta[...] = jnp.zeros_like(delta)

    def body(c, carry):
        cols = pl.ds(pl.multiple_of(c * span, span), span)
        now = level[:, cols]
        charge = high_low(step_size * (now - earlier(now)), 0).astype(jnp.float32)
        hot = one_hot(unit_lane, cols, width)
        block = jnp.broadcast_to(unit_block[:, cols], charge.shape)
        held = jnp.concatenate([jnp.where(block == b, charge, 0.0) for b in range(count)], axis=0)
        part = lax.dot_general(held.astype(jnp.bfloat16), hot, NT, preferred_element_type=jnp.float32)
        for b in range(count):
            high, low = part[2 * b * hours : (2 * b + 1) * hours], part[(2 * b + 1) * hours : (2 * b + 2) * hours]
            delta[b] = delta[b] + (high + low)
        return carry

    lax.fori_loop(0, level.shape[1] // span, body, 0)


def storage_kernel(level, unit_block, unit_lane, delta):
    storage_pass(level, unit_block, unit_lane, delta)


def level_kernel(price, level, unit_block, unit_lane, gain, level_out, delta):
    level_pass(price, level, unit_block, unit_lane, gain, level_out, False)
    storage_pass(level_out, unit_block, unit_lane, delta)


def shards(base_injection, ptdf_tiles, tile_block, limits, stor_bus, stor_gain, soc_init):
    hour_rows = base_injection.shape[0]
    bus_count = base_injection.shape[1]
    line_count = limits.shape[0]
    groups, depth, lines, width = ptdf_tiles.shape
    units = stor_bus.shape[0]
    devices = lax.axis_size("tm")
    me = lax.axis_index("tm")
    buses = bus_count // devices
    bus_blocks = buses // width
    hours = hour_rows * devices
    own_groups = groups // devices
    blocks = tile_block.reshape(groups * depth)
    unit_block = (stor_bus // width - me * bus_blocks).reshape(1, units)
    unit_lane = (stor_bus % width).reshape(1, units)
    gain = stor_gain.reshape(1, units)
    own_limits = lax.dynamic_slice_in_dim(limits.reshape(groups, 1, lines), me * own_groups, own_groups, 0)

    chips = devices // 2
    half_groups = chips * own_groups
    sibling = [(d, d + 1 - 2 * (d % 2)) for d in range(devices)]

    same_core = [[2 * chip + c for chip in range(chips)] for c in range(2)]

    def exchange(value):
        return lax.all_to_all(value, "tm", split_axis=0, concat_axis=0, axis_index_groups=same_core, tiled=True)

    half_bytes = ptdf_tiles.size
    half_flops = hours * ptdf_tiles.size
    stream = [pltpu.VMEM((half_groups, *ptdf_tiles.shape[1:]), ptdf_tiles.dtype), pltpu.SemaphoreType.DMA((chips,))]
    stream += [pltpu.SMEM(blocks.shape, blocks.dtype), pltpu.SemaphoreType.DMA]
    sums = [pltpu.VMEM((bus_blocks, hours, width), jnp.float32)] * depth
    large = pltpu.CompilerParams(vmem_limit_bytes=48 << 20)
    picked_shape = jax.ShapeDtypeStruct((bus_blocks, hours, width), jnp.bfloat16)
    block_shape = jax.ShapeDtypeStruct((bus_blocks, hours, width), jnp.float32)
    level_shape = jax.ShapeDtypeStruct((hours, units), jnp.float32)
    flow_shape = jax.ShapeDtypeStruct((half_groups, hours, lines), jnp.float32)

    def product(kernel, name, outs, operands, scratch, passes=1):
        return pl.pallas_call(
            kernel,
            out_shape=outs,
            in_specs=[HBM] * 2 + [VMEM] * len(operands),
            out_specs=[VMEM] * len(outs),
            scratch_shapes=stream + scratch,
            compiler_params=large,
            cost_estimate=pl.CostEstimate(
                flops=passes * half_flops, bytes_accessed=passes * half_bytes, transcendentals=0
            ),
            name=name,
        )(blocks, ptdf_tiles, *operands)

    def small(kernel, name, outs, operands, scratch=(), last=VMEM):
        return pl.pallas_call(
            kernel,
            out_shape=outs,
            in_specs=[VMEM] * (len(operands) - 1) + [last],
            out_specs=[VMEM] * len(outs),
            scratch_shapes=scratch,
            compiler_params=SMALL,
            cost_estimate=pl.CostEstimate(flops=half_flops, bytes_accessed=4 << 20, transcendentals=0),
            name=name,
        )(*operands)

    unit_rows = units // width

    def whole_tiles(rows):
        return -(-rows // 16) * 16

    rows_in = whole_tiles(bus_blocks + unit_rows)
    rows_out = whole_tiles(bus_blocks + unit_rows + own_groups)
    (sent,) = small(
        pack_kernel,
        "pack",
        [jax.ShapeDtypeStruct((devices, hour_rows * rows_in, width), jnp.bfloat16)],
        [base_injection, soc_init],
        [
            pltpu.VMEM((devices * hour_rows * rows_in, width), jnp.float32),
            pltpu.VMEM(soc_init.shape, soc_init.dtype),
            pltpu.SemaphoreType.DMA,
        ],
        HBM,
    )
    came = lax.all_to_all(sent, "tm", split_axis=0, concat_axis=0, tiled=True)
    away, base, level = product(
        first_flow_kernel,
        "first_flow",
        [flow_shape, picked_shape, level_shape],
        [came.reshape(hours * rows_in, width)],
        [pltpu.VMEM((hours * rows_in, width), jnp.float32)],
    )
    picked = base
    price = None
    line_dual = jnp.zeros((own_groups, hours, lines), jnp.float32)
    for iteration in range(ITERS):
        arrived = lax.ppermute(away, "tm", sibling)
        (flows,) = product(own_flow_kernel, "own_flow", [flow_shape], [picked], [])
        pair = (flows + arrived).astype(jnp.bfloat16).reshape(chips, own_groups, hours, lines)
        parts = exchange(pair)
        if iteration == 0:
            (delta,) = small(storage_kernel, "storage", [block_shape], [level, unit_block, unit_lane])
        else:
            level, delta = small(
                level_kernel, "storage", [level_shape, block_shape], [price, level, unit_block, unit_lane, gain]
            )
        parts, level, delta = lax.optimization_barrier((parts, level, delta))
        shifted = jnp.sum(parts.astype(jnp.float32), axis=0) + line_dual
        clipped = jnp.clip(shifted, -own_limits, own_limits)
        line_dual = shifted - clipped
        dual = exchange(jnp.broadcast_to(line_dual.astype(jnp.bfloat16)[None], (chips, own_groups, hours, lines)))
        dual = dual.reshape(half_groups, hours, lines)
        other = lax.ppermute(dual, "tm", sibling)
        (before,) = product(own_price_kernel, "own_price", [block_shape], [dual], sums)
        if iteration < ITERS - 1:
            price, inject, picked, away = product(
                middle_kernel,
                "price_then_flow",
                [block_shape, block_shape, picked_shape, flow_shape],
                [other, before, base, delta],
                sums,
                2,
            )
        else:
            (out,) = product(
                last_kernel,
                "last_price",
                [jax.ShapeDtypeStruct((hours * rows_out, width), jnp.bfloat16)],
                [other, before, base, inject, delta, level, line_dual, unit_block, unit_lane, gain],
                [
                    pltpu.VMEM(block_shape.shape, jnp.float32),
                    pltpu.VMEM(level_shape.shape, jnp.float32),
                    pltpu.VMEM((hours * rows_out, width), jnp.float32),
                ]
                + sums,
            )

    back = lax.all_to_all(
        out.reshape(devices, hour_rows * rows_out, width), "tm", split_axis=0, concat_axis=0, tiled=True
    )
    inject, own_dual, level = small(
        unpack_kernel,
        "unpack",
        [
            jax.ShapeDtypeStruct((hour_rows, bus_count // width, width), jnp.float32),
            jax.ShapeDtypeStruct((hour_rows, line_count // width, width), jnp.float32),
            jax.ShapeDtypeStruct((hour_rows, unit_rows, width), jnp.float32),
        ],
        [back],
    )
    inject = inject.reshape(hour_rows, bus_count)
    own_dual = own_dual.reshape(hour_rows, line_count)
    level = level.reshape(hour_rows, units)
    return (inject, own_dual, level)


def solution(mesh):
    in_specs = (
        P(("scen", "tm"), None),
        P(None, "tm", None, None),
        P(None, "tm"),
        P(),
        P(),
        P(),
        P(("scen", "tm"), None),
    )
    out_specs = (P(("scen", "tm"), None), P(("scen", "tm"), None), P(("scen", "tm"), None))
    return jax.shard_map(shards, mesh=mesh, in_specs=in_specs, out_specs=out_specs, check_vma=False)
```

```python
import functools

import jax
import jax.numpy as jnp
from jax import lax
from jax.experimental import pallas as pl
from jax.experimental.pallas import tpu as pltpu
from jax.sharding import PartitionSpec as P

ITERS = 2


step_size = 0.5
penalty = 4.0
ramp_weight = 0.5

NT = (((1,), (1,)), ((), ()))
VMEM = pl.BlockSpec(memory_space=pltpu.VMEM)
HBM = pl.BlockSpec(memory_space=pl.ANY)
SMALL = pltpu.CompilerParams(vmem_limit_bytes=12 << 20)
STRAIGHT = 32


class Half:
    def __init__(self, sibling, blocks_hbm, tiles_hbm, tiles, sems, blocks, block_sem):
        me = lax.axis_index("tm")
        self.core = 1 - me % 2 if sibling else me % 2
        self.blocks, self.tiles_hbm, self.tiles, self.sems = blocks, tiles_hbm, tiles, sems
        self.chunks = sems.shape[0]
        self.own = tiles.shape[0] // self.chunks
        for chunk in range(self.chunks):
            self.fetch(chunk).start()
        self.block_copy = pltpu.make_async_copy(blocks_hbm, blocks, block_sem)
        self.block_copy.start()

    def first_group(self, chunk):
        return (2 * chunk + self.core) * self.own

    def fetch(self, chunk):
        there = pl.ds(self.first_group(chunk), self.own)
        here = pl.ds(chunk * self.own, self.own)
        return pltpu.make_async_copy(self.tiles_hbm.at[there], self.tiles.at[here], self.sems.at[chunk])

    def each_four(self, wait, four):
        depth = self.tiles.shape[1]
        if wait:
            self.block_copy.wait()
        per = max(1, STRAIGHT // self.own)

        def body(step, carry):
            for c in range(per):
                chunk = step * per + c
                if wait:
                    self.fetch(chunk).wait()
                for sub in range(0, self.own, 4):
                    first = (self.first_group(chunk) + sub) * depth
                    four(chunk * self.own + sub, lambda u, k: self.blocks[first + u * depth + k])
            return carry

        lax.fori_loop(0, self.chunks // per, body, 0)


def wide(parts):
    return jnp.concatenate([jnp.concatenate(row, axis=1) for row in parts], axis=0)


def flow_pass(picked, half, flows, wait):
    tiles = half.tiles
    depth = tiles.shape[1]
    hours = picked.shape[1]
    even = depth - depth % 2

    def side(parts):
        return jnp.concatenate(parts, axis=1)

    def four(base, block):
        rows = [[picked[block(u, k)] for k in range(depth)] for u in range(4)]
        zero = jnp.zeros_like(rows[0][0])
        for first in (0, 2):
            g = base + first
            totals = [
                lax.dot_general(
                    side(rows[first + u][:even]),
                    side([tiles[g + u, k] for k in range(even)]),
                    NT,
                    preferred_element_type=jnp.float32,
                )
                for u in range(2)
            ]
            if depth % 2:
                left = wide([[rows[first][even], zero], [zero, rows[first + 1][even]]])
                right = side([tiles[g, even], tiles[g + 1, even]])
                part = lax.dot_general(left, right, NT, preferred_element_type=jnp.float32)
                totals = [totals[u] + part[u * hours : (u + 1) * hours] for u in range(2)]
            for u in range(2):
                flows[g + u] = totals[u].astype(flows.dtype)

    half.each_four(wait, four)


def price_pass(dual, half, sums, wait):
    tiles = half.tiles
    depth, width = tiles.shape[1], tiles.shape[3]
    hours = dual.shape[1]
    for ref in sums:
        ref[...] = jnp.zeros_like(ref)

    def four(base, block):
        rows = [dual[base + u] for u in range(4)]
        zero = jnp.zeros_like(rows[0])
        parts = []
        for first in (0, 2):
            left = wide([[rows[first], zero], [zero, rows[first + 1]]])
            for k in range(0, depth - 1, 2):
                g = base + first
                right = wide([[tiles[g, k], tiles[g, k + 1]], [tiles[g + 1, k], tiles[g + 1, k + 1]]])
                part = jnp.dot(left, right, preferred_element_type=jnp.float32)
                for u in range(2):
                    for j in range(2):
                        piece = part[u * hours : (u + 1) * hours, j * width : (j + 1) * width]
                        parts.append((first + u, k + j, piece))
        if depth % 2:
            k = depth - 1
            left = wide([[rows[0], zero], [zero, rows[1]], [rows[2], zero], [zero, rows[3]]])
            right = wide([[tiles[base, k], tiles[base + 2, k]], [tiles[base + 1, k], tiles[base + 3, k]]])
            part = jnp.dot(left, right, preferred_element_type=jnp.float32)
            for u in range(4):
                at = (u // 2) * width
                parts.append((u, k, part[u * hours : (u + 1) * hours, at : at + width]))
        for u, k, part in parts:
            at = block(u, k)
            sums[k][at] = sums[k][at] + part

    half.each_four(wait, four)


def earlier(values):
    return jnp.concatenate([values[-1:], values[:-1]], axis=0)


def later(values):
    return jnp.concatenate([values[1:], values[:1]], axis=0)


def total(sums, block):
    price = sums[0][block]
    for ref in sums[1:]:
        price = price + ref[block]
    return price


def update_pass(sums, before, inject, base, delta, price_out, out):
    for block in range(sums[0].shape[0]):
        price = before[block] + total(sums, block)
        price_out[block] = price
        now = inject(block)
        new = now - step_size * (
            (now - base(block))
            + penalty * price
            + ramp_weight * (2.0 * now - earlier(now) - later(now))
        )
        out(block, new - delta[block])


def one_hot(unit_lane, cols, width):
    lane = jnp.broadcast_to(unit_lane[:, cols], (width, cols.size))
    return (lane == lax.broadcasted_iota(jnp.int32, (width, cols.size), 0)).astype(jnp.bfloat16)


def high_low(values, axis):
    high = values.astype(jnp.bfloat16)
    low = (values - high.astype(jnp.float32)).astype(jnp.bfloat16)
    return jnp.concatenate([high, low], axis=axis)


def level_pass(price, level, unit_block, unit_lane, gain, out, mine):
    count, hours, width = price.shape
    span = 2 * width
    prices = high_low(jnp.concatenate([price[b] for b in range(count)], axis=0), 1)

    def body(c, carry):
        cols = pl.ds(pl.multiple_of(c * span, span), span)
        hot = one_hot(unit_lane, cols, width)
        picked = jnp.dot(prices, jnp.concatenate([hot, hot], axis=0), preferred_element_type=jnp.float32)
        block = jnp.broadcast_to(unit_block[:, cols], (hours, span))
        found = jnp.zeros((hours, span), jnp.float32)
        for b in range(count):
            found = jnp.where(block == b, picked[b * hours : (b + 1) * hours], found)
        now = level[:, cols]
        new = 0.5 * (now + earlier(now)) - gain[:, cols] * found
        if mine:
            new = jnp.where((block >= 0) & (block < count), new, 0.0)
        out[:, cols] = new
        return carry

    lax.fori_loop(0, level.shape[1] // span, body, 0)


def pack_kernel(base, soc_hbm, out, flat, soc, sem):
    devices, rows, width = out.shape
    hour_rows = soc.shape[0]
    rows = rows // hour_rows
    count = base.shape[1] // (devices * width)
    units = soc.shape[1] // width
    copy = pltpu.make_async_copy(soc_hbm, soc, sem)
    copy.start()
    flat[...] = jnp.zeros_like(flat)
    for r in range(hour_rows):
        for d in range(devices):
            at = (d * hour_rows + r) * rows
            for b in range(count):
                first = (d * count + b) * width
                flat[at + b : at + b + 1, :] = base[r : r + 1, first : first + width].astype(jnp.float32)
    copy.wait()
    for r in range(hour_rows):
        levels = jnp.concatenate([soc[r : r + 1, c * width : (c + 1) * width] for c in range(units)], axis=0)
        for d in range(devices):
            at = (d * hour_rows + r) * rows
            flat[at + count : at + count + units, :] = levels
    out[...] = flat[...].reshape(out.shape).astype(out.dtype)


def first_flow_kernel(blocks_hbm, tiles_hbm, came, flows, picked, level, *scratch):
    stream, (flat,) = (blocks_hbm, tiles_hbm, *scratch[:4]), scratch[4:]
    half = Half(True, *stream)
    count, hours, width = picked.shape
    flat[...] = came[...].astype(jnp.float32)
    rows = flat.shape[0] // hours
    for b in range(count):
        picked[b] = flat[pl.ds(b, hours, stride=rows), :].astype(picked.dtype)
    for c in range(level.shape[1] // width):
        level[:, c * width : (c + 1) * width] = flat[pl.ds(count + c, hours, stride=rows), :]
    flow_pass(picked, half, flows, True)


def own_flow_kernel(blocks_hbm, tiles_hbm, picked, flows, *scratch):
    stream = (blocks_hbm, tiles_hbm, *scratch)
    half = Half(False, *stream)
    flow_pass(picked, half, flows, True)


def own_price_kernel(blocks_hbm, tiles_hbm, dual, price, *scratch):
    stream, sums = (blocks_hbm, tiles_hbm, *scratch[:4]), scratch[4:]
    half = Half(False, *stream)
    price_pass(dual, half, sums, True)
    for b in range(price.shape[0]):
        price[b] = total(sums, b)


def middle_kernel(
    blocks_hbm, tiles_hbm, dual, before, base, delta, price, inject_out, picked, flows, *scratch
):
    stream, sums = (blocks_hbm, tiles_hbm, *scratch[:4]), scratch[4:]
    half = Half(True, *stream)
    price_pass(dual, half, sums, True)

    def start(b):
        return base[b].astype(jnp.float32)

    def write(b, new):
        inject_out[b] = new
        picked[b] = new.astype(picked.dtype)

    update_pass(sums, before, start, start, delta, price, write)
    flow_pass(picked, half, flows, False)


def last_kernel(
    blocks_hbm, tiles_hbm, dual, before, base, inject, delta, level, line_dual, unit_block, unit_lane, gain,
    out, *scratch
):
    stream, (price, level_out, flat, *sums) = (blocks_hbm, tiles_hbm, *scratch[:4]), scratch[4:]
    half = Half(True, *stream)
    count, hours, width = price.shape
    rows = flat.shape[0] // hours
    flat[...] = jnp.zeros_like(flat)
    units = level.shape[1] // width
    for g in range(line_dual.shape[0]):
        flat[pl.ds(count + units + g, hours, stride=rows), :] = line_dual[g]
    price_pass(dual, half, sums, True)

    def start(b):
        return base[b].astype(jnp.float32)

    def write(b, new):
        flat[pl.ds(b, hours, stride=rows), :] = new

    update_pass(sums, before, lambda b: inject[b], start, delta, price, write)
    level_pass(price, level, unit_block, unit_lane, gain, level_out, True)
    for c in range(units):
        flat[pl.ds(count + c, hours, stride=rows), :] = level_out[:, c * width : (c + 1) * width]
    out[...] = flat[...].astype(out.dtype)


def unpack_kernel(back, inject, line_dual, level):
    devices = back.shape[0]
    hour_rows, units = level.shape[0], level.shape[1]
    count, own = inject.shape[1] // devices, line_dual.shape[1] // devices
    rows = back.shape[1] // hour_rows
    for r in range(hour_rows):
        sum_levels = None
        for d in range(devices):
            came = back[d, r * rows : (r + 1) * rows].astype(jnp.float32)
            inject[r, d * count : (d + 1) * count] = came[:count]
            line_dual[r, d * own : (d + 1) * own] = came[count + units : count + units + own]
            part = came[count : count + units]
            sum_levels = part if sum_levels is None else sum_levels + part
        level[r] = sum_levels


def storage_pass(level, unit_block, unit_lane, delta):
    count, hours, width = delta.shape
    span = 2 * width
    delta[...] = jnp.zeros_like(delta)

    def body(c, carry):
        cols = pl.ds(pl.multiple_of(c * span, span), span)
        now = level[:, cols]
        charge = high_low(step_size * (now - earlier(now)), 0).astype(jnp.float32)
        hot = one_hot(unit_lane, cols, width)
        block = jnp.broadcast_to(unit_block[:, cols], charge.shape)
        held = jnp.concatenate([jnp.where(block == b, charge, 0.0) for b in range(count)], axis=0)
        part = lax.dot_general(held.astype(jnp.bfloat16), hot, NT, preferred_element_type=jnp.float32)
        for b in range(count):
            high, low = part[2 * b * hours : (2 * b + 1) * hours], part[(2 * b + 1) * hours : (2 * b + 2) * hours]
            delta[b] = delta[b] + (high + low)
        return carry

    lax.fori_loop(0, level.shape[1] // span, body, 0)


def storage_kernel(level, unit_block, unit_lane, delta):
    storage_pass(level, unit_block, unit_lane, delta)


def level_kernel(price, level, unit_block, unit_lane, gain, level_out, delta):
    level_pass(price, level, unit_block, unit_lane, gain, level_out, False)
    storage_pass(level_out, unit_block, unit_lane, delta)


def shards(base_injection, ptdf_tiles, tile_block, limits, stor_bus, stor_gain, soc_init):
    hour_rows = base_injection.shape[0]
    bus_count = base_injection.shape[1]
    line_count = limits.shape[0]
    groups, depth, lines, width = ptdf_tiles.shape
    units = stor_bus.shape[0]
    devices = lax.axis_size("tm")
    me = lax.axis_index("tm")
    buses = bus_count // devices
    bus_blocks = buses // width
    hours = hour_rows * devices
    own_groups = groups // devices
    blocks = tile_block.reshape(groups * depth)
    unit_block = (stor_bus // width - me * bus_blocks).reshape(1, units)
    unit_lane = (stor_bus % width).reshape(1, units)
    gain = stor_gain.reshape(1, units)
    own_limits = lax.dynamic_slice_in_dim(limits.reshape(groups, 1, lines), me * own_groups, own_groups, 0)

    chips = devices // 2
    half_groups = chips * own_groups
    sibling = [(d, d + 1 - 2 * (d % 2)) for d in range(devices)]

    same_core = [[2 * chip + c for chip in range(chips)] for c in range(2)]

    def exchange(value):
        return lax.all_to_all(value, "tm", split_axis=0, concat_axis=0, axis_index_groups=same_core, tiled=True)

    half_bytes = ptdf_tiles.size
    half_flops = hours * ptdf_tiles.size
    stream = [pltpu.VMEM((half_groups, *ptdf_tiles.shape[1:]), ptdf_tiles.dtype), pltpu.SemaphoreType.DMA((chips,))]
    stream += [pltpu.SMEM(blocks.shape, blocks.dtype), pltpu.SemaphoreType.DMA]
    sums = [pltpu.VMEM((bus_blocks, hours, width), jnp.float32)] * depth
    large = pltpu.CompilerParams(vmem_limit_bytes=48 << 20)
    picked_shape = jax.ShapeDtypeStruct((bus_blocks, hours, width), jnp.bfloat16)
    block_shape = jax.ShapeDtypeStruct((bus_blocks, hours, width), jnp.float32)
    level_shape = jax.ShapeDtypeStruct((hours, units), jnp.float32)
    flow_shape = jax.ShapeDtypeStruct((half_groups, hours, lines), jnp.float32)

    def product(kernel, name, outs, operands, scratch, passes=1):
        return pl.pallas_call(
            kernel,
            out_shape=outs,
            in_specs=[HBM] * 2 + [VMEM] * len(operands),
            out_specs=[VMEM] * len(outs),
            scratch_shapes=stream + scratch,
            compiler_params=large,
            cost_estimate=pl.CostEstimate(
                flops=passes * half_flops, bytes_accessed=passes * half_bytes, transcendentals=0
            ),
            name=name,
        )(blocks, ptdf_tiles, *operands)

    def small(kernel, name, outs, operands, scratch=(), last=VMEM):
        return pl.pallas_call(
            kernel,
            out_shape=outs,
            in_specs=[VMEM] * (len(operands) - 1) + [last],
            out_specs=[VMEM] * len(outs),
            scratch_shapes=scratch,
            compiler_params=SMALL,
            cost_estimate=pl.CostEstimate(flops=half_flops, bytes_accessed=4 << 20, transcendentals=0),
            name=name,
        )(*operands)

    unit_rows = units // width

    def whole_tiles(rows):
        return -(-rows // 16) * 16

    rows_in = whole_tiles(bus_blocks + unit_rows)
    rows_out = whole_tiles(bus_blocks + unit_rows + own_groups)
    (sent,) = small(
        pack_kernel,
        "pack",
        [jax.ShapeDtypeStruct((devices, hour_rows * rows_in, width), jnp.bfloat16)],
        [base_injection, soc_init],
        [
            pltpu.VMEM((devices * hour_rows * rows_in, width), jnp.float32),
            pltpu.VMEM(soc_init.shape, soc_init.dtype),
            pltpu.SemaphoreType.DMA,
        ],
        HBM,
    )
    came = lax.all_to_all(sent, "tm", split_axis=0, concat_axis=0, tiled=True)
    away, base, level = product(
        first_flow_kernel,
        "first_flow",
        [flow_shape, picked_shape, level_shape],
        [came.reshape(hours * rows_in, width)],
        [pltpu.VMEM((hours * rows_in, width), jnp.float32)],
    )
    picked = base
    price = None
    line_dual = jnp.zeros((own_groups, hours, lines), jnp.float32)
    for iteration in range(ITERS):
        arrived = lax.ppermute(away, "tm", sibling)
        (flows,) = product(own_flow_kernel, "own_flow", [flow_shape], [picked], [])
        pair = (flows + arrived).astype(jnp.bfloat16).reshape(chips, own_groups, hours, lines)
        parts = exchange(pair)
        if iteration == 0:
            (delta,) = small(storage_kernel, "storage", [block_shape], [level, unit_block, unit_lane])
        else:
            level, delta = small(
                level_kernel, "storage", [level_shape, block_shape], [price, level, unit_block, unit_lane, gain]
            )
        parts, level, delta = lax.optimization_barrier((parts, level, delta))
        shifted = jnp.sum(parts.astype(jnp.float32), axis=0) + line_dual
        clipped = jnp.clip(shifted, -own_limits, own_limits)
        line_dual = shifted - clipped
        dual = lax.all_gather(
            line_dual.astype(jnp.bfloat16), "tm", axis=0, axis_index_groups=same_core, tiled=True
        )
        other = lax.ppermute(dual, "tm", sibling)
        (before,) = product(own_price_kernel, "own_price", [block_shape], [dual], sums)
        if iteration < ITERS - 1:
            price, inject, picked, away = product(
                middle_kernel,
                "price_then_flow",
                [block_shape, block_shape, picked_shape, flow_shape],
                [other, before, base, delta],
                sums,
                2,
            )
        else:
            (out,) = product(
                last_kernel,
                "last_price",
                [jax.ShapeDtypeStruct((hours * rows_out, width), jnp.bfloat16)],
                [other, before, base, inject, delta, level, line_dual, unit_block, unit_lane, gain],
                [
                    pltpu.VMEM(block_shape.shape, jnp.float32),
                    pltpu.VMEM(level_shape.shape, jnp.float32),
                    pltpu.VMEM((hours * rows_out, width), jnp.float32),
                ]
                + sums,
            )

    back = lax.all_to_all(
        out.reshape(devices, hour_rows * rows_out, width), "tm", split_axis=0, concat_axis=0, tiled=True
    )
    inject, own_dual, level = small(
        unpack_kernel,
        "unpack",
        [
            jax.ShapeDtypeStruct((hour_rows, bus_count // width, width), jnp.float32),
            jax.ShapeDtypeStruct((hour_rows, line_count // width, width), jnp.float32),
            jax.ShapeDtypeStruct((hour_rows, unit_rows, width), jnp.float32),
        ],
        [back],
    )
    inject = inject.reshape(hour_rows, bus_count)
    own_dual = own_dual.reshape(hour_rows, line_count)
    level = level.reshape(hour_rows, units)
    return (inject, own_dual, level)


def solution(mesh):
    in_specs = (
        P(("scen", "tm"), None),
        P(None, "tm", None, None),
        P(None, "tm"),
        P(),
        P(),
        P(),
        P(("scen", "tm"), None),
    )
    out_specs = (P(("scen", "tm"), None), P(("scen", "tm"), None), P(("scen", "tm"), None))
    return jax.shard_map(shards, mesh=mesh, in_specs=in_specs, out_specs=out_specs, check_vma=False)
```

```python
import functools

import jax
import jax.numpy as jnp
from jax import lax
from jax.experimental import pallas as pl
from jax.experimental.pallas import tpu as pltpu
from jax.sharding import PartitionSpec as P

ITERS = 2


step_size = 0.5
penalty = 4.0
ramp_weight = 0.5

NT = (((1,), (1,)), ((), ()))
VMEM = pl.BlockSpec(memory_space=pltpu.VMEM)
HBM = pl.BlockSpec(memory_space=pl.ANY)
SMALL = pltpu.CompilerParams(vmem_limit_bytes=12 << 20)
STRAIGHT = 16


class Half:
    def __init__(self, sibling, hbm, tiles, blocks, block_sem, sems=None, head=None):
        me = lax.axis_index("tm")
        self.core = 1 - me % 2 if sibling else me % 2
        self.tiles, self.head, self.blocks, self.sems = tiles, head, blocks, sems
        self.blocks_hbm, self.tiles_hbm = hbm
        self.chunks = lax.axis_size("tm") // 2
        self.own = self.tiles_hbm.shape[0] // (2 * self.chunks)
        self.ahead = 0 if head is None else head.shape[0] // self.own
        self.depth, self.lines, self.width = self.tiles_hbm.shape[1:]
        if sems is not None:
            for chunk in range(self.ahead, self.chunks):
                self.fetch(chunk).start()
        self.block_copy = pltpu.make_async_copy(self.blocks_hbm, blocks, block_sem)
        self.block_copy.start()

    def first_group(self, chunk):
        return (2 * chunk + self.core) * self.own

    def fetch(self, chunk):
        there = pl.ds(self.first_group(chunk), self.own)
        here = pl.ds((chunk - self.ahead) * self.own, self.own)
        return pltpu.make_async_copy(self.tiles_hbm.at[there], self.tiles.at[here], self.sems.at[chunk])

    def each_four(self, wait, four):
        per = max(1, STRAIGHT // self.own)

        def one(chunk, ref, at):
            for sub in range(0, self.own, 4):
                first = (self.first_group(chunk) + sub) * self.depth
                four(
                    lambda u, k: ref[at + sub + u, k],
                    chunk * self.own + sub,
                    lambda u, k: self.blocks[first + u * self.depth + k],
                )

        def body(step, carry):
            for c in range(per):
                chunk = self.ahead + step * per + c
                if wait and self.sems is not None:
                    self.fetch(chunk).wait()
                one(chunk, self.tiles, (chunk - self.ahead) * self.own)
            return carry

        if wait:
            self.block_copy.wait()
        for chunk in range(self.ahead):
            one(chunk, self.head, chunk * self.own)
        lax.fori_loop(0, (self.chunks - self.ahead) // per, body, 0)


class Ahead:
    def __init__(self, half, head, sem):
        self.copies = []
        for chunk in range(head.shape[0] // half.own):
            there = pl.ds((2 * chunk + 1 - half.core) * half.own, half.own)
            here = pl.ds(chunk * half.own, half.own)
            self.copies.append(pltpu.make_async_copy(half.tiles_hbm.at[there], head.at[here], sem.at[chunk]))
            self.copies[-1].start()

    def wait(self):
        for copy in self.copies:
            copy.wait()


def wide(parts):
    return jnp.concatenate([jnp.concatenate(row, axis=1) for row in parts], axis=0)


def flow_pass(picked, half, flows, wait):
    depth = half.depth
    hours = picked.shape[1]
    even = depth - depth % 2

    def side(parts):
        return jnp.concatenate(parts, axis=1)

    def four(tile, g, block):
        rows = [[picked[block(u, k)] for k in range(depth)] for u in range(4)]
        zero = jnp.zeros_like(rows[0][0])
        for first in (0, 2):
            totals = [
                lax.dot_general(
                    side(rows[first + u][:even]),
                    side([tile(first + u, k) for k in range(even)]),
                    NT,
                    preferred_element_type=jnp.float32,
                )
                for u in range(2)
            ]
            if depth % 2:
                left = wide([[rows[first][even], zero], [zero, rows[first + 1][even]]])
                right = side([tile(first, even), tile(first + 1, even)])
                part = lax.dot_general(left, right, NT, preferred_element_type=jnp.float32)
                totals = [totals[u] + part[u * hours : (u + 1) * hours] for u in range(2)]
            for u in range(2):
                flows[g + first + u] = totals[u].astype(flows.dtype)

    half.each_four(wait, four)


def price_pass(dual, half, sums, wait):
    depth, width = half.depth, half.width
    hours = dual.shape[1]
    for ref in sums:
        ref[...] = jnp.zeros_like(ref)

    def four(tile, g, block):
        rows = [dual[g + u] for u in range(4)]
        zero = jnp.zeros_like(rows[0])
        parts = []
        for first in (0, 2):
            left = wide([[rows[first], zero], [zero, rows[first + 1]]])
            for k in range(0, depth - 1, 2):
                right = wide([[tile(first + u, k), tile(first + u, k + 1)] for u in range(2)])
                part = jnp.dot(left, right, preferred_element_type=jnp.float32)
                for u in range(2):
                    for j in range(2):
                        piece = part[u * hours : (u + 1) * hours, j * width : (j + 1) * width]
                        parts.append((first + u, k + j, piece))
        if depth % 2:
            k = depth - 1
            left = wide([[rows[0], zero], [zero, rows[1]], [rows[2], zero], [zero, rows[3]]])
            right = wide([[tile(0, k), tile(2, k)], [tile(1, k), tile(3, k)]])
            part = jnp.dot(left, right, preferred_element_type=jnp.float32)
            for u in range(4):
                at = (u // 2) * width
                parts.append((u, k, part[u * hours : (u + 1) * hours, at : at + width]))
        for u, k, part in parts:
            at = block(u, k)
            sums[k][at] = sums[k][at] + part

    half.each_four(wait, four)


def earlier(values):
    return jnp.concatenate([values[-1:], values[:-1]], axis=0)


def later(values):
    return jnp.concatenate([values[1:], values[:1]], axis=0)


def total(sums, block):
    price = sums[0][block]
    for ref in sums[1:]:
        price = price + ref[block]
    return price


def update_pass(sums, before, inject, base, delta, price_out, out):
    for block in range(sums[0].shape[0]):
        price = before[block] + total(sums, block)
        price_out[block] = price
        now = inject(block)
        new = now - step_size * (
            (now - base(block))
            + penalty * price
            + ramp_weight * (2.0 * now - earlier(now) - later(now))
        )
        out(block, new - delta[block])


def one_hot(unit_lane, cols, width):
    lane = jnp.broadcast_to(unit_lane[:, cols], (width, cols.size))
    return (lane == lax.broadcasted_iota(jnp.int32, (width, cols.size), 0)).astype(jnp.bfloat16)


def high_low(values, axis):
    high = values.astype(jnp.bfloat16)
    low = (values - high.astype(jnp.float32)).astype(jnp.bfloat16)
    return jnp.concatenate([high, low], axis=axis)


def level_pass(price, level, unit_block, unit_lane, gain, out, mine):
    count, hours, width = price.shape
    span = 2 * width
    prices = high_low(jnp.concatenate([price[b] for b in range(count)], axis=0), 1)

    def body(c, carry):
        cols = pl.ds(pl.multiple_of(c * span, span), span)
        hot = one_hot(unit_lane, cols, width)
        picked = jnp.dot(prices, jnp.concatenate([hot, hot], axis=0), preferred_element_type=jnp.float32)
        block = jnp.broadcast_to(unit_block[:, cols], (hours, span))
        found = jnp.zeros((hours, span), jnp.float32)
        for b in range(count):
            found = jnp.where(block == b, picked[b * hours : (b + 1) * hours], found)
        now = level[:, cols]
        new = 0.5 * (now + earlier(now)) - gain[:, cols] * found
        if mine:
            new = jnp.where((block >= 0) & (block < count), new, 0.0)
        out[:, cols] = new
        return carry

    lax.fori_loop(0, level.shape[1] // span, body, 0)


def pack_kernel(base, soc_hbm, out, flat, soc, sem):
    devices, rows, width = out.shape
    hour_rows = soc.shape[0]
    rows = rows // hour_rows
    count = base.shape[1] // (devices * width)
    units = soc.shape[1] // width
    copy = pltpu.make_async_copy(soc_hbm, soc, sem)
    copy.start()
    flat[...] = jnp.zeros_like(flat)
    for r in range(hour_rows):
        for d in range(devices):
            at = (d * hour_rows + r) * rows
            for b in range(count):
                first = (d * count + b) * width
                flat[at + b : at + b + 1, :] = base[r : r + 1, first : first + width].astype(jnp.float32)
    copy.wait()
    for r in range(hour_rows):
        levels = jnp.concatenate([soc[r : r + 1, c * width : (c + 1) * width] for c in range(units)], axis=0)
        for d in range(devices):
            at = (d * hour_rows + r) * rows
            flat[at + count : at + count + units, :] = levels
    out[...] = flat[...].reshape(out.shape).astype(out.dtype)


def first_flow_kernel(
    blocks_hbm, tiles_hbm, came, flows, picked, level, head, blocks, block_sem, tiles, sems, ahead_sem, flat
):
    half = Half(True, (blocks_hbm, tiles_hbm), tiles, blocks, block_sem, sems)
    ahead = Ahead(half, head, ahead_sem)
    count, hours, width = picked.shape
    flat[...] = came[...].astype(jnp.float32)
    rows = flat.shape[0] // hours
    for b in range(count):
        picked[b] = flat[pl.ds(b, hours, stride=rows), :].astype(picked.dtype)
    for c in range(level.shape[1] // width):
        level[:, c * width : (c + 1) * width] = flat[pl.ds(count + c, hours, stride=rows), :]
    flow_pass(picked, half, flows, True)
    ahead.wait()


def own_flow_kernel(blocks_hbm, tiles_hbm, picked, head, flows, blocks, block_sem, tiles, sems):
    flow_pass(picked, Half(False, (blocks_hbm, tiles_hbm), tiles, blocks, block_sem, sems, head), flows, True)


def held_flow_kernel(blocks_hbm, tiles_hbm, picked, tiles, flows, blocks, block_sem):
    flow_pass(picked, Half(False, (blocks_hbm, tiles_hbm), tiles, blocks, block_sem), flows, True)


def own_price_kernel(blocks_hbm, tiles_hbm, dual, price, head, tiles, blocks, block_sem, sems, ahead_sem, *sums):
    half = Half(False, (blocks_hbm, tiles_hbm), tiles, blocks, block_sem, sems)
    ahead = Ahead(half, head, ahead_sem)
    price_pass(dual, half, sums, True)
    for b in range(price.shape[0]):
        price[b] = total(sums, b)
    ahead.wait()


def middle_kernel(
    blocks_hbm, tiles_hbm, dual, before, base, delta, head, price, inject_out, picked, flows,
    blocks, block_sem, tiles, sems, *sums
):
    half = Half(True, (blocks_hbm, tiles_hbm), tiles, blocks, block_sem, sems, head)
    price_pass(dual, half, sums, True)

    def start(b):
        return base[b].astype(jnp.float32)

    def write(b, new):
        inject_out[b] = new
        picked[b] = new.astype(picked.dtype)

    update_pass(sums, before, start, start, delta, price, write)
    flow_pass(picked, half, flows, False)


def last_kernel(
    blocks_hbm, tiles_hbm, dual, before, base, inject, delta, level, line_dual, unit_block, unit_lane, gain, head,
    out, blocks, block_sem, tiles, sems, price, level_out, flat, *sums
):
    half = Half(True, (blocks_hbm, tiles_hbm), tiles, blocks, block_sem, sems, head)
    count, hours, width = price.shape
    rows = flat.shape[0] // hours
    flat[...] = jnp.zeros_like(flat)
    units = level.shape[1] // width
    for g in range(line_dual.shape[0]):
        flat[pl.ds(count + units + g, hours, stride=rows), :] = line_dual[g]
    price_pass(dual, half, sums, True)

    def start(b):
        return base[b].astype(jnp.float32)

    def write(b, new):
        flat[pl.ds(b, hours, stride=rows), :] = new

    update_pass(sums, before, lambda b: inject[b], start, delta, price, write)
    level_pass(price, level, unit_block, unit_lane, gain, level_out, True)
    for c in range(units):
        flat[pl.ds(count + c, hours, stride=rows), :] = level_out[:, c * width : (c + 1) * width]
    out[...] = flat[...].astype(out.dtype)


def unpack_kernel(back, inject, line_dual, level):
    devices = back.shape[0]
    hour_rows, units = level.shape[0], level.shape[1]
    count, own = inject.shape[1] // devices, line_dual.shape[1] // devices
    rows = back.shape[1] // hour_rows
    for r in range(hour_rows):
        sum_levels = None
        for d in range(devices):
            came = back[d, r * rows : (r + 1) * rows].astype(jnp.float32)
            inject[r, d * count : (d + 1) * count] = came[:count]
            line_dual[r, d * own : (d + 1) * own] = came[count + units : count + units + own]
            part = came[count : count + units]
            sum_levels = part if sum_levels is None else sum_levels + part
        level[r] = sum_levels


def storage_pass(level, unit_block, unit_lane, delta):
    count, hours, width = delta.shape
    span = 2 * width
    delta[...] = jnp.zeros_like(delta)

    def body(c, carry):
        cols = pl.ds(pl.multiple_of(c * span, span), span)
        now = level[:, cols]
        charge = high_low(step_size * (now - earlier(now)), 0).astype(jnp.float32)
        hot = one_hot(unit_lane, cols, width)
        block = jnp.broadcast_to(unit_block[:, cols], charge.shape)
        held = jnp.concatenate([jnp.where(block == b, charge, 0.0) for b in range(count)], axis=0)
        part = lax.dot_general(held.astype(jnp.bfloat16), hot, NT, preferred_element_type=jnp.float32)
        for b in range(count):
            high, low = part[2 * b * hours : (2 * b + 1) * hours], part[(2 * b + 1) * hours : (2 * b + 2) * hours]
            delta[b] = delta[b] + (high + low)
        return carry

    lax.fori_loop(0, level.shape[1] // span, body, 0)


def storage_kernel(level, unit_block, unit_lane, delta):
    storage_pass(level, unit_block, unit_lane, delta)


def level_kernel(price, level, unit_block, unit_lane, gain, level_out, delta):
    level_pass(price, level, unit_block, unit_lane, gain, level_out, False)
    storage_pass(level_out, unit_block, unit_lane, delta)


def shards(base_injection, ptdf_tiles, tile_block, limits, stor_bus, stor_gain, soc_init):
    hour_rows = base_injection.shape[0]
    bus_count = base_injection.shape[1]
    line_count = limits.shape[0]
    groups, depth, lines, width = ptdf_tiles.shape
    units = stor_bus.shape[0]
    devices = lax.axis_size("tm")
    me = lax.axis_index("tm")
    buses = bus_count // devices
    bus_blocks = buses // width
    hours = hour_rows * devices
    own_groups = groups // devices
    blocks = tile_block.reshape(groups * depth)
    unit_block = (stor_bus // width - me * bus_blocks).reshape(1, units)
    unit_lane = (stor_bus % width).reshape(1, units)
    gain = stor_gain.reshape(1, units)
    own_limits = lax.dynamic_slice_in_dim(limits.reshape(groups, 1, lines), me * own_groups, own_groups, 0)

    chips = devices // 2
    half_groups = chips * own_groups
    sibling = [(d, d + 1 - 2 * (d % 2)) for d in range(devices)]

    same_core = [[2 * chip + c for chip in range(chips)] for c in range(2)]

    def exchange(value):
        return lax.all_to_all(value, "tm", split_axis=0, concat_axis=0, axis_index_groups=same_core, tiled=True)

    half_bytes = ptdf_tiles.size
    half_flops = hours * ptdf_tiles.size
    ahead = max(1, chips // 4)

    def tile_shape(chunks):
        return jax.ShapeDtypeStruct((chunks * own_groups, *ptdf_tiles.shape[1:]), ptdf_tiles.dtype)

    def scratch(shape):
        return pltpu.VMEM(shape.shape, shape.dtype)

    picked_shape = jax.ShapeDtypeStruct((bus_blocks, hours, width), jnp.bfloat16)
    block_shape = jax.ShapeDtypeStruct((bus_blocks, hours, width), jnp.float32)
    level_shape = jax.ShapeDtypeStruct((hours, units), jnp.float32)
    flow_shape = jax.ShapeDtypeStruct((half_groups, hours, lines), jnp.float32)
    head_shape, half_shape, rest_shape = tile_shape(ahead), tile_shape(chips), tile_shape(chips - ahead)
    sems, ahead_sems = pltpu.SemaphoreType.DMA((chips,)), pltpu.SemaphoreType.DMA((ahead,))
    sums = [scratch(block_shape)] * depth

    def product(kernel, name, outs, operands, temporary, passes=1, limit=48):
        return pl.pallas_call(
            kernel,
            out_shape=outs,
            in_specs=[HBM] * 2 + [VMEM] * len(operands),
            out_specs=[VMEM] * len(outs),
            scratch_shapes=[pltpu.SMEM(blocks.shape, blocks.dtype), pltpu.SemaphoreType.DMA, *temporary],
            compiler_params=pltpu.CompilerParams(vmem_limit_bytes=limit << 20),
            cost_estimate=pl.CostEstimate(
                flops=passes * half_flops, bytes_accessed=passes * half_bytes, transcendentals=0
            ),
            name=name,
        )(blocks, ptdf_tiles, *operands)

    def small(kernel, name, outs, operands, scratch=(), last=VMEM):
        return pl.pallas_call(
            kernel,
            out_shape=outs,
            in_specs=[VMEM] * (len(operands) - 1) + [last],
            out_specs=[VMEM] * len(outs),
            scratch_shapes=scratch,
            compiler_params=SMALL,
            cost_estimate=pl.CostEstimate(flops=half_flops, bytes_accessed=4 << 20, transcendentals=0),
            name=name,
        )(*operands)

    unit_rows = units // width

    def whole_tiles(rows):
        return -(-rows // 16) * 16

    rows_in = whole_tiles(bus_blocks + unit_rows)
    rows_out = whole_tiles(bus_blocks + unit_rows + own_groups)
    (sent,) = small(
        pack_kernel,
        "pack",
        [jax.ShapeDtypeStruct((devices, hour_rows * rows_in, width), jnp.bfloat16)],
        [base_injection, soc_init],
        [
            pltpu.VMEM((devices * hour_rows * rows_in, width), jnp.float32),
            pltpu.VMEM(soc_init.shape, soc_init.dtype),
            pltpu.SemaphoreType.DMA,
        ],
        HBM,
    )
    came = lax.all_to_all(sent, "tm", split_axis=0, concat_axis=0, tiled=True)
    away, base, level, head = product(
        first_flow_kernel,
        "first_flow",
        [flow_shape, picked_shape, level_shape, head_shape],
        [came.reshape(hours * rows_in, width)],
        [scratch(half_shape), sems, ahead_sems, pltpu.VMEM((hours * rows_in, width), jnp.float32)],
    )
    picked = base
    price = None
    line_dual = jnp.zeros((own_groups, hours, lines), jnp.float32)
    for iteration in range(ITERS):
        arrived = lax.ppermute(away, "tm", sibling)
        if iteration == 0:
            (flows,) = product(
                own_flow_kernel, "own_flow", [flow_shape], [picked, head], [scratch(rest_shape), sems]
            )
        else:
            (flows,) = product(held_flow_kernel, "held_flow", [flow_shape], [picked, held], [], limit=40)
        pair = (flows + arrived).astype(jnp.bfloat16).reshape(chips, own_groups, hours, lines)
        parts = exchange(pair)
        if iteration == 0:
            (delta,) = small(storage_kernel, "storage", [block_shape], [level, unit_block, unit_lane])
        else:
            level, delta = small(
                level_kernel, "storage", [level_shape, block_shape], [price, level, unit_block, unit_lane, gain]
            )
        parts, level, delta = lax.optimization_barrier((parts, level, delta))
        shifted = jnp.sum(parts.astype(jnp.float32), axis=0) + line_dual
        clipped = jnp.clip(shifted, -own_limits, own_limits)
        line_dual = shifted - clipped
        dual = exchange(jnp.broadcast_to(line_dual.astype(jnp.bfloat16)[None], (chips, own_groups, hours, lines)))
        dual = dual.reshape(half_groups, hours, lines)
        other = lax.ppermute(dual, "tm", sibling)
        if iteration < ITERS - 1:
            before, head, held = product(
                own_price_kernel,
                "own_price",
                [block_shape, head_shape, half_shape],
                [dual],
                [sems, ahead_sems] + sums,
                limit=36,
            )
            price, inject, picked, away = product(
                middle_kernel,
                "price_then_flow",
                [block_shape, block_shape, picked_shape, flow_shape],
                [other, before, base, delta, head],
                [scratch(rest_shape), sems] + sums,
                2,
                limit=36,
            )
        else:
            before, head = product(
                lambda *refs: own_price_kernel(*refs[:5], refs[7], *refs[5:7], *refs[8:]),
                "own_price",
                [block_shape, head_shape],
                [dual],
                [scratch(half_shape), sems, ahead_sems] + sums,
            )
            (out,) = product(
                last_kernel,
                "last_price",
                [jax.ShapeDtypeStruct((hours * rows_out, width), jnp.bfloat16)],
                [other, before, base, inject, delta, level, line_dual, unit_block, unit_lane, gain, head],
                [
                    scratch(rest_shape),
                    sems,
                    scratch(block_shape),
                    scratch(level_shape),
                    pltpu.VMEM((hours * rows_out, width), jnp.float32),
                ]
                + sums,
            )

    back = lax.all_to_all(
        out.reshape(devices, hour_rows * rows_out, width), "tm", split_axis=0, concat_axis=0, tiled=True
    )
    inject, own_dual, level = small(
        unpack_kernel,
        "unpack",
        [
            jax.ShapeDtypeStruct((hour_rows, bus_count // width, width), jnp.float32),
            jax.ShapeDtypeStruct((hour_rows, line_count // width, width), jnp.float32),
            jax.ShapeDtypeStruct((hour_rows, unit_rows, width), jnp.float32),
        ],
        [back],
    )
    inject = inject.reshape(hour_rows, bus_count)
    own_dual = own_dual.reshape(hour_rows, line_count)
    level = level.reshape(hour_rows, units)
    return (inject, own_dual, level)


def solution(mesh):
    in_specs = (
        P(("scen", "tm"), None),
        P(None, "tm", None, None),
        P(None, "tm"),
        P(),
        P(),
        P(),
        P(("scen", "tm"), None),
    )
    out_specs = (P(("scen", "tm"), None), P(("scen", "tm"), None), P(("scen", "tm"), None))
    return jax.shard_map(shards, mesh=mesh, in_specs=in_specs, out_specs=out_specs, check_vma=False)
```

```python
import functools

import jax
import jax.numpy as jnp
from jax import lax
from jax.experimental import pallas as pl
from jax.experimental.pallas import tpu as pltpu
from jax.sharding import PartitionSpec as P

ITERS = 2


step_size = 0.5
penalty = 4.0
ramp_weight = 0.5

NT = (((1,), (1,)), ((), ()))
VMEM = pl.BlockSpec(memory_space=pltpu.VMEM)
HBM = pl.BlockSpec(memory_space=pl.ANY)
SMALL = pltpu.CompilerParams(vmem_limit_bytes=12 << 20)
STRAIGHT = 64


class Half:
    def __init__(self, sibling, hbm, tiles, blocks, block_sem, sems=None, head=None):
        me = lax.axis_index("tm")
        self.core = 1 - me % 2 if sibling else me % 2
        self.tiles, self.head, self.blocks, self.sems = tiles, head, blocks, sems
        self.blocks_hbm, self.tiles_hbm = hbm
        self.chunks = lax.axis_size("tm") // 2
        self.own = self.tiles_hbm.shape[0] // (2 * self.chunks)
        self.ahead = 0 if head is None else head.shape[0] // self.own
        self.depth, self.lines, self.width = self.tiles_hbm.shape[1:]
        if sems is not None:
            for chunk in range(self.ahead, self.chunks):
                self.fetch(chunk).start()
        self.block_copy = pltpu.make_async_copy(self.blocks_hbm, blocks, block_sem)
        self.block_copy.start()

    def first_group(self, chunk):
        return (2 * chunk + self.core) * self.own

    def fetch(self, chunk):
        there = pl.ds(self.first_group(chunk), self.own)
        here = pl.ds((chunk - self.ahead) * self.own, self.own)
        return pltpu.make_async_copy(self.tiles_hbm.at[there], self.tiles.at[here], self.sems.at[chunk])

    def each_four(self, wait, four):
        rest = self.chunks - self.ahead
        per = max(n for n in range(1, rest + 1) if rest % n == 0 and n * self.own <= max(STRAIGHT, self.own))

        def one(chunk, ref, at):
            for sub in range(0, self.own, 4):
                first = (self.first_group(chunk) + sub) * self.depth
                four(
                    lambda u, k: ref[at + sub + u, k],
                    chunk * self.own + sub,
                    lambda u, k: self.blocks[first + u * self.depth + k],
                )

        def body(step, carry):
            for c in range(per):
                chunk = self.ahead + step * per + c
                if wait and self.sems is not None:
                    self.fetch(chunk).wait()
                one(chunk, self.tiles, (chunk - self.ahead) * self.own)
            return carry

        if wait:
            self.block_copy.wait()
        for chunk in range(self.ahead):
            one(chunk, self.head, chunk * self.own)
        if per == rest:
            body(0, 0)
        else:
            lax.fori_loop(0, rest // per, body, 0)


class Ahead:
    def __init__(self, half, head, sem):
        self.copies = []
        for chunk in range(head.shape[0] // half.own):
            there = pl.ds((2 * chunk + 1 - half.core) * half.own, half.own)
            here = pl.ds(chunk * half.own, half.own)
            self.copies.append(pltpu.make_async_copy(half.tiles_hbm.at[there], head.at[here], sem.at[chunk]))
            self.copies[-1].start()

    def wait(self):
        for copy in self.copies:
            copy.wait()


def wide(parts):
    return jnp.concatenate([jnp.concatenate(row, axis=1) for row in parts], axis=0)


def flow_pass(picked, half, flows, wait):
    depth = half.depth
    hours = picked.shape[1]
    even = depth - depth % 2

    def side(parts):
        return jnp.concatenate(parts, axis=1)

    def four(tile, g, block):
        rows = [[picked[block(u, k)] for k in range(depth)] for u in range(4)]
        zero = jnp.zeros_like(rows[0][0])
        for first in (0, 2):
            totals = [
                lax.dot_general(
                    side(rows[first + u][:even]),
                    side([tile(first + u, k) for k in range(even)]),
                    NT,
                    preferred_element_type=jnp.float32,
                )
                for u in range(2)
            ]
            if depth % 2:
                left = wide([[rows[first][even], zero], [zero, rows[first + 1][even]]])
                right = side([tile(first, even), tile(first + 1, even)])
                part = lax.dot_general(left, right, NT, preferred_element_type=jnp.float32)
                totals = [totals[u] + part[u * hours : (u + 1) * hours] for u in range(2)]
            for u in range(2):
                flows[g + first + u] = totals[u].astype(flows.dtype)

    half.each_four(wait, four)


def price_pass(dual, half, sums, wait):
    depth, width = half.depth, half.width
    hours = dual.shape[1]
    for ref in sums:
        ref[...] = jnp.zeros_like(ref)

    def four(tile, g, block):
        rows = [dual[g + u] for u in range(4)]
        zero = jnp.zeros_like(rows[0])
        parts = []
        for first in (0, 2):
            left = wide([[rows[first], zero], [zero, rows[first + 1]]])
            for k in range(0, depth - 1, 2):
                right = wide([[tile(first + u, k), tile(first + u, k + 1)] for u in range(2)])
                part = jnp.dot(left, right, preferred_element_type=jnp.float32)
                for u in range(2):
                    for j in range(2):
                        piece = part[u * hours : (u + 1) * hours, j * width : (j + 1) * width]
                        parts.append((first + u, k + j, piece))
        if depth % 2:
            k = depth - 1
            left = wide([[rows[0], zero], [zero, rows[1]], [rows[2], zero], [zero, rows[3]]])
            right = wide([[tile(0, k), tile(2, k)], [tile(1, k), tile(3, k)]])
            part = jnp.dot(left, right, preferred_element_type=jnp.float32)
            for u in range(4):
                at = (u // 2) * width
                parts.append((u, k, part[u * hours : (u + 1) * hours, at : at + width]))
        for u, k, part in parts:
            at = block(u, k)
            sums[k][at] = sums[k][at] + part

    half.each_four(wait, four)


def earlier(values):
    return jnp.concatenate([values[-1:], values[:-1]], axis=0)


def later(values):
    return jnp.concatenate([values[1:], values[:1]], axis=0)


def total(sums, block):
    price = sums[0][block]
    for ref in sums[1:]:
        price = price + ref[block]
    return price


def update_pass(sums, before, inject, base, delta, price_out, out):
    for block in range(sums[0].shape[0]):
        price = before[block] + total(sums, block)
        price_out[block] = price
        now = inject(block)
        new = now - step_size * (
            (now - base(block))
            + penalty * price
            + ramp_weight * (2.0 * now - earlier(now) - later(now))
        )
        out(block, new - delta[block])


def one_hot(unit_lane, cols, width):
    lane = jnp.broadcast_to(unit_lane[:, cols], (width, cols.size))
    return (lane == lax.broadcasted_iota(jnp.int32, (width, cols.size), 0)).astype(jnp.bfloat16)


def high_low(values, axis):
    high = values.astype(jnp.bfloat16)
    low = (values - high.astype(jnp.float32)).astype(jnp.bfloat16)
    return jnp.concatenate([high, low], axis=axis)


def level_pass(price, level, unit_block, unit_lane, gain, out, mine):
    count, hours, width = price.shape
    span = 2 * width
    prices = high_low(jnp.concatenate([price[b] for b in range(count)], axis=0), 1)

    def body(c, carry):
        cols = pl.ds(pl.multiple_of(c * span, span), span)
        hot = one_hot(unit_lane, cols, width)
        picked = jnp.dot(prices, jnp.concatenate([hot, hot], axis=0), preferred_element_type=jnp.float32)
        block = jnp.broadcast_to(unit_block[:, cols], (hours, span))
        found = jnp.zeros((hours, span), jnp.float32)
        for b in range(count):
            found = jnp.where(block == b, picked[b * hours : (b + 1) * hours], found)
        now = level[:, cols]
        new = 0.5 * (now + earlier(now)) - gain[:, cols] * found
        if mine:
            new = jnp.where((block >= 0) & (block < count), new, 0.0)
        out[:, cols] = new
        return carry

    lax.fori_loop(0, level.shape[1] // span, body, 0)


def storage_pass(level, unit_block, unit_lane, delta):
    count, hours, width = delta.shape
    span = 2 * width
    delta[...] = jnp.zeros_like(delta)

    def body(c, carry):
        cols = pl.ds(pl.multiple_of(c * span, span), span)
        now = level[:, cols]
        charge = step_size * (now - earlier(now))
        hot = one_hot(unit_lane, cols, width)
        block = jnp.broadcast_to(unit_block[:, cols], (hours, span))
        held = jnp.concatenate([jnp.where(block == b, charge, 0.0) for b in range(count)], axis=0)
        part = lax.dot_general(held.astype(jnp.bfloat16), hot, NT, preferred_element_type=jnp.float32)
        for b in range(count):
            delta[b] = delta[b] + part[b * hours : (b + 1) * hours]
        return carry

    lax.fori_loop(0, level.shape[1] // span, body, 0)


def pack_kernel(base, soc_hbm, out, flat, soc, sem):
    devices, rows, width = out.shape
    hour_rows = soc.shape[0]
    rows = rows // hour_rows
    count = base.shape[1] // (devices * width)
    units = soc.shape[1] // width
    copy = pltpu.make_async_copy(soc_hbm, soc, sem)
    copy.start()
    flat[...] = jnp.zeros_like(flat)
    for r in range(hour_rows):
        for d in range(devices):
            at = (d * hour_rows + r) * rows
            for b in range(count):
                first = (d * count + b) * width
                flat[at + b : at + b + 1, :] = base[r : r + 1, first : first + width].astype(jnp.float32)
    copy.wait()
    for r in range(hour_rows):
        levels = jnp.concatenate([soc[r : r + 1, c * width : (c + 1) * width] for c in range(units)], axis=0)
        for d in range(devices):
            at = (d * hour_rows + r) * rows
            flat[at + count : at + count + units, :] = levels
    out[...] = flat[...].reshape(out.shape).astype(out.dtype)


def first_flow_kernel(
    blocks_hbm, tiles_hbm, came, flows, picked, level, head, blocks, block_sem, tiles, sems, ahead_sem, flat
):
    half = Half(True, (blocks_hbm, tiles_hbm), tiles, blocks, block_sem, sems)
    ahead = Ahead(half, head, ahead_sem)
    count, hours, width = picked.shape
    flat[...] = came[...].astype(jnp.float32)
    rows = flat.shape[0] // hours
    for b in range(count):
        picked[b] = flat[pl.ds(b, hours, stride=rows), :].astype(picked.dtype)
    for c in range(level.shape[1] // width):
        level[:, c * width : (c + 1) * width] = flat[pl.ds(count + c, hours, stride=rows), :]
    flow_pass(picked, half, flows, True)
    ahead.wait()


def own_flow_kernel(blocks_hbm, tiles_hbm, picked, head, flows, blocks, block_sem, tiles, sems):
    flow_pass(picked, Half(False, (blocks_hbm, tiles_hbm), tiles, blocks, block_sem, sems, head), flows, True)


def held_flow_kernel(blocks_hbm, tiles_hbm, picked, tiles, flows, blocks, block_sem):
    flow_pass(picked, Half(False, (blocks_hbm, tiles_hbm), tiles, blocks, block_sem), flows, True)


def own_price(half, ahead, dual, price, sums):
    price_pass(dual, half, sums, True)
    for b in range(price.shape[0]):
        price[b] = total(sums, b)
    ahead.wait()


def own_price_kernel(
    blocks_hbm, tiles_hbm, dual, level, unit_block, unit_lane, before, delta, head, tiles,
    blocks, block_sem, sems, ahead_sem, *sums
):
    half = Half(False, (blocks_hbm, tiles_hbm), tiles, blocks, block_sem, sems)
    ahead = Ahead(half, head, ahead_sem)
    storage_pass(level, unit_block, unit_lane, delta)
    own_price(half, ahead, dual, before, sums)


def own_price_level_kernel(
    blocks_hbm, tiles_hbm, dual, price, level, unit_block, unit_lane, gain, before, level_out, delta, head,
    blocks, block_sem, tiles, sems, ahead_sem, *sums
):
    half = Half(False, (blocks_hbm, tiles_hbm), tiles, blocks, block_sem, sems)
    ahead = Ahead(half, head, ahead_sem)
    level_pass(price, level, unit_block, unit_lane, gain, level_out, False)
    storage_pass(level_out, unit_block, unit_lane, delta)
    own_price(half, ahead, dual, before, sums)


def middle_kernel(
    blocks_hbm, tiles_hbm, dual, before, base, delta, head, price, inject_out, picked, flows,
    blocks, block_sem, tiles, sems, *sums
):
    half = Half(True, (blocks_hbm, tiles_hbm), tiles, blocks, block_sem, sems, head)
    price_pass(dual, half, sums, True)

    def start(b):
        return base[b].astype(jnp.float32)

    def write(b, new):
        inject_out[b] = new
        picked[b] = new.astype(picked.dtype)

    update_pass(sums, before, start, start, delta, price, write)
    flow_pass(picked, half, flows, False)


def last_kernel(
    blocks_hbm, tiles_hbm, dual, before, base, inject, delta, level, line_dual, unit_block, unit_lane, gain, head,
    out, blocks, block_sem, tiles, sems, price, level_out, flat, *sums
):
    half = Half(True, (blocks_hbm, tiles_hbm), tiles, blocks, block_sem, sems, head)
    count, hours, width = price.shape
    rows = flat.shape[0] // hours
    flat[...] = jnp.zeros_like(flat)
    units = level.shape[1] // width
    for g in range(line_dual.shape[0]):
        flat[pl.ds(count + units + g, hours, stride=rows), :] = line_dual[g]
    price_pass(dual, half, sums, True)

    def start(b):
        return base[b].astype(jnp.float32)

    def write(b, new):
        flat[pl.ds(b, hours, stride=rows), :] = new

    update_pass(sums, before, lambda b: inject[b], start, delta, price, write)
    level_pass(price, level, unit_block, unit_lane, gain, level_out, True)
    for c in range(units):
        flat[pl.ds(count + c, hours, stride=rows), :] = level_out[:, c * width : (c + 1) * width]
    out[...] = flat[...].astype(out.dtype)


def unpack_kernel(back, inject, line_dual, level):
    devices = back.shape[0]
    hour_rows, units = level.shape[0], level.shape[1]
    count, own = inject.shape[1] // devices, line_dual.shape[1] // devices
    rows = back.shape[1] // hour_rows
    for r in range(hour_rows):
        sum_levels = None
        for d in range(devices):
            came = back[d, r * rows : (r + 1) * rows].astype(jnp.float32)
            inject[r, d * count : (d + 1) * count] = came[:count]
            line_dual[r, d * own : (d + 1) * own] = came[count + units : count + units + own]
            part = came[count : count + units]
            sum_levels = part if sum_levels is None else sum_levels + part
        level[r] = sum_levels


def shards(base_injection, ptdf_tiles, tile_block, limits, stor_bus, stor_gain, soc_init):
    hour_rows = base_injection.shape[0]
    bus_count = base_injection.shape[1]
    line_count = limits.shape[0]
    groups, depth, lines, width = ptdf_tiles.shape
    units = stor_bus.shape[0]
    devices = lax.axis_size("tm")
    me = lax.axis_index("tm")
    buses = bus_count // devices
    bus_blocks = buses // width
    hours = hour_rows * devices
    own_groups = groups // devices
    blocks = tile_block.reshape(groups * depth)
    unit_block = (stor_bus // width - me * bus_blocks).reshape(1, units)
    unit_lane = (stor_bus % width).reshape(1, units)
    gain = stor_gain.reshape(1, units)
    own_limits = lax.dynamic_slice_in_dim(limits.reshape(groups, 1, lines), me * own_groups, own_groups, 0)

    chips = devices // 2
    half_groups = chips * own_groups
    sibling = [(d, d + 1 - 2 * (d % 2)) for d in range(devices)]

    same_core = [[2 * chip + c for chip in range(chips)] for c in range(2)]

    def exchange(value):
        return lax.all_to_all(value, "tm", split_axis=0, concat_axis=0, axis_index_groups=same_core, tiled=True)

    half_bytes = ptdf_tiles.size
    half_flops = hours * ptdf_tiles.size
    ahead = max(1, chips // 4)

    def tile_shape(chunks):
        return jax.ShapeDtypeStruct((chunks * own_groups, *ptdf_tiles.shape[1:]), ptdf_tiles.dtype)

    def scratch(shape):
        return pltpu.VMEM(shape.shape, shape.dtype)

    picked_shape = jax.ShapeDtypeStruct((bus_blocks, hours, width), jnp.bfloat16)
    block_shape = jax.ShapeDtypeStruct((bus_blocks, hours, width), jnp.float32)
    level_shape = jax.ShapeDtypeStruct((hours, units), jnp.float32)
    flow_shape = jax.ShapeDtypeStruct((half_groups, hours, lines), jnp.float32)
    head_shape, half_shape, rest_shape = tile_shape(ahead), tile_shape(chips), tile_shape(chips - ahead)
    sems, ahead_sems = pltpu.SemaphoreType.DMA((chips,)), pltpu.SemaphoreType.DMA((ahead,))
    sums = [scratch(block_shape)] * depth

    def product(kernel, name, outs, operands, temporary, passes=1, limit=48):
        return pl.pallas_call(
            kernel,
            out_shape=outs,
            in_specs=[HBM] * 2 + [VMEM] * len(operands),
            out_specs=[VMEM] * len(outs),
            scratch_shapes=[pltpu.SMEM(blocks.shape, blocks.dtype), pltpu.SemaphoreType.DMA, *temporary],
            compiler_params=pltpu.CompilerParams(vmem_limit_bytes=limit << 20),
            cost_estimate=pl.CostEstimate(
                flops=passes * half_flops, bytes_accessed=passes * half_bytes, transcendentals=0
            ),
            name=name,
        )(blocks, ptdf_tiles, *operands)

    def small(kernel, name, outs, operands, scratch=(), last=VMEM):
        return pl.pallas_call(
            kernel,
            out_shape=outs,
            in_specs=[VMEM] * (len(operands) - 1) + [last],
            out_specs=[VMEM] * len(outs),
            scratch_shapes=scratch,
            compiler_params=SMALL,
            cost_estimate=pl.CostEstimate(flops=half_flops, bytes_accessed=4 << 20, transcendentals=0),
            name=name,
        )(*operands)

    unit_rows = units // width

    def whole_tiles(rows):
        return -(-rows // 16) * 16

    rows_in = whole_tiles(bus_blocks + unit_rows)
    rows_out = whole_tiles(bus_blocks + unit_rows + own_groups)
    (sent,) = small(
        pack_kernel,
        "pack",
        [jax.ShapeDtypeStruct((devices, hour_rows * rows_in, width), jnp.bfloat16)],
        [base_injection, soc_init],
        [
            pltpu.VMEM((devices * hour_rows * rows_in, width), jnp.float32),
            pltpu.VMEM(soc_init.shape, soc_init.dtype),
            pltpu.SemaphoreType.DMA,
        ],
        HBM,
    )
    came = lax.all_to_all(sent, "tm", split_axis=0, concat_axis=0, tiled=True)
    came, own_limits, unit_block, unit_lane, gain, blocks = lax.optimization_barrier(
        (came, own_limits, unit_block, unit_lane, gain, blocks)
    )
    away, base, level, head = product(
        first_flow_kernel,
        "first_flow",
        [flow_shape, picked_shape, level_shape, head_shape],
        [came.reshape(hours * rows_in, width)],
        [scratch(half_shape), sems, ahead_sems, pltpu.VMEM((hours * rows_in, width), jnp.float32)],
    )
    picked = base
    price = None
    line_dual = jnp.zeros((own_groups, hours, lines), jnp.float32)
    for iteration in range(ITERS):
        arrived = lax.ppermute(away, "tm", sibling)
        if iteration == 0:
            (flows,) = product(
                own_flow_kernel, "own_flow", [flow_shape], [picked, head], [scratch(rest_shape), sems]
            )
        else:
            (flows,) = product(held_flow_kernel, "held_flow", [flow_shape], [picked, held], [], limit=40)
        pair = (flows + arrived).astype(jnp.bfloat16).reshape(chips, own_groups, hours, lines)
        parts = exchange(pair)
        shifted = jnp.sum(parts.astype(jnp.float32), axis=0) + line_dual
        clipped = jnp.clip(shifted, -own_limits, own_limits)
        line_dual = shifted - clipped
        dual = exchange(jnp.broadcast_to(line_dual.astype(jnp.bfloat16)[None], (chips, own_groups, hours, lines)))
        dual = dual.reshape(half_groups, hours, lines)
        other = lax.ppermute(dual, "tm", sibling)
        if iteration < ITERS - 1:
            before, delta, head, held = product(
                own_price_kernel,
                "own_price",
                [block_shape, block_shape, head_shape, half_shape],
                [dual, level, unit_block, unit_lane],
                [sems, ahead_sems] + sums,
                limit=36,
            )
            price, inject, picked, away = product(
                middle_kernel,
                "price_then_flow",
                [block_shape, block_shape, picked_shape, flow_shape],
                [other, before, base, delta, head],
                [scratch(rest_shape), sems] + sums,
                2,
                limit=36,
            )
        else:
            before, level, delta, head = product(
                own_price_level_kernel,
                "own_price",
                [block_shape, level_shape, block_shape, head_shape],
                [dual, price, level, unit_block, unit_lane, gain],
                [scratch(half_shape), sems, ahead_sems] + sums,
            )
            (out,) = product(
                last_kernel,
                "last_price",
                [jax.ShapeDtypeStruct((hours * rows_out, width), jnp.bfloat16)],
                [other, before, base, inject, delta, level, line_dual, unit_block, unit_lane, gain, head],
                [
                    scratch(rest_shape),
                    sems,
                    scratch(block_shape),
                    scratch(level_shape),
                    pltpu.VMEM((hours * rows_out, width), jnp.float32),
                ]
                + sums,
            )

    back = lax.all_to_all(
        out.reshape(devices, hour_rows * rows_out, width), "tm", split_axis=0, concat_axis=0, tiled=True
    )
    inject, own_dual, level = small(
        unpack_kernel,
        "unpack",
        [
            jax.ShapeDtypeStruct((hour_rows, bus_count // width, width), jnp.float32),
            jax.ShapeDtypeStruct((hour_rows, line_count // width, width), jnp.float32),
            jax.ShapeDtypeStruct((hour_rows, unit_rows, width), jnp.float32),
        ],
        [back],
    )
    inject = inject.reshape(hour_rows, bus_count)
    own_dual = own_dual.reshape(hour_rows, line_count)
    level = level.reshape(hour_rows, units)
    return (inject, own_dual, level)


def solution(mesh):
    in_specs = (
        P(("scen", "tm"), None),
        P(None, "tm", None, None),
        P(None, "tm"),
        P(),
        P(),
        P(),
        P(("scen", "tm"), None),
    )
    out_specs = (P(("scen", "tm"), None), P(("scen", "tm"), None), P(("scen", "tm"), None))
    return jax.shard_map(shards, mesh=mesh, in_specs=in_specs, out_specs=out_specs, check_vma=False)
```

```python
import functools

import jax
import jax.numpy as jnp
from jax import lax
from jax.experimental import pallas as pl
from jax.experimental.pallas import tpu as pltpu
from jax.sharding import PartitionSpec as P

ITERS = 2


step_size = 0.5
penalty = 4.0
ramp_weight = 0.5

NT = (((1,), (1,)), ((), ()))
VMEM = pl.BlockSpec(memory_space=pltpu.VMEM)
HBM = pl.BlockSpec(memory_space=pl.ANY)
SMALL = pltpu.CompilerParams(vmem_limit_bytes=12 << 20)
STRAIGHT = 64


class Half:
    def __init__(self, sibling, hbm, tiles, blocks, block_sem, sems=None, head=None):
        me = lax.axis_index("tm")
        self.core = 1 - me % 2 if sibling else me % 2
        self.tiles, self.head, self.blocks, self.sems = tiles, head, blocks, sems
        self.blocks_hbm, self.tiles_hbm = hbm
        self.chunks = lax.axis_size("tm") // 2
        self.own = self.tiles_hbm.shape[0] // (2 * self.chunks)
        self.ahead = 0 if head is None else head.shape[0] // self.own
        self.depth, self.lines, self.width = self.tiles_hbm.shape[1:]
        if sems is not None:
            for chunk in range(self.ahead, self.chunks):
                self.fetch(chunk).start()
        self.block_copy = pltpu.make_async_copy(self.blocks_hbm, blocks, block_sem)
        self.block_copy.start()

    def first_group(self, chunk):
        return (2 * chunk + self.core) * self.own

    def fetch(self, chunk):
        there = pl.ds(self.first_group(chunk), self.own)
        here = pl.ds((chunk - self.ahead) * self.own, self.own)
        return pltpu.make_async_copy(self.tiles_hbm.at[there], self.tiles.at[here], self.sems.at[chunk])

    def each_four(self, wait, four):
        rest = self.chunks - self.ahead
        per = max(n for n in range(1, rest + 1) if rest % n == 0 and n * self.own <= max(STRAIGHT, self.own))

        def one(chunk, ref, at):
            for sub in range(0, self.own, 4):
                first = (self.first_group(chunk) + sub) * self.depth
                four(
                    lambda u, k: ref[at + sub + u, k],
                    chunk * self.own + sub,
                    lambda u, k: self.blocks[first + u * self.depth + k],
                )

        def body(step, carry):
            for c in range(per):
                chunk = self.ahead + step * per + c
                if wait and self.sems is not None:
                    self.fetch(chunk).wait()
                one(chunk, self.tiles, (chunk - self.ahead) * self.own)
            return carry

        if wait:
            self.block_copy.wait()
        for chunk in range(self.ahead):
            one(chunk, self.head, chunk * self.own)
        if per == rest:
            body(0, 0)
        else:
            lax.fori_loop(0, rest // per, body, 0)


class Ahead:
    def __init__(self, half, head, sem):
        self.copies = []
        for chunk in range(head.shape[0] // half.own):
            there = pl.ds((2 * chunk + 1 - half.core) * half.own, half.own)
            here = pl.ds(chunk * half.own, half.own)
            self.copies.append(pltpu.make_async_copy(half.tiles_hbm.at[there], head.at[here], sem.at[chunk]))
            self.copies[-1].start()

    def wait(self):
        for copy in self.copies:
            copy.wait()


def wide(parts):
    return jnp.concatenate([jnp.concatenate(row, axis=1) for row in parts], axis=0)


def flow_pass(picked, half, flows, wait):
    depth = half.depth
    hours = picked.shape[1]
    even = depth - depth % 2

    def side(parts):
        return jnp.concatenate(parts, axis=1)

    def four(tile, g, block):
        rows = [[picked[block(u, k)] for k in range(depth)] for u in range(4)]
        zero = jnp.zeros_like(rows[0][0])
        for first in (0, 2):
            totals = [
                lax.dot_general(
                    side(rows[first + u][:even]),
                    side([tile(first + u, k) for k in range(even)]),
                    NT,
                    preferred_element_type=jnp.float32,
                )
                for u in range(2)
            ]
            if depth % 2:
                left = wide([[rows[first][even], zero], [zero, rows[first + 1][even]]])
                right = side([tile(first, even), tile(first + 1, even)])
                part = lax.dot_general(left, right, NT, preferred_element_type=jnp.float32)
                totals = [totals[u] + part[u * hours : (u + 1) * hours] for u in range(2)]
            for u in range(2):
                flows[g + first + u] = totals[u].astype(flows.dtype)

    half.each_four(wait, four)


def price_pass(dual, half, sums, wait):
    depth, width = half.depth, half.width
    hours = dual.shape[1]
    for ref in sums:
        ref[...] = jnp.zeros_like(ref)

    def four(tile, g, block):
        rows = [dual[g + u] for u in range(4)]
        zero = jnp.zeros_like(rows[0])
        parts = []
        for first in (0, 2):
            left = wide([[rows[first], zero], [zero, rows[first + 1]]])
            for k in range(0, depth - 1, 2):
                right = wide([[tile(first + u, k), tile(first + u, k + 1)] for u in range(2)])
                part = jnp.dot(left, right, preferred_element_type=jnp.float32)
                for u in range(2):
                    for j in range(2):
                        piece = part[u * hours : (u + 1) * hours, j * width : (j + 1) * width]
                        parts.append((first + u, k + j, piece))
        if depth % 2:
            k = depth - 1
            left = wide([[rows[0], zero], [zero, rows[1]], [rows[2], zero], [zero, rows[3]]])
            right = wide([[tile(0, k), tile(2, k)], [tile(1, k), tile(3, k)]])
            part = jnp.dot(left, right, preferred_element_type=jnp.float32)
            for u in range(4):
                at = (u // 2) * width
                parts.append((u, k, part[u * hours : (u + 1) * hours, at : at + width]))
        for u, k, part in parts:
            at = block(u, k)
            sums[k][at] = sums[k][at] + part

    half.each_four(wait, four)


def earlier(values):
    return jnp.concatenate([values[-1:], values[:-1]], axis=0)


def later(values):
    return jnp.concatenate([values[1:], values[:1]], axis=0)


def total(sums, block):
    price = sums[0][block]
    for ref in sums[1:]:
        price = price + ref[block]
    return price


def update_pass(sums, before, inject, base, delta, price_out, out):
    for block in range(sums[0].shape[0]):
        price = before[block] + total(sums, block)
        price_out[block] = price
        now = inject(block)
        new = now - step_size * (
            (now - base(block))
            + penalty * price
            + ramp_weight * (2.0 * now - earlier(now) - later(now))
        )
        out(block, new - delta[block])


def one_hot(unit_lane, cols, width):
    lane = jnp.broadcast_to(unit_lane[:, cols], (width, cols.size))
    return (lane == lax.broadcasted_iota(jnp.int32, (width, cols.size), 0)).astype(jnp.bfloat16)


def high_low(values, axis):
    high = values.astype(jnp.bfloat16)
    low = (values - high.astype(jnp.float32)).astype(jnp.bfloat16)
    return jnp.concatenate([high, low], axis=axis)


def storage_pass(level, unit_block, unit_lane, delta, gain=None, price=None, out=None):
    hours = level.shape[0]
    count, _, width = (price if delta is None else delta).shape
    span = 2 * width
    if price is not None:
        prices = high_low(jnp.concatenate([price[b] for b in range(count)], axis=0), 1)
    if delta is not None:
        delta[...] = jnp.zeros_like(delta)

    def body(c, carry):
        cols = pl.ds(pl.multiple_of(c * span, span), span)
        hot = one_hot(unit_lane, cols, width)
        block = jnp.broadcast_to(unit_block[:, cols], (hours, span))
        here = [block == b for b in range(count)]
        now = level[:, cols]
        if price is not None:
            picked = jnp.dot(prices, jnp.concatenate([hot, hot], axis=0), preferred_element_type=jnp.float32)
            found = jnp.zeros((hours, span), jnp.float32)
            for b in range(count):
                found = jnp.where(here[b], picked[b * hours : (b + 1) * hours], found)
            now = 0.5 * (now + earlier(now)) - gain[:, cols] * found
            if delta is None:
                now = jnp.where((block >= 0) & (block < count), now, 0.0)
            out[:, cols] = now
        if delta is not None:
            charge = step_size * (now - earlier(now))
            held = jnp.concatenate([jnp.where(here[b], charge, 0.0) for b in range(count)], axis=0)
            part = lax.dot_general(held.astype(jnp.bfloat16), hot, NT, preferred_element_type=jnp.float32)
            for b in range(count):
                delta[b] = delta[b] + part[b * hours : (b + 1) * hours]
        return carry

    lax.fori_loop(0, level.shape[1] // span, body, 0)


def pack_kernel(joined, out, *, units):
    devices, rows, width = out.shape
    hour_rows = joined.shape[0]
    count = (joined.shape[1] - units) // devices
    pad = jnp.zeros((rows // hour_rows - count - units, width), jnp.float32)
    for d in range(devices):
        parts = []
        for r in range(hour_rows):
            parts += [joined[r, d * count : (d + 1) * count], joined[r, devices * count :], pad]
        out[d] = jnp.concatenate(parts, axis=0).astype(out.dtype)


def first_flow_kernel(
    blocks_hbm, tiles_hbm, came, flows, picked, level, head, blocks, block_sem, tiles, sems, ahead_sem, flat
):
    half = Half(True, (blocks_hbm, tiles_hbm), tiles, blocks, block_sem, sems)
    ahead = Ahead(half, head, ahead_sem)
    count, hours, width = picked.shape
    flat[...] = came[...].astype(jnp.float32)
    rows = flat.shape[0] // hours
    for b in range(count):
        picked[b] = flat[pl.ds(b, hours, stride=rows), :].astype(picked.dtype)
    for c in range(level.shape[1] // width):
        level[:, c * width : (c + 1) * width] = flat[pl.ds(count + c, hours, stride=rows), :]
    flow_pass(picked, half, flows, True)
    ahead.wait()


def own_flow_kernel(blocks_hbm, tiles_hbm, picked, head, flows, blocks, block_sem, tiles, sems):
    flow_pass(picked, Half(False, (blocks_hbm, tiles_hbm), tiles, blocks, block_sem, sems, head), flows, True)


def held_flow_kernel(blocks_hbm, tiles_hbm, picked, tiles, flows, blocks, block_sem):
    flow_pass(picked, Half(False, (blocks_hbm, tiles_hbm), tiles, blocks, block_sem), flows, True)


def own_price(half, ahead, dual, price, sums):
    price_pass(dual, half, sums, True)
    for b in range(price.shape[0]):
        price[b] = total(sums, b)
    ahead.wait()


def own_price_kernel(
    blocks_hbm, tiles_hbm, dual, level, unit_block, unit_lane, before, delta, head, tiles,
    blocks, block_sem, sems, ahead_sem, *sums
):
    half = Half(False, (blocks_hbm, tiles_hbm), tiles, blocks, block_sem, sems)
    ahead = Ahead(half, head, ahead_sem)
    storage_pass(level, unit_block, unit_lane, delta)
    own_price(half, ahead, dual, before, sums)


def own_price_level_kernel(
    blocks_hbm, tiles_hbm, dual, price, level, unit_block, unit_lane, gain, before, level_out, delta, head,
    blocks, block_sem, tiles, sems, ahead_sem, *sums
):
    half = Half(False, (blocks_hbm, tiles_hbm), tiles, blocks, block_sem, sems)
    ahead = Ahead(half, head, ahead_sem)
    storage_pass(level, unit_block, unit_lane, delta, gain, price, level_out)
    own_price(half, ahead, dual, before, sums)


def middle_kernel(
    blocks_hbm, tiles_hbm, dual, before, base, delta, head, price, inject_out, picked, flows,
    blocks, block_sem, tiles, sems, *sums
):
    half = Half(True, (blocks_hbm, tiles_hbm), tiles, blocks, block_sem, sems, head)
    price_pass(dual, half, sums, True)

    def start(b):
        return base[b].astype(jnp.float32)

    def write(b, new):
        inject_out[b] = new
        picked[b] = new.astype(picked.dtype)

    update_pass(sums, before, start, start, delta, price, write)
    flow_pass(picked, half, flows, False)


def last_kernel(
    blocks_hbm, tiles_hbm, dual, before, base, inject, delta, level, line_dual, unit_block, unit_lane, gain, head,
    out, blocks, block_sem, tiles, sems, price, level_out, flat, *sums
):
    half = Half(True, (blocks_hbm, tiles_hbm), tiles, blocks, block_sem, sems, head)
    count, hours, width = price.shape
    rows = flat.shape[0] // hours
    flat[...] = jnp.zeros_like(flat)
    units = level.shape[1] // width
    for g in range(line_dual.shape[0]):
        flat[pl.ds(count + units + g, hours, stride=rows), :] = line_dual[g]
    price_pass(dual, half, sums, True)

    def start(b):
        return base[b].astype(jnp.float32)

    def write(b, new):
        flat[pl.ds(b, hours, stride=rows), :] = new

    update_pass(sums, before, lambda b: inject[b], start, delta, price, write)
    storage_pass(level, unit_block, unit_lane, None, gain, price, level_out)
    for c in range(units):
        flat[pl.ds(count + c, hours, stride=rows), :] = level_out[:, c * width : (c + 1) * width]
    out[...] = flat[...].astype(out.dtype)


def unpack_kernel(back, inject, line_dual, level):
    devices = back.shape[0]
    hour_rows, units = level.shape[0], level.shape[1]
    count, own = inject.shape[1] // devices, line_dual.shape[1] // devices
    rows = back.shape[1] // hour_rows
    for r in range(hour_rows):
        sum_levels = None
        for d in range(devices):
            came = back[d, r * rows : (r + 1) * rows].astype(jnp.float32)
            inject[r, d * count : (d + 1) * count] = came[:count]
            line_dual[r, d * own : (d + 1) * own] = came[count + units : count + units + own]
            part = came[count : count + units]
            sum_levels = part if sum_levels is None else sum_levels + part
        level[r] = sum_levels


def shards(base_injection, ptdf_tiles, tile_block, limits, stor_bus, stor_gain, soc_init):
    hour_rows = base_injection.shape[0]
    bus_count = base_injection.shape[1]
    line_count = limits.shape[0]
    groups, depth, lines, width = ptdf_tiles.shape
    units = stor_bus.shape[0]
    devices = lax.axis_size("tm")
    me = lax.axis_index("tm")
    buses = bus_count // devices
    bus_blocks = buses // width
    hours = hour_rows * devices
    own_groups = groups // devices
    blocks = tile_block.reshape(groups * depth)
    unit_block = (stor_bus // width - me * bus_blocks).reshape(1, units)
    unit_lane = (stor_bus % width).reshape(1, units)
    gain = stor_gain.reshape(1, units)
    own_limits = lax.dynamic_slice_in_dim(limits.reshape(groups, 1, lines), me * own_groups, own_groups, 0)

    chips = devices // 2
    half_groups = chips * own_groups
    sibling = [(d, d + 1 - 2 * (d % 2)) for d in range(devices)]

    same_core = [[2 * chip + c for chip in range(chips)] for c in range(2)]

    def exchange(value):
        return lax.all_to_all(value, "tm", split_axis=0, concat_axis=0, axis_index_groups=same_core, tiled=True)

    half_bytes = ptdf_tiles.size
    half_flops = hours * ptdf_tiles.size
    ahead = max(1, chips // 4)

    def tile_shape(chunks):
        return jax.ShapeDtypeStruct((chunks * own_groups, *ptdf_tiles.shape[1:]), ptdf_tiles.dtype)

    def scratch(shape):
        return pltpu.VMEM(shape.shape, shape.dtype)

    picked_shape = jax.ShapeDtypeStruct((bus_blocks, hours, width), jnp.bfloat16)
    block_shape = jax.ShapeDtypeStruct((bus_blocks, hours, width), jnp.float32)
    level_shape = jax.ShapeDtypeStruct((hours, units), jnp.float32)
    flow_shape = jax.ShapeDtypeStruct((half_groups, hours, lines), jnp.float32)
    head_shape, half_shape, rest_shape = tile_shape(ahead), tile_shape(chips), tile_shape(chips - ahead)
    sems, ahead_sems = pltpu.SemaphoreType.DMA((chips,)), pltpu.SemaphoreType.DMA((ahead,))
    sums = [scratch(block_shape)] * depth

    def product(kernel, name, outs, operands, temporary, passes=1, limit=48):
        return pl.pallas_call(
            kernel,
            out_shape=outs,
            in_specs=[HBM] * 2 + [VMEM] * len(operands),
            out_specs=[VMEM] * len(outs),
            scratch_shapes=[pltpu.SMEM(blocks.shape, blocks.dtype), pltpu.SemaphoreType.DMA, *temporary],
            compiler_params=pltpu.CompilerParams(vmem_limit_bytes=limit << 20),
            cost_estimate=pl.CostEstimate(
                flops=passes * half_flops, bytes_accessed=passes * half_bytes, transcendentals=0
            ),
            name=name,
        )(blocks, ptdf_tiles, *operands)

    def small(kernel, name, outs, operands):
        return pl.pallas_call(
            kernel,
            out_shape=outs,
            in_specs=[VMEM] * len(operands),
            out_specs=[VMEM] * len(outs),
            compiler_params=SMALL,
            cost_estimate=pl.CostEstimate(flops=half_flops, bytes_accessed=4 << 20, transcendentals=0),
            name=name,
        )(*operands)

    unit_rows = units // width

    def whole_tiles(rows):
        return -(-rows // 16) * 16

    rows_in = whole_tiles(bus_blocks + unit_rows)
    rows_out = whole_tiles(bus_blocks + unit_rows + own_groups)
    joined = jnp.concatenate([base_injection.astype(jnp.float32), soc_init], axis=1)
    (sent,) = small(
        functools.partial(pack_kernel, units=unit_rows),
        "pack",
        [jax.ShapeDtypeStruct((devices, hour_rows * rows_in, width), jnp.bfloat16)],
        [joined.reshape(hour_rows, (bus_count + units) // width, width)],
    )
    came = lax.all_to_all(sent, "tm", split_axis=0, concat_axis=0, tiled=True)
    came, high, low, unit_block, unit_lane, gain, blocks = lax.optimization_barrier(
        (came, own_limits, -own_limits, unit_block, unit_lane, gain, blocks)
    )
    away, base, level, head = product(
        first_flow_kernel,
        "first_flow",
        [flow_shape, picked_shape, level_shape, head_shape],
        [came.reshape(hours * rows_in, width)],
        [scratch(half_shape), sems, ahead_sems, pltpu.VMEM((hours * rows_in, width), jnp.float32)],
    )
    picked = base
    price = None
    line_dual = jnp.zeros((own_groups, hours, lines), jnp.float32)
    for iteration in range(ITERS):
        arrived = lax.ppermute(away, "tm", sibling)
        if iteration == 0:
            (flows,) = product(
                own_flow_kernel, "own_flow", [flow_shape], [picked, head], [scratch(rest_shape), sems]
            )
        else:
            (flows,) = product(held_flow_kernel, "held_flow", [flow_shape], [picked, held], [], limit=40)
        pair = (flows + arrived).astype(jnp.bfloat16).reshape(chips, own_groups, hours, lines)
        parts = exchange(pair)
        shifted = jnp.sum(parts.astype(jnp.float32), axis=0) + line_dual
        clipped = jnp.clip(shifted, low, high)
        line_dual = shifted - clipped
        dual = exchange(jnp.broadcast_to(line_dual.astype(jnp.bfloat16)[None], (chips, own_groups, hours, lines)))
        dual = dual.reshape(half_groups, hours, lines)
        other = lax.ppermute(dual, "tm", sibling)
        if iteration < ITERS - 1:
            before, delta, head, held = product(
                own_price_kernel,
                "own_price",
                [block_shape, block_shape, head_shape, half_shape],
                [dual, level, unit_block, unit_lane],
                [sems, ahead_sems] + sums,
                limit=36,
            )
            price, inject, picked, away = product(
                middle_kernel,
                "price_then_flow",
                [block_shape, block_shape, picked_shape, flow_shape],
                [other, before, base, delta, head],
                [scratch(rest_shape), sems] + sums,
                2,
                limit=36,
            )
        else:
            before, level, delta, head = product(
                own_price_level_kernel,
                "own_price",
                [block_shape, level_shape, block_shape, head_shape],
                [dual, price, level, unit_block, unit_lane, gain],
                [scratch(half_shape), sems, ahead_sems] + sums,
            )
            (out,) = product(
                last_kernel,
                "last_price",
                [jax.ShapeDtypeStruct((hours * rows_out, width), jnp.bfloat16)],
                [other, before, base, inject, delta, level, line_dual, unit_block, unit_lane, gain, head],
                [
                    scratch(rest_shape),
                    sems,
                    scratch(block_shape),
                    scratch(level_shape),
                    pltpu.VMEM((hours * rows_out, width), jnp.float32),
                ]
                + sums,
            )

    back = lax.all_to_all(
        out.reshape(devices, hour_rows * rows_out, width), "tm", split_axis=0, concat_axis=0, tiled=True
    )
    inject, own_dual, level = small(
        unpack_kernel,
        "unpack",
        [
            jax.ShapeDtypeStruct((hour_rows, bus_count // width, width), jnp.float32),
            jax.ShapeDtypeStruct((hour_rows, line_count // width, width), jnp.float32),
            jax.ShapeDtypeStruct((hour_rows, unit_rows, width), jnp.float32),
        ],
        [back],
    )
    inject = inject.reshape(hour_rows, bus_count)
    own_dual = own_dual.reshape(hour_rows, line_count)
    level = level.reshape(hour_rows, units)
    return (inject, own_dual, level)


def solution(mesh):
    in_specs = (
        P(("scen", "tm"), None),
        P(None, "tm", None, None),
        P(None, "tm"),
        P(),
        P(),
        P(),
        P(("scen", "tm"), None),
    )
    out_specs = (P(("scen", "tm"), None), P(("scen", "tm"), None), P(("scen", "tm"), None))
    return jax.shard_map(shards, mesh=mesh, in_specs=in_specs, out_specs=out_specs, check_vma=False)
```

```python
import functools

import jax
import jax.numpy as jnp
from jax import lax
from jax.experimental import pallas as pl
from jax.experimental.pallas import tpu as pltpu
from jax.sharding import PartitionSpec as P

ITERS = 2


step_size = 0.5
penalty = 4.0
ramp_weight = 0.5

NT = (((1,), (1,)), ((), ()))
VMEM = pl.BlockSpec(memory_space=pltpu.VMEM)
HBM = pl.BlockSpec(memory_space=pl.ANY)
SMALL = pltpu.CompilerParams(vmem_limit_bytes=12 << 20)
STRAIGHT = 64


class Half:
    def __init__(self, sibling, hbm, tiles, blocks, block_sem, sems=None, head=None):
        me = lax.axis_index("tm")
        self.core = 1 - me % 2 if sibling else me % 2
        self.tiles, self.head, self.blocks, self.sems = tiles, head, blocks, sems
        self.blocks_hbm, self.tiles_hbm = hbm
        self.chunks = lax.axis_size("tm") // 2
        ahead_groups = 0 if head is None else head.shape[0]
        self.own = (ahead_groups + tiles.shape[0]) // self.chunks
        self.ahead = ahead_groups // self.own
        self.depth, self.lines, self.width = tiles.shape[1:]
        if sems is not None:
            for chunk in range(self.ahead, self.chunks):
                self.fetch(chunk).start()
        self.block_copy = pltpu.make_async_copy(self.blocks_hbm, blocks, block_sem)
        self.block_copy.start()

    def first_group(self, chunk):
        return (2 * chunk + self.core) * self.own

    def fetch(self, chunk):
        there = pl.ds(self.first_group(chunk), self.own)
        here = pl.ds((chunk - self.ahead) * self.own, self.own)
        return pltpu.make_async_copy(self.tiles_hbm.at[there], self.tiles.at[here], self.sems.at[chunk])

    def each_four(self, wait, four):
        rest = self.chunks - self.ahead
        per = max(n for n in range(1, rest + 1) if rest % n == 0 and n * self.own <= max(STRAIGHT, self.own))

        def one(chunk, ref, at):
            for sub in range(0, self.own, 4):
                first = (self.first_group(chunk) + sub) * self.depth
                four(
                    lambda u, k: ref[at + sub + u, k],
                    chunk * self.own + sub,
                    lambda u, k: self.blocks[first + u * self.depth + k],
                )

        def body(step, carry):
            for c in range(per):
                chunk = self.ahead + step * per + c
                if wait and self.sems is not None:
                    self.fetch(chunk).wait()
                one(chunk, self.tiles, (chunk - self.ahead) * self.own)
            return carry

        if wait:
            self.block_copy.wait()
        for chunk in range(self.ahead):
            one(chunk, self.head, chunk * self.own)
        if per == rest:
            body(0, 0)
        else:
            lax.fori_loop(0, rest // per, body, 0)


class Ahead:
    def __init__(self, half, head, sem):
        self.copies = []
        for chunk in range(head.shape[0] // half.own):
            there = pl.ds((2 * chunk + 1 - half.core) * half.own, half.own)
            here = pl.ds(chunk * half.own, half.own)
            self.copies.append(pltpu.make_async_copy(half.tiles_hbm.at[there], head.at[here], sem.at[chunk]))
            self.copies[-1].start()

    def wait(self):
        for copy in self.copies:
            copy.wait()


def wide(parts):
    return jnp.concatenate([jnp.concatenate(row, axis=1) for row in parts], axis=0)


def flow_pass(picked, half, flows, wait):
    depth = half.depth
    hours = picked.shape[1]
    even = depth - depth % 2

    def side(parts):
        return jnp.concatenate(parts, axis=1)

    def four(tile, g, block):
        rows = [[picked[block(u, k)] for k in range(depth)] for u in range(4)]
        zero = jnp.zeros_like(rows[0][0])
        for first in (0, 2):
            totals = [
                lax.dot_general(
                    side(rows[first + u][:even]),
                    side([tile(first + u, k) for k in range(even)]),
                    NT,
                    preferred_element_type=jnp.float32,
                )
                for u in range(2)
            ]
            if depth % 2:
                left = wide([[rows[first][even], zero], [zero, rows[first + 1][even]]])
                right = side([tile(first, even), tile(first + 1, even)])
                part = lax.dot_general(left, right, NT, preferred_element_type=jnp.float32)
                totals = [totals[u] + part[u * hours : (u + 1) * hours] for u in range(2)]
            for u in range(2):
                flows[g + first + u] = totals[u].astype(flows.dtype)

    half.each_four(wait, four)


def price_pass(dual, half, sums, wait):
    depth, width = half.depth, half.width
    hours = dual.shape[1]
    even = depth - depth % 2
    for ref in sums:
        ref[...] = jnp.zeros_like(ref)

    def four(tile, g, block):
        rows = [dual[g + u] for u in range(4)]
        parts = []
        for first in (0, 2):
            for u in (first, first + 1):
                right = jnp.concatenate([tile(u, k) for k in range(even)], axis=1)
                part = jnp.dot(rows[u], right, preferred_element_type=jnp.float32)
                parts += [(u, k, part[:, k * width : (k + 1) * width]) for k in range(even)]
            if depth % 2:
                left = jnp.concatenate(rows[first : first + 2], axis=0)
                right = jnp.concatenate([tile(first, even), tile(first + 1, even)], axis=1)
                part = jnp.dot(left, right, preferred_element_type=jnp.float32)
                for u in range(2):
                    parts.append((first + u, even, part[u * hours : (u + 1) * hours, u * width : (u + 1) * width]))
        for u, k, part in parts:
            at = block(u, k)
            sums[k][at] = sums[k][at] + part

    half.each_four(wait, four)


def earlier(values):
    return jnp.concatenate([values[-1:], values[:-1]], axis=0)


def later(values):
    return jnp.concatenate([values[1:], values[:1]], axis=0)


def total(sums, block):
    price = sums[0][block]
    for ref in sums[1:]:
        price = price + ref[block]
    return price


def update_pass(sums, before, inject, base, delta, price_out, out):
    for block in range(sums[0].shape[0]):
        price = before[block] + total(sums, block)
        price_out[block] = price
        now = inject(block)
        new = now - step_size * (
            (now - base(block))
            + penalty * price
            + ramp_weight * (2.0 * now - earlier(now) - later(now))
        )
        out(block, new - delta[block])


def one_hot(unit_lane, cols, width):
    lane = jnp.broadcast_to(unit_lane[:, cols], (width, cols.size))
    return (lane == lax.broadcasted_iota(jnp.int32, (width, cols.size), 0)).astype(jnp.bfloat16)


def high_low(values, axis):
    high = values.astype(jnp.bfloat16)
    low = (values - high.astype(jnp.float32)).astype(jnp.bfloat16)
    return jnp.concatenate([high, low], axis=axis)


def storage_pass(level, unit_block, unit_lane, delta, gain=None, price=None, out=None):
    hours = level.shape[0]
    count, _, width = (price if delta is None else delta).shape
    span = 2 * width
    if price is not None:
        prices = high_low(jnp.concatenate([price[b] for b in range(count)], axis=0), 1)
    if delta is not None:
        delta[...] = jnp.zeros_like(delta)

    def body(c, carry):
        cols = pl.ds(pl.multiple_of(c * span, span), span)
        hot = one_hot(unit_lane, cols, width)
        block = jnp.broadcast_to(unit_block[:, cols], (hours, span))
        here = [block == b for b in range(count)]
        now = level[:, cols]
        if price is not None:
            picked = jnp.dot(prices, jnp.concatenate([hot, hot], axis=0), preferred_element_type=jnp.float32)
            found = jnp.zeros((hours, span), jnp.float32)
            for b in range(count):
                found = jnp.where(here[b], picked[b * hours : (b + 1) * hours], found)
            now = 0.5 * (now + earlier(now)) - gain[:, cols] * found
            if delta is None:
                now = jnp.where((block >= 0) & (block < count), now, 0.0)
            out[:, cols] = now
        if delta is not None:
            charge = step_size * (now - earlier(now))
            held = jnp.concatenate([jnp.where(here[b], charge, 0.0) for b in range(count)], axis=0)
            part = lax.dot_general(held.astype(jnp.bfloat16), hot, NT, preferred_element_type=jnp.float32)
            for b in range(count):
                delta[b] = delta[b] + part[b * hours : (b + 1) * hours]
        return carry

    lax.fori_loop(0, level.shape[1] // span, body, 0)


def pack_kernel(joined, out, flat, *, units):
    devices, rows, width = out.shape
    hour_rows = joined.shape[0]
    rows = rows // hour_rows
    count = (joined.shape[1] // width - units) // devices
    flat[...] = jnp.zeros_like(flat)

    def row(r, at):
        return joined[r : r + 1, at * width : (at + 1) * width].astype(jnp.float32)

    for r in range(hour_rows):
        levels = jnp.concatenate([row(r, devices * count + c) for c in range(units)], axis=0)
        for d in range(devices):
            at = (d * hour_rows + r) * rows
            for b in range(count):
                flat[at + b : at + b + 1, :] = row(r, d * count + b)
            flat[at + count : at + count + units, :] = levels
    out[...] = flat[...].reshape(out.shape).astype(out.dtype)


def first_flow_kernel(
    blocks_hbm, tiles_hbm, came, flows, picked, level, head, tiles, blocks, block_sem, sems, ahead_sem, flat
):
    half = Half(True, (blocks_hbm, tiles_hbm), tiles, blocks, block_sem, sems)
    ahead = Ahead(half, head, ahead_sem)
    count, hours, width = picked.shape
    flat[...] = came[...].astype(jnp.float32)
    rows = flat.shape[0] // hours
    for b in range(count):
        picked[b] = flat[pl.ds(b, hours, stride=rows), :].astype(picked.dtype)
    for c in range(level.shape[1] // width):
        level[:, c * width : (c + 1) * width] = flat[pl.ds(count + c, hours, stride=rows), :]
    flow_pass(picked, half, flows, True)
    ahead.wait()


def own_flow_kernel(blocks_hbm, tiles_hbm, picked, head, flows, tiles, blocks, block_sem, sems):
    flow_pass(picked, Half(False, (blocks_hbm, tiles_hbm), tiles, blocks, block_sem, sems, head), flows, True)


def held_flow_kernel(blocks_hbm, head, tiles, picked, flows, blocks, block_sem):
    flow_pass(picked, Half(False, (blocks_hbm, None), tiles, blocks, block_sem, head=head), flows, True)


def own_price(half, dual, price, sums):
    price_pass(dual, half, sums, True)
    for b in range(price.shape[0]):
        price[b] = total(sums, b)


def own_price_kernel(
    blocks_hbm, head, tiles, dual, level, unit_block, unit_lane, before, delta, blocks, block_sem, *sums
):
    half = Half(False, (blocks_hbm, None), tiles, blocks, block_sem, head=head)
    storage_pass(level, unit_block, unit_lane, delta)
    own_price(half, dual, before, sums)


def own_price_level_kernel(
    blocks_hbm, head, tiles, dual, price, level, unit_block, unit_lane, gain, before, level_out, delta,
    blocks, block_sem, *sums
):
    half = Half(False, (blocks_hbm, None), tiles, blocks, block_sem, head=head)
    storage_pass(level, unit_block, unit_lane, delta, gain, price, level_out)
    own_price(half, dual, before, sums)


def middle_kernel(
    blocks_hbm, tiles, dual, before, base, delta, price, inject_out, picked, flows, blocks, block_sem, *sums
):
    half = Half(True, (blocks_hbm, None), tiles, blocks, block_sem)
    price_pass(dual, half, sums, True)

    def start(b):
        return base[b].astype(jnp.float32)

    def write(b, new):
        inject_out[b] = new
        picked[b] = new.astype(picked.dtype)

    update_pass(sums, before, start, start, delta, price, write)
    flow_pass(picked, half, flows, False)


def last_kernel(
    blocks_hbm, tiles, dual, before, base, inject, delta, level, line_dual, unit_block, unit_lane, gain,
    out, blocks, block_sem, price, level_out, flat, *sums
):
    half = Half(True, (blocks_hbm, None), tiles, blocks, block_sem)
    count, hours, width = price.shape
    rows = flat.shape[0] // hours
    flat[...] = jnp.zeros_like(flat)
    units = level.shape[1] // width
    for g in range(line_dual.shape[0]):
        flat[pl.ds(count + units + g, hours, stride=rows), :] = line_dual[g]
    price_pass(dual, half, sums, True)

    def start(b):
        return base[b].astype(jnp.float32)

    def write(b, new):
        flat[pl.ds(b, hours, stride=rows), :] = new

    update_pass(sums, before, lambda b: inject[b], start, delta, price, write)
    storage_pass(level, unit_block, unit_lane, None, gain, price, level_out)
    for c in range(units):
        flat[pl.ds(count + c, hours, stride=rows), :] = level_out[:, c * width : (c + 1) * width]
    out[...] = flat[...].astype(out.dtype)


def unpack_kernel(back, inject, line_dual, level):
    devices = back.shape[0]
    hour_rows, units = level.shape[0], level.shape[1]
    count, own = inject.shape[1] // devices, line_dual.shape[1] // devices
    rows = back.shape[1] // hour_rows
    for r in range(hour_rows):
        sum_levels = None
        for d in range(devices):
            came = back[d, r * rows : (r + 1) * rows].astype(jnp.float32)
            inject[r, d * count : (d + 1) * count] = came[:count]
            line_dual[r, d * own : (d + 1) * own] = came[count + units : count + units + own]
            part = came[count : count + units]
            sum_levels = part if sum_levels is None else sum_levels + part
        level[r] = sum_levels


def shards(base_injection, ptdf_tiles, tile_block, limits, stor_bus, stor_gain, soc_init):
    hour_rows = base_injection.shape[0]
    bus_count = base_injection.shape[1]
    line_count = limits.shape[0]
    groups, depth, lines, width = ptdf_tiles.shape
    units = stor_bus.shape[0]
    devices = lax.axis_size("tm")
    me = lax.axis_index("tm")
    buses = bus_count // devices
    bus_blocks = buses // width
    hours = hour_rows * devices
    own_groups = groups // devices
    blocks = tile_block.reshape(groups * depth)
    unit_block = (stor_bus // width - me * bus_blocks).reshape(1, units)
    unit_lane = (stor_bus % width).reshape(1, units)
    gain = stor_gain.reshape(1, units)
    own_limits = lax.dynamic_slice_in_dim(limits.reshape(groups, 1, lines), me * own_groups, own_groups, 0)

    chips = devices // 2
    half_groups = chips * own_groups
    sibling = [(d, d + 1 - 2 * (d % 2)) for d in range(devices)]

    same_core = [[2 * chip + c for chip in range(chips)] for c in range(2)]

    def exchange(value):
        return lax.all_to_all(value, "tm", split_axis=0, concat_axis=0, axis_index_groups=same_core, tiled=True)

    half_bytes = ptdf_tiles.size
    half_flops = hours * ptdf_tiles.size
    ahead = max(1, chips // 4)

    def tile_shape(chunks):
        return jax.ShapeDtypeStruct((chunks * own_groups, *ptdf_tiles.shape[1:]), ptdf_tiles.dtype)

    def scratch(shape):
        return pltpu.VMEM(shape.shape, shape.dtype)

    picked_shape = jax.ShapeDtypeStruct((bus_blocks, hours, width), jnp.bfloat16)
    block_shape = jax.ShapeDtypeStruct((bus_blocks, hours, width), jnp.float32)
    level_shape = jax.ShapeDtypeStruct((hours, units), jnp.float32)
    flow_shape = jax.ShapeDtypeStruct((half_groups, hours, lines), jnp.float32)
    head_shape, half_shape, rest_shape = tile_shape(ahead), tile_shape(chips), tile_shape(chips - ahead)
    sems, ahead_sems = pltpu.SemaphoreType.DMA((chips,)), pltpu.SemaphoreType.DMA((ahead,))
    sums = [scratch(block_shape)] * depth

    def product(kernel, name, outs, operands, temporary, passes=1, hbm=(), limit=16):
        return pl.pallas_call(
            kernel,
            out_shape=outs,
            in_specs=[HBM] * (1 + len(hbm)) + [VMEM] * len(operands),
            out_specs=[VMEM] * len(outs),
            scratch_shapes=[pltpu.SMEM(blocks.shape, blocks.dtype), pltpu.SemaphoreType.DMA, *temporary],
            compiler_params=pltpu.CompilerParams(vmem_limit_bytes=limit << 20),
            cost_estimate=pl.CostEstimate(
                flops=passes * half_flops, bytes_accessed=passes * half_bytes, transcendentals=0
            ),
            name=name,
        )(blocks, *hbm, *operands)

    def small(kernel, name, outs, operands, temporary=()):
        return pl.pallas_call(
            kernel,
            out_shape=outs,
            in_specs=[VMEM] * len(operands),
            out_specs=[VMEM] * len(outs),
            scratch_shapes=temporary,
            compiler_params=SMALL,
            cost_estimate=pl.CostEstimate(flops=half_flops, bytes_accessed=4 << 20, transcendentals=0),
            name=name,
        )(*operands)

    unit_rows = units // width

    def whole_tiles(rows):
        return -(-rows // 16) * 16

    rows_in = whole_tiles(bus_blocks + unit_rows)
    rows_out = whole_tiles(bus_blocks + unit_rows + own_groups)
    joined = jnp.concatenate([base_injection, soc_init.astype(jnp.bfloat16)], axis=1)
    (sent,) = small(
        functools.partial(pack_kernel, units=unit_rows),
        "pack",
        [jax.ShapeDtypeStruct((devices, hour_rows * rows_in, width), jnp.bfloat16)],
        [joined],
        [pltpu.VMEM((devices * hour_rows * rows_in, width), jnp.float32)],
    )
    came = lax.all_to_all(sent, "tm", split_axis=0, concat_axis=0, tiled=True)
    came, high, low, unit_block, unit_lane, gain, blocks = lax.optimization_barrier(
        (came, own_limits, -own_limits, unit_block, unit_lane, gain, blocks)
    )
    away, base, level, head, other_half = product(
        first_flow_kernel,
        "first_flow",
        [flow_shape, picked_shape, level_shape, head_shape, half_shape],
        [came.reshape(hours * rows_in, width)],
        [sems, ahead_sems, pltpu.VMEM((hours * rows_in, width), jnp.float32)],
        hbm=[ptdf_tiles],
        limit=36,
    )
    picked = base
    price = None
    line_dual = jnp.zeros((own_groups, hours, lines), jnp.float32)
    for iteration in range(ITERS):
        arrived = lax.ppermute(away, "tm", sibling)
        if iteration == 0:
            flows, rest = product(
                own_flow_kernel,
                "own_flow",
                [flow_shape, rest_shape],
                [picked, head],
                [sems],
                hbm=[ptdf_tiles],
                limit=28,
            )
        else:
            (flows,) = product(held_flow_kernel, "held_flow", [flow_shape], [head, rest, picked], [])
        pair = (flows + arrived).astype(jnp.bfloat16).reshape(chips, own_groups, hours, lines)
        parts = exchange(pair)
        shifted = jnp.sum(parts.astype(jnp.float32), axis=0) + line_dual
        clipped = jnp.clip(shifted, low, high)
        line_dual = shifted - clipped
        dual = exchange(jnp.broadcast_to(line_dual.astype(jnp.bfloat16)[None], (chips, own_groups, hours, lines)))
        dual = dual.reshape(half_groups, hours, lines)
        other = lax.ppermute(dual, "tm", sibling)
        if iteration < ITERS - 1:
            before, delta = product(
                own_price_kernel,
                "own_price",
                [block_shape, block_shape],
                [head, rest, dual, level, unit_block, unit_lane],
                sums,
            )
            price, inject, picked, away = product(
                middle_kernel,
                "price_then_flow",
                [block_shape, block_shape, picked_shape, flow_shape],
                [other_half, other, before, base, delta],
                sums,
                2,
            )
        else:
            before, level, delta = product(
                own_price_level_kernel,
                "own_price",
                [block_shape, level_shape, block_shape],
                [head, rest, dual, price, level, unit_block, unit_lane, gain],
                sums,
            )
            (out,) = product(
                last_kernel,
                "last_price",
                [jax.ShapeDtypeStruct((hours * rows_out, width), jnp.bfloat16)],
                [other_half, other, before, base, inject, delta, level, line_dual, unit_block, unit_lane, gain],
                [
                    scratch(block_shape),
                    scratch(level_shape),
                    pltpu.VMEM((hours * rows_out, width), jnp.float32),
                ]
                + sums,
            )

    back = lax.all_to_all(
        out.reshape(devices, hour_rows * rows_out, width), "tm", split_axis=0, concat_axis=0, tiled=True
    )
    inject, own_dual, level = small(
        unpack_kernel,
        "unpack",
        [
            jax.ShapeDtypeStruct((hour_rows, bus_count // width, width), jnp.float32),
            jax.ShapeDtypeStruct((hour_rows, line_count // width, width), jnp.float32),
            jax.ShapeDtypeStruct((hour_rows, unit_rows, width), jnp.float32),
        ],
        [back],
    )
    inject = inject.reshape(hour_rows, bus_count)
    own_dual = own_dual.reshape(hour_rows, line_count)
    level = level.reshape(hour_rows, units)
    return (inject, own_dual, level)


def solution(mesh):
    in_specs = (
        P(("scen", "tm"), None),
        P(None, "tm", None, None),
        P(None, "tm"),
        P(),
        P(),
        P(),
        P(("scen", "tm"), None),
    )
    out_specs = (P(("scen", "tm"), None), P(("scen", "tm"), None), P(("scen", "tm"), None))
    return jax.shard_map(shards, mesh=mesh, in_specs=in_specs, out_specs=out_specs, check_vma=False)
```

```python
import functools

import jax
import jax.numpy as jnp
from jax import lax
from jax.experimental import pallas as pl
from jax.experimental.pallas import tpu as pltpu
from jax.sharding import PartitionSpec as P

ITERS = 2


step_size = 0.5
penalty = 4.0
ramp_weight = 0.5

NT = (((1,), (1,)), ((), ()))
VMEM = pl.BlockSpec(memory_space=pltpu.VMEM)
HBM = pl.BlockSpec(memory_space=pl.ANY)
SMALL = pltpu.CompilerParams(vmem_limit_bytes=12 << 20)
STRAIGHT = 64


class Half:
    def __init__(self, sibling, hbm, tiles, blocks, block_sem, sems=None, head=None):
        me = lax.axis_index("tm")
        self.core = 1 - me % 2 if sibling else me % 2
        self.tiles, self.head, self.blocks, self.sems = tiles, head, blocks, sems
        self.blocks_hbm, self.tiles_hbm = hbm
        self.chunks = lax.axis_size("tm") // 2
        ahead_groups = 0 if head is None else head.shape[0]
        self.own = (ahead_groups + tiles.shape[0]) // self.chunks
        self.ahead = ahead_groups // self.own
        self.depth, self.lines, self.width = tiles.shape[1:]
        if sems is not None:
            for chunk in range(self.ahead, self.chunks):
                self.fetch(chunk).start()
        self.block_copy = pltpu.make_async_copy(self.blocks_hbm, blocks, block_sem)
        self.block_copy.start()

    def first_group(self, chunk):
        return (2 * chunk + self.core) * self.own

    def fetch(self, chunk):
        there = pl.ds(self.first_group(chunk), self.own)
        here = pl.ds((chunk - self.ahead) * self.own, self.own)
        return pltpu.make_async_copy(self.tiles_hbm.at[there], self.tiles.at[here], self.sems.at[chunk])

    def each_four(self, wait, four):
        rest = self.chunks - self.ahead
        per = max(n for n in range(1, rest + 1) if rest % n == 0 and n * self.own <= max(STRAIGHT, self.own))

        def one(chunk, ref, at):
            for sub in range(0, self.own, 4):
                first = (self.first_group(chunk) + sub) * self.depth
                four(
                    lambda u, k: ref[at + sub + u, k],
                    chunk * self.own + sub,
                    lambda u, k: self.blocks[first + u * self.depth + k],
                )

        def body(step, carry):
            for c in range(per):
                chunk = self.ahead + step * per + c
                if wait and self.sems is not None:
                    self.fetch(chunk).wait()
                one(chunk, self.tiles, (chunk - self.ahead) * self.own)
            return carry

        if wait:
            self.block_copy.wait()
        for chunk in range(self.ahead):
            one(chunk, self.head, chunk * self.own)
        if per == rest:
            body(0, 0)
        else:
            lax.fori_loop(0, rest // per, body, 0)


class Ahead:
    def __init__(self, half, head, sem):
        self.copies = []
        for chunk in range(head.shape[0] // half.own):
            there = pl.ds((2 * chunk + 1 - half.core) * half.own, half.own)
            here = pl.ds(chunk * half.own, half.own)
            self.copies.append(pltpu.make_async_copy(half.tiles_hbm.at[there], head.at[here], sem.at[chunk]))
            self.copies[-1].start()

    def wait(self):
        for copy in self.copies:
            copy.wait()


def wide(parts):
    return jnp.concatenate([jnp.concatenate(row, axis=1) for row in parts], axis=0)


def flow_pass(picked, half, flows, wait):
    depth = half.depth
    hours = picked.shape[1]
    even = depth - depth % 2

    def side(parts):
        return jnp.concatenate(parts, axis=1)

    def four(tile, g, block):
        rows = [[picked[block(u, k)] for k in range(depth)] for u in range(4)]
        zero = jnp.zeros_like(rows[0][0])
        for first in (0, 2):
            totals = [
                lax.dot_general(
                    side(rows[first + u][:even]),
                    side([tile(first + u, k) for k in range(even)]),
                    NT,
                    preferred_element_type=jnp.float32,
                )
                for u in range(2)
            ]
            if depth % 2:
                left = wide([[rows[first][even], zero], [zero, rows[first + 1][even]]])
                right = side([tile(first, even), tile(first + 1, even)])
                part = lax.dot_general(left, right, NT, preferred_element_type=jnp.float32)
                totals = [totals[u] + part[u * hours : (u + 1) * hours] for u in range(2)]
            for u in range(2):
                flows[g + first + u] = totals[u].astype(flows.dtype)

    half.each_four(wait, four)


def price_pass(dual, half, sums, wait):
    depth, width = half.depth, half.width
    hours = dual.shape[1]
    even = depth - depth % 2
    for ref in sums:
        ref[...] = jnp.zeros_like(ref)

    def four(tile, g, block):
        rows = [dual[g + u] for u in range(4)]
        parts = []
        for first in (0, 2):
            for u in (first, first + 1):
                right = jnp.concatenate([tile(u, k) for k in range(even)], axis=1)
                part = jnp.dot(rows[u], right, preferred_element_type=jnp.float32)
                parts += [(u, k, part[:, k * width : (k + 1) * width]) for k in range(even)]
            if depth % 2:
                left = jnp.concatenate(rows[first : first + 2], axis=0)
                right = jnp.concatenate([tile(first, even), tile(first + 1, even)], axis=1)
                part = jnp.dot(left, right, preferred_element_type=jnp.float32)
                for u in range(2):
                    parts.append((first + u, even, part[u * hours : (u + 1) * hours, u * width : (u + 1) * width]))
        for u, k, part in parts:
            at = block(u, k)
            sums[k][at] = sums[k][at] + part

    half.each_four(wait, four)


def earlier(values):
    return jnp.concatenate([values[-1:], values[:-1]], axis=0)


def later(values):
    return jnp.concatenate([values[1:], values[:1]], axis=0)


def total(sums, block):
    price = sums[0][block]
    for ref in sums[1:]:
        price = price + ref[block]
    return price


def update_pass(sums, before, inject, base, delta, price_out, out):
    for block in range(sums[0].shape[0]):
        price = before[block] + total(sums, block)
        price_out[block] = price
        now = inject(block)
        new = now - step_size * (
            (now - base(block))
            + penalty * price
            + ramp_weight * (2.0 * now - earlier(now) - later(now))
        )
        out(block, new - delta[block])


def one_hot(unit_lane, cols, width):
    lane = jnp.broadcast_to(unit_lane[:, cols], (width, cols.size))
    return (lane == lax.broadcasted_iota(jnp.int32, (width, cols.size), 0)).astype(jnp.bfloat16)


def high_low(values, axis):
    high = values.astype(jnp.bfloat16)
    low = (values - high.astype(jnp.float32)).astype(jnp.bfloat16)
    return jnp.concatenate([high, low], axis=axis)


def storage_pass(level, unit_block, unit_lane, delta, gain=None, price=None, out=None):
    hours = level.shape[0]
    count, _, width = (price if delta is None else delta).shape
    span = 2 * width
    if price is not None:
        prices = high_low(jnp.concatenate([price[b] for b in range(count)], axis=0), 1)
    if delta is not None:
        delta[...] = jnp.zeros_like(delta)

    for c in range(level.shape[1] // span):
        cols = pl.ds(c * span, span)
        hot = one_hot(unit_lane, cols, width)
        block = jnp.broadcast_to(unit_block[:, cols], (hours, span))
        here = [block == b for b in range(count)]
        now = level[:, cols]
        if price is not None:
            picked = jnp.dot(prices, jnp.concatenate([hot, hot], axis=0), preferred_element_type=jnp.float32)
            found = jnp.zeros((hours, span), jnp.float32)
            for b in range(count):
                found = jnp.where(here[b], picked[b * hours : (b + 1) * hours], found)
            now = 0.5 * (now + earlier(now)) - gain[:, cols] * found
            if delta is None:
                now = jnp.where((block >= 0) & (block < count), now, 0.0)
            out[:, cols] = now
        if delta is not None:
            charge = step_size * (now - earlier(now))
            held = jnp.concatenate([jnp.where(here[b], charge, 0.0) for b in range(count)], axis=0)
            part = lax.dot_general(held.astype(jnp.bfloat16), hot, NT, preferred_element_type=jnp.float32)
            for b in range(count):
                delta[b] = delta[b] + part[b * hours : (b + 1) * hours]


def pack_kernel(joined, out, flat, *, units):
    devices, rows, width = out.shape
    hour_rows = joined.shape[0]
    rows = rows // hour_rows
    count = (joined.shape[1] // width - units) // devices
    flat[...] = jnp.zeros_like(flat)

    def row(r, at):
        return joined[r : r + 1, at * width : (at + 1) * width].astype(jnp.float32)

    for r in range(hour_rows):
        levels = jnp.concatenate([row(r, devices * count + c) for c in range(units)], axis=0)
        for d in range(devices):
            at = (d * hour_rows + r) * rows
            for b in range(count):
                flat[at + b : at + b + 1, :] = row(r, d * count + b)
            flat[at + count : at + count + units, :] = levels
    out[...] = flat[...].reshape(out.shape).astype(out.dtype)


def first_flow_kernel(
    blocks_hbm, tiles_hbm, came, flows, picked, level, head, tiles, blocks, block_sem, sems, ahead_sem, flat
):
    half = Half(True, (blocks_hbm, tiles_hbm), tiles, blocks, block_sem, sems)
    ahead = Ahead(half, head, ahead_sem)
    count, hours, width = picked.shape
    flat[...] = came[...].astype(jnp.float32)
    rows = flat.shape[0] // hours
    for b in range(count):
        picked[b] = flat[pl.ds(b, hours, stride=rows), :].astype(picked.dtype)
    for c in range(level.shape[1] // width):
        level[:, c * width : (c + 1) * width] = flat[pl.ds(count + c, hours, stride=rows), :]
    flow_pass(picked, half, flows, True)
    ahead.wait()


def own_flow_kernel(blocks_hbm, tiles_hbm, picked, head, flows, tiles, blocks, block_sem, sems):
    flow_pass(picked, Half(False, (blocks_hbm, tiles_hbm), tiles, blocks, block_sem, sems, head), flows, True)


def held_flow_kernel(blocks_hbm, head, tiles, picked, flows, blocks, block_sem):
    flow_pass(picked, Half(False, (blocks_hbm, None), tiles, blocks, block_sem, head=head), flows, True)


def own_price(half, dual, price, sums):
    price_pass(dual, half, sums, True)
    for b in range(price.shape[0]):
        price[b] = total(sums, b)


def own_price_kernel(
    blocks_hbm, head, tiles, dual, level, unit_block, unit_lane, before, delta, blocks, block_sem, *sums
):
    half = Half(False, (blocks_hbm, None), tiles, blocks, block_sem, head=head)
    storage_pass(level, unit_block, unit_lane, delta)
    own_price(half, dual, before, sums)


def own_price_level_kernel(
    blocks_hbm, head, tiles, dual, price, level, unit_block, unit_lane, gain, before, level_out, delta,
    blocks, block_sem, *sums
):
    half = Half(False, (blocks_hbm, None), tiles, blocks, block_sem, head=head)
    storage_pass(level, unit_block, unit_lane, delta, gain, price, level_out)
    own_price(half, dual, before, sums)


def middle_kernel(
    blocks_hbm, tiles, dual, before, base, delta, price, inject_out, picked, flows, blocks, block_sem, *sums
):
    half = Half(True, (blocks_hbm, None), tiles, blocks, block_sem)
    price_pass(dual, half, sums, True)

    def start(b):
        return base[b].astype(jnp.float32)

    def write(b, new):
        inject_out[b] = new
        picked[b] = new.astype(picked.dtype)

    update_pass(sums, before, start, start, delta, price, write)
    flow_pass(picked, half, flows, False)


def last_kernel(
    blocks_hbm, tiles, dual, before, base, inject, delta, level, line_dual, unit_block, unit_lane, gain,
    out, blocks, block_sem, price, level_out, flat, *sums
):
    half = Half(True, (blocks_hbm, None), tiles, blocks, block_sem)
    count, hours, width = price.shape
    rows = flat.shape[0] // hours
    flat[...] = jnp.zeros_like(flat)
    units = level.shape[1] // width
    for g in range(line_dual.shape[0]):
        flat[pl.ds(count + units + g, hours, stride=rows), :] = line_dual[g]
    price_pass(dual, half, sums, True)

    def start(b):
        return base[b].astype(jnp.float32)

    def write(b, new):
        flat[pl.ds(b, hours, stride=rows), :] = new

    update_pass(sums, before, lambda b: inject[b], start, delta, price, write)
    storage_pass(level, unit_block, unit_lane, None, gain, price, level_out)
    for c in range(units):
        flat[pl.ds(count + c, hours, stride=rows), :] = level_out[:, c * width : (c + 1) * width]
    out[...] = flat[...].astype(out.dtype)


def unpack_kernel(back, inject, line_dual, level):
    devices = back.shape[0]
    hour_rows, units = level.shape[0], level.shape[1]
    count, own = inject.shape[1] // devices, line_dual.shape[1] // devices
    rows = back.shape[1] // hour_rows
    for r in range(hour_rows):
        sum_levels = None
        for d in range(devices):
            came = back[d, r * rows : (r + 1) * rows].astype(jnp.float32)
            inject[r, d * count : (d + 1) * count] = came[:count]
            line_dual[r, d * own : (d + 1) * own] = came[count + units : count + units + own]
            part = came[count : count + units]
            sum_levels = part if sum_levels is None else sum_levels + part
        level[r] = sum_levels


def shards(base_injection, ptdf_tiles, tile_block, limits, stor_bus, stor_gain, soc_init):
    hour_rows = base_injection.shape[0]
    bus_count = base_injection.shape[1]
    line_count = limits.shape[0]
    groups, depth, lines, width = ptdf_tiles.shape
    units = stor_bus.shape[0]
    devices = lax.axis_size("tm")
    me = lax.axis_index("tm")
    buses = bus_count // devices
    bus_blocks = buses // width
    hours = hour_rows * devices
    own_groups = groups // devices
    blocks = tile_block.reshape(groups * depth)
    unit_block = (stor_bus // width - me * bus_blocks).reshape(1, units)
    unit_lane = (stor_bus % width).reshape(1, units)
    gain = stor_gain.reshape(1, units)
    own_limits = lax.dynamic_slice_in_dim(limits.reshape(groups, 1, lines), me * own_groups, own_groups, 0)

    chips = devices // 2
    half_groups = chips * own_groups
    sibling = [(d, d + 1 - 2 * (d % 2)) for d in range(devices)]

    same_core = [[2 * chip + c for chip in range(chips)] for c in range(2)]

    def exchange(value):
        return lax.all_to_all(value, "tm", split_axis=0, concat_axis=0, axis_index_groups=same_core, tiled=True)

    half_bytes = ptdf_tiles.size
    half_flops = hours * ptdf_tiles.size
    ahead = max(1, chips // 4)

    def tile_shape(chunks):
        return jax.ShapeDtypeStruct((chunks * own_groups, *ptdf_tiles.shape[1:]), ptdf_tiles.dtype)

    def scratch(shape):
        return pltpu.VMEM(shape.shape, shape.dtype)

    picked_shape = jax.ShapeDtypeStruct((bus_blocks, hours, width), jnp.bfloat16)
    block_shape = jax.ShapeDtypeStruct((bus_blocks, hours, width), jnp.float32)
    level_shape = jax.ShapeDtypeStruct((hours, units), jnp.float32)
    flow_shape = jax.ShapeDtypeStruct((half_groups, hours, lines), jnp.float32)
    head_shape, half_shape, rest_shape = tile_shape(ahead), tile_shape(chips), tile_shape(chips - ahead)
    sems, ahead_sems = pltpu.SemaphoreType.DMA((chips,)), pltpu.SemaphoreType.DMA((ahead,))
    sums = [scratch(block_shape)] * depth

    def product(kernel, name, outs, operands, temporary, passes=1, hbm=(), limit=16):
        return pl.pallas_call(
            kernel,
            out_shape=outs,
            in_specs=[HBM] * (1 + len(hbm)) + [VMEM] * len(operands),
            out_specs=[VMEM] * len(outs),
            scratch_shapes=[pltpu.SMEM(blocks.shape, blocks.dtype), pltpu.SemaphoreType.DMA, *temporary],
            compiler_params=pltpu.CompilerParams(vmem_limit_bytes=limit << 20),
            cost_estimate=pl.CostEstimate(
                flops=passes * half_flops, bytes_accessed=passes * half_bytes, transcendentals=0
            ),
            name=name,
        )(blocks, *hbm, *operands)

    def small(kernel, name, outs, operands, temporary=()):
        return pl.pallas_call(
            kernel,
            out_shape=outs,
            in_specs=[VMEM] * len(operands),
            out_specs=[VMEM] * len(outs),
            scratch_shapes=temporary,
            compiler_params=SMALL,
            cost_estimate=pl.CostEstimate(flops=half_flops, bytes_accessed=4 << 20, transcendentals=0),
            name=name,
        )(*operands)

    unit_rows = units // width

    def whole_tiles(rows):
        return -(-rows // 16) * 16

    rows_in = whole_tiles(bus_blocks + unit_rows)
    rows_out = whole_tiles(bus_blocks + unit_rows + own_groups)
    joined = jnp.concatenate([base_injection, soc_init.astype(jnp.bfloat16)], axis=1)
    (sent,) = small(
        functools.partial(pack_kernel, units=unit_rows),
        "pack",
        [jax.ShapeDtypeStruct((devices, hour_rows * rows_in, width), jnp.bfloat16)],
        [joined],
        [pltpu.VMEM((devices * hour_rows * rows_in, width), jnp.float32)],
    )
    came = lax.all_to_all(sent, "tm", split_axis=0, concat_axis=0, tiled=True)
    came, high, low, unit_block, unit_lane, gain, blocks = lax.optimization_barrier(
        (came, own_limits, -own_limits, unit_block, unit_lane, gain, blocks)
    )
    away, base, level, head, other_half = product(
        first_flow_kernel,
        "first_flow",
        [flow_shape, picked_shape, level_shape, head_shape, half_shape],
        [came.reshape(hours * rows_in, width)],
        [sems, ahead_sems, pltpu.VMEM((hours * rows_in, width), jnp.float32)],
        hbm=[ptdf_tiles],
        limit=36,
    )
    picked = base
    price = None
    line_dual = jnp.zeros((own_groups, hours, lines), jnp.float32)
    for iteration in range(ITERS):
        arrived = lax.ppermute(away, "tm", sibling)
        if iteration == 0:
            flows, rest = product(
                own_flow_kernel,
                "own_flow",
                [flow_shape, rest_shape],
                [picked, head],
                [sems],
                hbm=[ptdf_tiles],
                limit=28,
            )
        else:
            (flows,) = product(held_flow_kernel, "held_flow", [flow_shape], [head, rest, picked], [])
        pair = (flows + arrived).astype(jnp.bfloat16).reshape(chips, own_groups, hours, lines)
        parts = exchange(pair)
        shifted = jnp.sum(parts.astype(jnp.float32), axis=0) + line_dual
        clipped = jnp.clip(shifted, low, high)
        line_dual = shifted - clipped
        dual = exchange(jnp.broadcast_to(line_dual.astype(jnp.bfloat16)[None], (chips, own_groups, hours, lines)))
        dual = dual.reshape(half_groups, hours, lines)
        other = lax.ppermute(dual, "tm", sibling)
        if iteration < ITERS - 1:
            before, delta = product(
                own_price_kernel,
                "own_price",
                [block_shape, block_shape],
                [head, rest, dual, level, unit_block, unit_lane],
                sums,
            )
            price, inject, picked, away = product(
                middle_kernel,
                "price_then_flow",
                [block_shape, block_shape, picked_shape, flow_shape],
                [other_half, other, before, base, delta],
                sums,
                2,
            )
        else:
            before, level, delta = product(
                own_price_level_kernel,
                "own_price",
                [block_shape, level_shape, block_shape],
                [head, rest, dual, price, level, unit_block, unit_lane, gain],
                sums,
            )
            (out,) = product(
                last_kernel,
                "last_price",
                [jax.ShapeDtypeStruct((hours * rows_out, width), jnp.bfloat16)],
                [other_half, other, before, base, inject, delta, level, line_dual, unit_block, unit_lane, gain],
                [
                    scratch(block_shape),
                    scratch(level_shape),
                    pltpu.VMEM((hours * rows_out, width), jnp.float32),
                ]
                + sums,
            )

    back = lax.all_to_all(
        out.reshape(devices, hour_rows * rows_out, width), "tm", split_axis=0, concat_axis=0, tiled=True
    )
    inject, own_dual, level = small(
        unpack_kernel,
        "unpack",
        [
            jax.ShapeDtypeStruct((hour_rows, bus_count // width, width), jnp.float32),
            jax.ShapeDtypeStruct((hour_rows, line_count // width, width), jnp.float32),
            jax.ShapeDtypeStruct((hour_rows, unit_rows, width), jnp.float32),
        ],
        [back],
    )
    inject = inject.reshape(hour_rows, bus_count)
    own_dual = own_dual.reshape(hour_rows, line_count)
    level = level.reshape(hour_rows, units)
    return (inject, own_dual, level)


def solution(mesh):
    in_specs = (
        P(("scen", "tm"), None),
        P(None, "tm", None, None),
        P(None, "tm"),
        P(),
        P(),
        P(),
        P(("scen", "tm"), None),
    )
    out_specs = (P(("scen", "tm"), None), P(("scen", "tm"), None), P(("scen", "tm"), None))
    return jax.shard_map(shards, mesh=mesh, in_specs=in_specs, out_specs=out_specs, check_vma=False)
```

```python
import jax
import jax.numpy as jnp
from jax import lax
from jax.experimental import pallas as pl
from jax.experimental.pallas import tpu as pltpu
from jax.sharding import PartitionSpec as P

ITERS = 2


step_size = 0.5
penalty = 4.0
ramp_weight = 0.5

NT = (((1,), (1,)), ((), ()))
VMEM = pl.BlockSpec(memory_space=pltpu.VMEM)
HBM = pl.BlockSpec(memory_space=pl.ANY)
SMALL = pltpu.CompilerParams(vmem_limit_bytes=12 << 20)
STRAIGHT = 64


class Half:
    def __init__(self, sibling, hbm, tiles, blocks, block_sem, sems=None, head=None):
        me = lax.axis_index("tm")
        self.core = 1 - me % 2 if sibling else me % 2
        self.tiles, self.head, self.blocks, self.sems = tiles, head, blocks, sems
        self.blocks_hbm, self.tiles_hbm = hbm
        self.chunks = lax.axis_size("tm") // 2
        ahead_groups = 0 if head is None else head.shape[0]
        self.own = (ahead_groups + tiles.shape[0]) // self.chunks
        self.ahead = ahead_groups // self.own
        self.depth, self.lines, self.width = tiles.shape[1:]
        if sems is not None:
            for chunk in range(self.ahead, self.chunks):
                self.fetch(chunk).start()
        self.block_copy = pltpu.make_async_copy(self.blocks_hbm, blocks, block_sem)
        self.block_copy.start()

    def first_group(self, chunk):
        return (2 * chunk + self.core) * self.own

    def fetch(self, chunk):
        there = pl.ds(self.first_group(chunk), self.own)
        here = pl.ds((chunk - self.ahead) * self.own, self.own)
        return pltpu.make_async_copy(self.tiles_hbm.at[there], self.tiles.at[here], self.sems.at[chunk])

    def each_four(self, wait, four):
        rest = self.chunks - self.ahead
        per = max(n for n in range(1, rest + 1) if rest % n == 0 and n * self.own <= max(STRAIGHT, self.own))

        def one(chunk, ref, at):
            for sub in range(0, self.own, 4):
                first = (self.first_group(chunk) + sub) * self.depth
                four(
                    lambda u, k: ref[at + sub + u, k],
                    chunk * self.own + sub,
                    lambda u, k: self.blocks[first + u * self.depth + k],
                )

        def body(step, carry):
            for c in range(per):
                chunk = self.ahead + step * per + c
                if wait and self.sems is not None:
                    self.fetch(chunk).wait()
                one(chunk, self.tiles, (chunk - self.ahead) * self.own)
            return carry

        if wait:
            self.block_copy.wait()
        for chunk in range(self.ahead):
            one(chunk, self.head, chunk * self.own)
        if per == rest:
            body(0, 0)
        else:
            lax.fori_loop(0, rest // per, body, 0)


class Ahead:
    def __init__(self, half, head, sem):
        self.copies = []
        for chunk in range(head.shape[0] // half.own):
            there = pl.ds((2 * chunk + 1 - half.core) * half.own, half.own)
            here = pl.ds(chunk * half.own, half.own)
            self.copies.append(pltpu.make_async_copy(half.tiles_hbm.at[there], head.at[here], sem.at[chunk]))
            self.copies[-1].start()

    def wait(self):
        for copy in self.copies:
            copy.wait()


def wide(parts):
    return jnp.concatenate([jnp.concatenate(row, axis=1) for row in parts], axis=0)


def flow_pass(picked, half, flows, wait):
    depth = half.depth
    hours = picked.shape[1]
    even = depth - depth % 2

    def side(parts):
        return jnp.concatenate(parts, axis=1)

    def four(tile, g, block):
        rows = [[picked[block(u, k)] for k in range(depth)] for u in range(4)]
        zero = jnp.zeros_like(rows[0][0])
        for first in (0, 2):
            totals = [
                lax.dot_general(
                    side(rows[first + u][:even]),
                    side([tile(first + u, k) for k in range(even)]),
                    NT,
                    preferred_element_type=jnp.float32,
                )
                for u in range(2)
            ]
            if depth % 2:
                left = wide([[rows[first][even], zero], [zero, rows[first + 1][even]]])
                right = side([tile(first, even), tile(first + 1, even)])
                part = lax.dot_general(left, right, NT, preferred_element_type=jnp.float32)
                totals = [totals[u] + part[u * hours : (u + 1) * hours] for u in range(2)]
            for u in range(2):
                flows[g + first + u] = totals[u].astype(flows.dtype)

    half.each_four(wait, four)


def price_pass(dual, half, sums, wait):
    depth, width = half.depth, half.width
    hours = dual.shape[1]
    even = depth - depth % 2
    for ref in sums:
        ref[...] = jnp.zeros_like(ref)

    def four(tile, g, block):
        rows = [dual[g + u] for u in range(4)]
        parts = []
        for first in (0, 2):
            for u in (first, first + 1):
                right = jnp.concatenate([tile(u, k) for k in range(even)], axis=1)
                part = jnp.dot(rows[u], right, preferred_element_type=jnp.float32)
                parts += [(u, k, part[:, k * width : (k + 1) * width]) for k in range(even)]
            if depth % 2:
                left = jnp.concatenate(rows[first : first + 2], axis=0)
                right = jnp.concatenate([tile(first, even), tile(first + 1, even)], axis=1)
                part = jnp.dot(left, right, preferred_element_type=jnp.float32)
                for u in range(2):
                    parts.append((first + u, even, part[u * hours : (u + 1) * hours, u * width : (u + 1) * width]))
        for u, k, part in parts:
            at = block(u, k)
            sums[k][at] = sums[k][at] + part

    half.each_four(wait, four)


def earlier(values):
    return jnp.concatenate([values[-1:], values[:-1]], axis=0)


def later(values):
    return jnp.concatenate([values[1:], values[:1]], axis=0)


def total(sums, block):
    price = sums[0][block]
    for ref in sums[1:]:
        price = price + ref[block]
    return price


def update_pass(sums, before, inject, base, delta, price_out, out):
    for block in range(sums[0].shape[0]):
        price = before[block] + total(sums, block)
        price_out[block] = price
        now = inject(block)
        new = now - step_size * (
            (now - base(block))
            + penalty * price
            + ramp_weight * (2.0 * now - earlier(now) - later(now))
        )
        out(block, new - delta[block])


def one_hot(unit_lane, cols, width):
    lane = jnp.broadcast_to(unit_lane[:, cols], (width, cols.size))
    return (lane == lax.broadcasted_iota(jnp.int32, (width, cols.size), 0)).astype(jnp.bfloat16)


def high_low(values, axis):
    high = values.astype(jnp.bfloat16)
    low = (values - high.astype(jnp.float32)).astype(jnp.bfloat16)
    return jnp.concatenate([high, low], axis=axis)


def storage_pass(level, unit_block, unit_lane, delta, gain=None, price=None, out=None):
    hours = level.shape[0]
    count, _, width = (price if delta is None else delta).shape
    span = 2 * width
    if price is not None:
        prices = high_low(jnp.concatenate([price[b] for b in range(count)], axis=0), 1)
    if delta is not None:
        delta[...] = jnp.zeros_like(delta)

    for c in range(level.shape[1] // span):
        cols = pl.ds(c * span, span)
        hot = one_hot(unit_lane, cols, width)
        block = jnp.broadcast_to(unit_block[:, cols], (hours, span))
        here = [block == b for b in range(count)]
        now = level[:, cols]
        if price is not None:
            picked = jnp.dot(prices, jnp.concatenate([hot, hot], axis=0), preferred_element_type=jnp.float32)
            found = jnp.zeros((hours, span), jnp.float32)
            for b in range(count):
                found = jnp.where(here[b], picked[b * hours : (b + 1) * hours], found)
            now = 0.5 * (now + earlier(now)) - gain[:, cols] * found
            if delta is None:
                now = jnp.where((block >= 0) & (block < count), now, 0.0)
            out[:, cols] = now
        if delta is not None:
            charge = step_size * (now - earlier(now))
            held = jnp.concatenate([jnp.where(here[b], charge, 0.0) for b in range(count)], axis=0)
            part = lax.dot_general(held.astype(jnp.bfloat16), hot, NT, preferred_element_type=jnp.float32)
            for b in range(count):
                delta[b] = delta[b] + part[b * hours : (b + 1) * hours]


def pack_kernel(base, soc, out):
    devices, rows, width = out.shape
    hour_rows, units = soc.shape[0], soc.shape[1]
    count = base.shape[1] // devices
    pad = jnp.zeros((rows // hour_rows - count - units, width), jnp.float32)
    for d in range(devices):
        parts = []
        for r in range(hour_rows):
            parts += [base[r, d * count : (d + 1) * count], soc[r], pad]
        out[d] = jnp.concatenate(parts, axis=0).astype(out.dtype)


def first_flow_kernel(
    blocks_hbm, tiles_hbm, came, flows, picked, level, head, tiles, blocks, block_sem, sems, ahead_sem, flat
):
    half = Half(True, (blocks_hbm, tiles_hbm), tiles, blocks, block_sem, sems)
    ahead = Ahead(half, head, ahead_sem)
    count, hours, width = picked.shape
    flat[...] = came[...].astype(jnp.float32)
    rows = flat.shape[0] // hours
    for b in range(count):
        picked[b] = flat[pl.ds(b, hours, stride=rows), :].astype(picked.dtype)
    for c in range(level.shape[1] // width):
        level[:, c * width : (c + 1) * width] = flat[pl.ds(count + c, hours, stride=rows), :]
    flow_pass(picked, half, flows, True)
    ahead.wait()


def own_flow_kernel(blocks_hbm, tiles_hbm, picked, head, flows, tiles, blocks, block_sem, sems):
    flow_pass(picked, Half(False, (blocks_hbm, tiles_hbm), tiles, blocks, block_sem, sems, head), flows, True)


def held_flow_kernel(blocks_hbm, head, tiles, picked, flows, blocks, block_sem):
    flow_pass(picked, Half(False, (blocks_hbm, None), tiles, blocks, block_sem, head=head), flows, True)


def own_price(half, dual, price, sums):
    price_pass(dual, half, sums, True)
    for b in range(price.shape[0]):
        price[b] = total(sums, b)


def own_price_kernel(
    blocks_hbm, head, tiles, dual, level, unit_block, unit_lane, before, delta, blocks, block_sem, *sums
):
    half = Half(False, (blocks_hbm, None), tiles, blocks, block_sem, head=head)
    storage_pass(level, unit_block, unit_lane, delta)
    own_price(half, dual, before, sums)


def own_price_level_kernel(
    blocks_hbm, head, tiles, dual, price, level, unit_block, unit_lane, gain, before, level_out, delta,
    blocks, block_sem, *sums
):
    half = Half(False, (blocks_hbm, None), tiles, blocks, block_sem, head=head)
    storage_pass(level, unit_block, unit_lane, delta, gain, price, level_out)
    own_price(half, dual, before, sums)


def middle_kernel(
    blocks_hbm, tiles, dual, before, base, delta, price, inject_out, picked, flows, blocks, block_sem, *sums
):
    half = Half(True, (blocks_hbm, None), tiles, blocks, block_sem)
    price_pass(dual, half, sums, True)

    def start(b):
        return base[b].astype(jnp.float32)

    def write(b, new):
        inject_out[b] = new
        picked[b] = new.astype(picked.dtype)

    update_pass(sums, before, start, start, delta, price, write)
    flow_pass(picked, half, flows, False)


def last_kernel(
    blocks_hbm, tiles, dual, before, base, inject, delta, level, line_dual, unit_block, unit_lane, gain,
    out, blocks, block_sem, price, level_out, flat, *sums
):
    half = Half(True, (blocks_hbm, None), tiles, blocks, block_sem)
    count, hours, width = price.shape
    rows = flat.shape[0] // hours
    flat[...] = jnp.zeros_like(flat)
    units = level.shape[1] // width
    for g in range(line_dual.shape[0]):
        flat[pl.ds(count + units + g, hours, stride=rows), :] = line_dual[g]
    price_pass(dual, half, sums, True)

    def start(b):
        return base[b].astype(jnp.float32)

    def write(b, new):
        flat[pl.ds(b, hours, stride=rows), :] = new

    update_pass(sums, before, lambda b: inject[b], start, delta, price, write)
    storage_pass(level, unit_block, unit_lane, None, gain, price, level_out)
    for c in range(units):
        flat[pl.ds(count + c, hours, stride=rows), :] = level_out[:, c * width : (c + 1) * width]
    out[...] = flat[...].astype(out.dtype)


def unpack_kernel(back, inject, line_dual, level):
    devices = back.shape[0]
    hour_rows, units = level.shape[0], level.shape[1]
    count, own = inject.shape[1] // devices, line_dual.shape[1] // devices
    rows = back.shape[1] // hour_rows
    for r in range(hour_rows):
        sum_levels = None
        for d in range(devices):
            came = back[d, r * rows : (r + 1) * rows].astype(jnp.float32)
            inject[r, d * count : (d + 1) * count] = came[:count]
            line_dual[r, d * own : (d + 1) * own] = came[count + units : count + units + own]
            part = came[count : count + units]
            sum_levels = part if sum_levels is None else sum_levels + part
        level[r] = sum_levels


def shards(base_injection, ptdf_tiles, tile_block, limits, stor_bus, stor_gain, soc_init):
    hour_rows = base_injection.shape[0]
    bus_count = base_injection.shape[1]
    line_count = limits.shape[0]
    groups, depth, lines, width = ptdf_tiles.shape
    units = stor_bus.shape[0]
    devices = lax.axis_size("tm")
    me = lax.axis_index("tm")
    buses = bus_count // devices
    bus_blocks = buses // width
    hours = hour_rows * devices
    own_groups = groups // devices
    blocks = tile_block.reshape(groups * depth)
    unit_block = (stor_bus // width - me * bus_blocks).reshape(1, units)
    unit_lane = (stor_bus % width).reshape(1, units)
    gain = stor_gain.reshape(1, units)
    own_limits = lax.dynamic_slice_in_dim(limits.reshape(groups, 1, lines), me * own_groups, own_groups, 0)

    chips = devices // 2
    half_groups = chips * own_groups
    sibling = [(d, d + 1 - 2 * (d % 2)) for d in range(devices)]

    same_core = [[2 * chip + c for chip in range(chips)] for c in range(2)]

    def exchange(value):
        return lax.all_to_all(value, "tm", split_axis=0, concat_axis=0, axis_index_groups=same_core, tiled=True)

    half_bytes = ptdf_tiles.size
    half_flops = hours * ptdf_tiles.size
    ahead = max(1, chips // 4)

    def tile_shape(chunks):
        return jax.ShapeDtypeStruct((chunks * own_groups, *ptdf_tiles.shape[1:]), ptdf_tiles.dtype)

    def scratch(shape):
        return pltpu.VMEM(shape.shape, shape.dtype)

    picked_shape = jax.ShapeDtypeStruct((bus_blocks, hours, width), jnp.bfloat16)
    block_shape = jax.ShapeDtypeStruct((bus_blocks, hours, width), jnp.float32)
    level_shape = jax.ShapeDtypeStruct((hours, units), jnp.float32)
    flow_shape = jax.ShapeDtypeStruct((half_groups, hours, lines), jnp.float32)
    head_shape, half_shape, rest_shape = tile_shape(ahead), tile_shape(chips), tile_shape(chips - ahead)
    sems, ahead_sems = pltpu.SemaphoreType.DMA((chips,)), pltpu.SemaphoreType.DMA((ahead,))
    sums = [scratch(block_shape)] * depth

    def product(kernel, name, outs, operands, temporary, passes=1, hbm=(), limit=16):
        return pl.pallas_call(
            kernel,
            out_shape=outs,
            in_specs=[HBM] * (1 + len(hbm)) + [VMEM] * len(operands),
            out_specs=[VMEM] * len(outs),
            scratch_shapes=[pltpu.SMEM(blocks.shape, blocks.dtype), pltpu.SemaphoreType.DMA, *temporary],
            compiler_params=pltpu.CompilerParams(vmem_limit_bytes=limit << 20),
            cost_estimate=pl.CostEstimate(
                flops=passes * half_flops, bytes_accessed=passes * half_bytes, transcendentals=0
            ),
            name=name,
        )(blocks, *hbm, *operands)

    def small(kernel, name, outs, operands):
        return pl.pallas_call(
            kernel,
            out_shape=outs,
            in_specs=[VMEM] * len(operands),
            out_specs=[VMEM] * len(outs),
            compiler_params=SMALL,
            cost_estimate=pl.CostEstimate(flops=half_flops, bytes_accessed=4 << 20, transcendentals=0),
            name=name,
        )(*operands)

    unit_rows = units // width

    def whole_tiles(rows):
        return -(-rows // 16) * 16

    rows_in = whole_tiles(bus_blocks + unit_rows)
    rows_out = whole_tiles(bus_blocks + unit_rows + own_groups)
    (sent,) = small(
        pack_kernel,
        "pack",
        [jax.ShapeDtypeStruct((devices, hour_rows * rows_in, width), jnp.bfloat16)],
        [
            base_injection.astype(jnp.float32).reshape(hour_rows, bus_count // width, width),
            soc_init.reshape(hour_rows, unit_rows, width),
        ],
    )
    came = lax.all_to_all(sent, "tm", split_axis=0, concat_axis=0, tiled=True)
    came, high, low, unit_block, unit_lane, gain, blocks = lax.optimization_barrier(
        (came, own_limits, -own_limits, unit_block, unit_lane, gain, blocks)
    )
    away, base, level, head, other_half = product(
        first_flow_kernel,
        "first_flow",
        [flow_shape, picked_shape, level_shape, head_shape, half_shape],
        [came.reshape(hours * rows_in, width)],
        [sems, ahead_sems, pltpu.VMEM((hours * rows_in, width), jnp.float32)],
        hbm=[ptdf_tiles],
        limit=36,
    )
    picked = base
    price = None
    line_dual = jnp.zeros((own_groups, hours, lines), jnp.float32)
    for iteration in range(ITERS):
        arrived = lax.ppermute(away, "tm", sibling)
        if iteration == 0:
            flows, rest = product(
                own_flow_kernel,
                "own_flow",
                [flow_shape, rest_shape],
                [picked, head],
                [sems],
                hbm=[ptdf_tiles],
                limit=28,
            )
        else:
            (flows,) = product(held_flow_kernel, "held_flow", [flow_shape], [head, rest, picked], [])
        pair = (flows + arrived).astype(jnp.bfloat16).reshape(chips, own_groups, hours, lines)
        parts = exchange(pair)
        shifted = jnp.sum(parts.astype(jnp.float32), axis=0) + line_dual
        clipped = jnp.clip(shifted, low, high)
        line_dual = shifted - clipped
        dual = exchange(jnp.broadcast_to(line_dual.astype(jnp.bfloat16)[None], (chips, own_groups, hours, lines)))
        dual = dual.reshape(half_groups, hours, lines)
        other = lax.ppermute(dual, "tm", sibling)
        if iteration < ITERS - 1:
            before, delta = product(
                own_price_kernel,
                "own_price",
                [block_shape, block_shape],
                [head, rest, dual, level, unit_block, unit_lane],
                sums,
            )
            price, inject, picked, away = product(
                middle_kernel,
                "price_then_flow",
                [block_shape, block_shape, picked_shape, flow_shape],
                [other_half, other, before, base, delta],
                sums,
                2,
            )
        else:
            before, level, delta = product(
                own_price_level_kernel,
                "own_price",
                [block_shape, level_shape, block_shape],
                [head, rest, dual, price, level, unit_block, unit_lane, gain],
                sums,
            )
            (out,) = product(
                last_kernel,
                "last_price",
                [jax.ShapeDtypeStruct((hours * rows_out, width), jnp.bfloat16)],
                [other_half, other, before, base, inject, delta, level, line_dual, unit_block, unit_lane, gain],
                [
                    scratch(block_shape),
                    scratch(level_shape),
                    pltpu.VMEM((hours * rows_out, width), jnp.float32),
                ]
                + sums,
            )

    back = lax.all_to_all(
        out.reshape(devices, hour_rows * rows_out, width), "tm", split_axis=0, concat_axis=0, tiled=True
    )
    inject, own_dual, level = small(
        unpack_kernel,
        "unpack",
        [
            jax.ShapeDtypeStruct((hour_rows, bus_count // width, width), jnp.float32),
            jax.ShapeDtypeStruct((hour_rows, line_count // width, width), jnp.float32),
            jax.ShapeDtypeStruct((hour_rows, unit_rows, width), jnp.float32),
        ],
        [back],
    )
    inject = inject.reshape(hour_rows, bus_count)
    own_dual = own_dual.reshape(hour_rows, line_count)
    level = level.reshape(hour_rows, units)
    return (inject, own_dual, level)


def solution(mesh):
    in_specs = (
        P(("scen", "tm"), None),
        P(None, "tm", None, None),
        P(None, "tm"),
        P(),
        P(),
        P(),
        P(("scen", "tm"), None),
    )
    out_specs = (P(("scen", "tm"), None), P(("scen", "tm"), None), P(("scen", "tm"), None))
    return jax.shard_map(shards, mesh=mesh, in_specs=in_specs, out_specs=out_specs, check_vma=False)
```

```python
import jax
import jax.numpy as jnp
from jax import lax
from jax.experimental import pallas as pl
from jax.experimental.pallas import tpu as pltpu
from jax.sharding import PartitionSpec as P

ITERS = 2


step_size = 0.5
penalty = 4.0
ramp_weight = 0.5

NT = (((1,), (1,)), ((), ()))
VMEM = pl.BlockSpec(memory_space=pltpu.VMEM)
HBM = pl.BlockSpec(memory_space=pl.ANY)
SMALL = pltpu.CompilerParams(vmem_limit_bytes=12 << 20)
STRAIGHT = 64


class Half:
    def __init__(self, sibling, hbm, tiles, blocks, block_sem, sems=None, head=None):
        me = lax.axis_index("tm")
        self.core = 1 - me % 2 if sibling else me % 2
        self.tiles, self.head, self.blocks, self.sems = tiles, head, blocks, sems
        self.blocks_hbm, self.tiles_hbm = hbm
        self.chunks = lax.axis_size("tm") // 2
        ahead_groups = 0 if head is None else head.shape[0]
        self.own = (ahead_groups + tiles.shape[0]) // self.chunks
        self.ahead = ahead_groups // self.own
        self.depth, self.lines, self.width = tiles.shape[1:]
        if sems is not None:
            for chunk in range(self.ahead, self.chunks):
                self.fetch(chunk).start()
        self.block_copy = pltpu.make_async_copy(self.blocks_hbm, blocks, block_sem)
        self.block_copy.start()

    def first_group(self, chunk):
        return (2 * chunk + self.core) * self.own

    def fetch(self, chunk):
        there = pl.ds(self.first_group(chunk), self.own)
        here = pl.ds((chunk - self.ahead) * self.own, self.own)
        return pltpu.make_async_copy(self.tiles_hbm.at[there], self.tiles.at[here], self.sems.at[chunk])

    def each_four(self, wait, four):
        rest = self.chunks - self.ahead
        per = max(n for n in range(1, rest + 1) if rest % n == 0 and n * self.own <= max(STRAIGHT, self.own))

        def one(chunk, ref, at):
            for sub in range(0, self.own, 4):
                first = (self.first_group(chunk) + sub) * self.depth
                four(
                    lambda u, k: ref[at + sub + u, k],
                    chunk * self.own + sub,
                    lambda u, k: self.blocks[first + u * self.depth + k],
                )

        def body(step, carry):
            for c in range(per):
                chunk = self.ahead + step * per + c
                if wait and self.sems is not None:
                    self.fetch(chunk).wait()
                one(chunk, self.tiles, (chunk - self.ahead) * self.own)
            return carry

        if wait:
            self.block_copy.wait()
        for chunk in range(self.ahead):
            one(chunk, self.head, chunk * self.own)
        if per == rest:
            body(0, 0)
        else:
            lax.fori_loop(0, rest // per, body, 0)


class Ahead:
    def __init__(self, half, head, sem):
        self.copies = []
        for chunk in range(head.shape[0] // half.own):
            there = pl.ds((2 * chunk + 1 - half.core) * half.own, half.own)
            here = pl.ds(chunk * half.own, half.own)
            self.copies.append(pltpu.make_async_copy(half.tiles_hbm.at[there], head.at[here], sem.at[chunk]))
            self.copies[-1].start()

    def wait(self):
        for copy in self.copies:
            copy.wait()


def wide(parts):
    return jnp.concatenate([jnp.concatenate(row, axis=1) for row in parts], axis=0)


def flow_pass(picked, half, flows, wait):
    depth = half.depth
    hours = picked.shape[1]
    even = depth - depth % 2

    def side(parts):
        return jnp.concatenate(parts, axis=1)

    def four(tile, g, block):
        rows = [[picked[block(u, k)] for k in range(depth)] for u in range(4)]
        zero = jnp.zeros_like(rows[0][0])
        for first in (0, 2):
            totals = [
                lax.dot_general(
                    side(rows[first + u][:even]),
                    side([tile(first + u, k) for k in range(even)]),
                    NT,
                    preferred_element_type=jnp.float32,
                )
                for u in range(2)
            ]
            if depth % 2:
                left = wide([[rows[first][even], zero], [zero, rows[first + 1][even]]])
                right = side([tile(first, even), tile(first + 1, even)])
                part = lax.dot_general(left, right, NT, preferred_element_type=jnp.float32)
                totals = [totals[u] + part[u * hours : (u + 1) * hours] for u in range(2)]
            for u in range(2):
                flows[g + first + u] = totals[u].astype(flows.dtype)

    half.each_four(wait, four)


def price_pass(dual, half, sums, wait):
    depth, width = half.depth, half.width
    hours = dual.shape[1]
    even = depth - depth % 2
    for ref in sums:
        ref[...] = jnp.zeros_like(ref)

    def four(tile, g, block):
        rows = [dual[g + u] for u in range(4)]
        parts = []
        for first in (0, 2):
            for u in (first, first + 1):
                right = jnp.concatenate([tile(u, k) for k in range(even)], axis=1)
                part = jnp.dot(rows[u], right, preferred_element_type=jnp.float32)
                parts += [(u, k, part[:, k * width : (k + 1) * width]) for k in range(even)]
            if depth % 2:
                left = jnp.concatenate(rows[first : first + 2], axis=0)
                right = jnp.concatenate([tile(first, even), tile(first + 1, even)], axis=1)
                part = jnp.dot(left, right, preferred_element_type=jnp.float32)
                for u in range(2):
                    parts.append((first + u, even, part[u * hours : (u + 1) * hours, u * width : (u + 1) * width]))
        for u, k, part in parts:
            at = block(u, k)
            sums[k][at] = sums[k][at] + part

    half.each_four(wait, four)


def earlier(values):
    return jnp.concatenate([values[-1:], values[:-1]], axis=0)


def later(values):
    return jnp.concatenate([values[1:], values[:1]], axis=0)


def total(sums, block):
    price = sums[0][block]
    for ref in sums[1:]:
        price = price + ref[block]
    return price


def update_pass(sums, before, inject, base, delta, price_out, out):
    for block in range(sums[0].shape[0]):
        price = before[block] + total(sums, block)
        price_out[block] = price
        now = inject(block)
        new = now - step_size * (
            (now - base(block))
            + penalty * price
            + ramp_weight * (2.0 * now - earlier(now) - later(now))
        )
        out(block, new - delta[block])


def one_hot(unit_lane, cols, width):
    lane = jnp.broadcast_to(unit_lane[:, cols], (width, cols.size))
    return (lane == lax.broadcasted_iota(jnp.int32, (width, cols.size), 0)).astype(jnp.bfloat16)


def high_low(values, axis):
    high = values.astype(jnp.bfloat16)
    low = (values - high.astype(jnp.float32)).astype(jnp.bfloat16)
    return jnp.concatenate([high, low], axis=axis)


def storage_pass(level, unit_block, unit_lane, delta, gain=None, price=None, out=None):
    hours = level.shape[0]
    count, _, width = (price if delta is None else delta).shape
    span = 2 * width
    if price is not None:
        prices = high_low(jnp.concatenate([price[b] for b in range(count)], axis=0), 1)
    if delta is not None:
        delta[...] = jnp.zeros_like(delta)

    for c in range(level.shape[1] // span):
        cols = pl.ds(c * span, span)
        hot = one_hot(unit_lane, cols, width)
        block = jnp.broadcast_to(unit_block[:, cols], (hours, span))
        here = [block == b for b in range(count)]
        now = level[:, cols]
        if price is not None:
            picked = jnp.dot(prices, jnp.concatenate([hot, hot], axis=0), preferred_element_type=jnp.float32)
            found = jnp.zeros((hours, span), jnp.float32)
            for b in range(count):
                found = jnp.where(here[b], picked[b * hours : (b + 1) * hours], found)
            now = 0.5 * (now + earlier(now)) - gain[:, cols] * found
            if delta is None:
                now = jnp.where((block >= 0) & (block < count), now, 0.0)
            out[:, cols] = now
        if delta is not None:
            charge = step_size * (now - earlier(now))
            held = jnp.concatenate([jnp.where(here[b], charge, 0.0) for b in range(count)], axis=0)
            part = lax.dot_general(held.astype(jnp.bfloat16), hot, NT, preferred_element_type=jnp.float32)
            for b in range(count):
                delta[b] = delta[b] + part[b * hours : (b + 1) * hours]


def pack_kernel(base, soc, out):
    devices, rows, width = out.shape
    hour_rows, units = soc.shape[0], soc.shape[1]
    count = base.shape[1] // devices
    pad = jnp.zeros((rows // hour_rows - count - units, width), jnp.float32)
    for d in range(devices):
        parts = []
        for r in range(hour_rows):
            parts += [base[r, d * count : (d + 1) * count], soc[r], pad]
        out[d] = jnp.concatenate(parts, axis=0).astype(out.dtype)


def first_flow_kernel(
    blocks_hbm, tiles_hbm, came, flows, picked, level, head, tiles, blocks, block_sem, sems, ahead_sem, flat
):
    half = Half(True, (blocks_hbm, tiles_hbm), tiles, blocks, block_sem, sems)
    ahead = Ahead(half, head, ahead_sem)
    count, hours, width = picked.shape
    flat[...] = came[...].astype(jnp.float32)
    rows = flat.shape[0] // hours
    for b in range(count):
        picked[b] = flat[pl.ds(b, hours, stride=rows), :].astype(picked.dtype)
    for c in range(level.shape[1] // width):
        level[:, c * width : (c + 1) * width] = flat[pl.ds(count + c, hours, stride=rows), :]
    flow_pass(picked, half, flows, True)
    ahead.wait()


def own_flow_kernel(blocks_hbm, tiles_hbm, picked, head, flows, tiles, blocks, block_sem, sems):
    flow_pass(picked, Half(False, (blocks_hbm, tiles_hbm), tiles, blocks, block_sem, sems, head), flows, True)


def held_flow_kernel(blocks_hbm, head, tiles, picked, flows, blocks, block_sem):
    flow_pass(picked, Half(False, (blocks_hbm, None), tiles, blocks, block_sem, head=head), flows, True)


def own_price(half, dual, price, sums):
    price_pass(dual, half, sums, True)
    for b in range(price.shape[0]):
        price[b] = total(sums, b)


def own_price_kernel(
    blocks_hbm, head, tiles, dual, level, unit_block, unit_lane, before, delta, blocks, block_sem, *sums
):
    half = Half(False, (blocks_hbm, None), tiles, blocks, block_sem, head=head)
    storage_pass(level, unit_block, unit_lane, delta)
    own_price(half, dual, before, sums)


def own_price_level_kernel(
    blocks_hbm, head, tiles, dual, price, level, unit_block, unit_lane, gain, before, level_out, delta,
    blocks, block_sem, *sums
):
    half = Half(False, (blocks_hbm, None), tiles, blocks, block_sem, head=head)
    storage_pass(level, unit_block, unit_lane, delta, gain, price, level_out)
    own_price(half, dual, before, sums)


def middle_kernel(
    blocks_hbm, tiles, dual, before, base, delta, price, inject_out, picked, flows, blocks, block_sem, *sums
):
    half = Half(True, (blocks_hbm, None), tiles, blocks, block_sem)
    price_pass(dual, half, sums, True)

    def start(b):
        return base[b].astype(jnp.float32)

    def write(b, new):
        inject_out[b] = new
        picked[b] = new.astype(picked.dtype)

    update_pass(sums, before, start, start, delta, price, write)
    flow_pass(picked, half, flows, False)


def last_kernel(
    blocks_hbm, tiles, dual, before, base, inject, delta, level, line_dual, unit_block, unit_lane, gain,
    out, blocks, block_sem, price, level_out, flat, *sums
):
    half = Half(True, (blocks_hbm, None), tiles, blocks, block_sem)
    count, hours, width = price.shape
    rows = flat.shape[0] // hours
    flat[...] = jnp.zeros_like(flat)
    units = level.shape[1] // width
    for g in range(line_dual.shape[0]):
        flat[pl.ds(count + units + g, hours, stride=rows), :] = line_dual[g]
    price_pass(dual, half, sums, True)

    def start(b):
        return base[b].astype(jnp.float32)

    def write(b, new):
        flat[pl.ds(b, hours, stride=rows), :] = new

    update_pass(sums, before, lambda b: inject[b], start, delta, price, write)
    storage_pass(level, unit_block, unit_lane, None, gain, price, level_out)
    for c in range(units):
        flat[pl.ds(count + c, hours, stride=rows), :] = level_out[:, c * width : (c + 1) * width]
    out[...] = flat[...].astype(out.dtype)


def unpack_kernel(back, inject, line_dual, level):
    devices = back.shape[0]
    hour_rows, units = level.shape[0], level.shape[1]
    count, own = inject.shape[1] // devices, line_dual.shape[1] // devices
    rows = back.shape[1] // hour_rows
    for r in range(hour_rows):
        sum_levels = None
        for d in range(devices):
            came = back[d, r * rows : (r + 1) * rows].astype(jnp.float32)
            inject[r, d * count : (d + 1) * count] = came[:count]
            line_dual[r, d * own : (d + 1) * own] = came[count + units : count + units + own]
            part = came[count : count + units]
            sum_levels = part if sum_levels is None else sum_levels + part
        level[r] = sum_levels


def shards(base_injection, ptdf_tiles, tile_block, limits, stor_bus, stor_gain, soc_init):
    hour_rows = base_injection.shape[0]
    bus_count = base_injection.shape[1]
    line_count = limits.shape[0]
    groups, depth, lines, width = ptdf_tiles.shape
    units = stor_bus.shape[0]
    devices = lax.axis_size("tm")
    me = lax.axis_index("tm")
    buses = bus_count // devices
    bus_blocks = buses // width
    hours = hour_rows * devices
    own_groups = groups // devices
    blocks = tile_block.reshape(groups * depth)
    unit_block = (stor_bus // width - me * bus_blocks).reshape(1, units)
    unit_lane = (stor_bus % width).reshape(1, units)
    gain = stor_gain.reshape(1, units)
    own_limits = lax.dynamic_slice_in_dim(limits.reshape(groups, 1, lines), me * own_groups, own_groups, 0)

    chips = devices // 2
    half_groups = chips * own_groups
    sibling = [(d, d + 1 - 2 * (d % 2)) for d in range(devices)]

    same_core = [[2 * chip + c for chip in range(chips)] for c in range(2)]

    def exchange(value):
        return lax.all_to_all(value, "tm", split_axis=0, concat_axis=0, axis_index_groups=same_core, tiled=True)

    half_bytes = ptdf_tiles.size
    half_flops = hours * ptdf_tiles.size
    ahead = max(1, 3 * chips // 8)

    def tile_shape(chunks):
        return jax.ShapeDtypeStruct((chunks * own_groups, *ptdf_tiles.shape[1:]), ptdf_tiles.dtype)

    def scratch(shape):
        return pltpu.VMEM(shape.shape, shape.dtype)

    picked_shape = jax.ShapeDtypeStruct((bus_blocks, hours, width), jnp.bfloat16)
    block_shape = jax.ShapeDtypeStruct((bus_blocks, hours, width), jnp.float32)
    level_shape = jax.ShapeDtypeStruct((hours, units), jnp.float32)
    flow_shape = jax.ShapeDtypeStruct((half_groups, hours, lines), jnp.float32)
    head_shape, half_shape, rest_shape = tile_shape(ahead), tile_shape(chips), tile_shape(chips - ahead)
    sems, ahead_sems = pltpu.SemaphoreType.DMA((chips,)), pltpu.SemaphoreType.DMA((ahead,))
    sums = [scratch(block_shape)] * depth

    def product(kernel, name, outs, operands, temporary, passes=1, hbm=(), limit=16):
        return pl.pallas_call(
            kernel,
            out_shape=outs,
            in_specs=[HBM] * (1 + len(hbm)) + [VMEM] * len(operands),
            out_specs=[VMEM] * len(outs),
            scratch_shapes=[pltpu.SMEM(blocks.shape, blocks.dtype), pltpu.SemaphoreType.DMA, *temporary],
            compiler_params=pltpu.CompilerParams(vmem_limit_bytes=limit << 20),
            cost_estimate=pl.CostEstimate(
                flops=passes * half_flops, bytes_accessed=passes * half_bytes, transcendentals=0
            ),
            name=name,
        )(blocks, *hbm, *operands)

    def small(kernel, name, outs, operands):
        return pl.pallas_call(
            kernel,
            out_shape=outs,
            in_specs=[VMEM] * len(operands),
            out_specs=[VMEM] * len(outs),
            compiler_params=SMALL,
            cost_estimate=pl.CostEstimate(flops=half_flops, bytes_accessed=4 << 20, transcendentals=0),
            name=name,
        )(*operands)

    unit_rows = units // width

    def whole_tiles(rows):
        return -(-rows // 16) * 16

    rows_in = whole_tiles(bus_blocks + unit_rows)
    rows_out = whole_tiles(bus_blocks + unit_rows + own_groups)
    (sent,) = small(
        pack_kernel,
        "pack",
        [jax.ShapeDtypeStruct((devices, hour_rows * rows_in, width), jnp.bfloat16)],
        [
            base_injection.astype(jnp.float32).reshape(hour_rows, bus_count // width, width),
            soc_init.reshape(hour_rows, unit_rows, width),
        ],
    )
    came = lax.all_to_all(sent, "tm", split_axis=0, concat_axis=0, tiled=True)
    came, high, low, unit_block, unit_lane, gain, blocks = lax.optimization_barrier(
        (came, own_limits, -own_limits, unit_block, unit_lane, gain, blocks)
    )
    away, base, level, head, other_half = product(
        first_flow_kernel,
        "first_flow",
        [flow_shape, picked_shape, level_shape, head_shape, half_shape],
        [came.reshape(hours * rows_in, width)],
        [sems, ahead_sems, pltpu.VMEM((hours * rows_in, width), jnp.float32)],
        hbm=[ptdf_tiles],
        limit=36,
    )
    picked = base
    price = None
    line_dual = jnp.zeros((own_groups, hours, lines), jnp.float32)
    for iteration in range(ITERS):
        arrived = lax.ppermute(away, "tm", sibling)
        if iteration == 0:
            flows, rest = product(
                own_flow_kernel,
                "own_flow",
                [flow_shape, rest_shape],
                [picked, head],
                [sems],
                hbm=[ptdf_tiles],
                limit=28,
            )
        else:
            (flows,) = product(held_flow_kernel, "held_flow", [flow_shape], [head, rest, picked], [])
        pair = (flows + arrived).astype(jnp.bfloat16).reshape(chips, own_groups, hours, lines)
        parts = exchange(pair)
        shifted = jnp.sum(parts.astype(jnp.float32), axis=0) + line_dual
        clipped = jnp.clip(shifted, low, high)
        line_dual = shifted - clipped
        dual = exchange(jnp.broadcast_to(line_dual.astype(jnp.bfloat16)[None], (chips, own_groups, hours, lines)))
        dual = dual.reshape(half_groups, hours, lines)
        other = lax.ppermute(dual, "tm", sibling)
        if iteration < ITERS - 1:
            before, delta = product(
                own_price_kernel,
                "own_price",
                [block_shape, block_shape],
                [head, rest, dual, level, unit_block, unit_lane],
                sums,
            )
            price, inject, picked, away = product(
                middle_kernel,
                "price_then_flow",
                [block_shape, block_shape, picked_shape, flow_shape],
                [other_half, other, before, base, delta],
                sums,
                2,
            )
        else:
            before, level, delta = product(
                own_price_level_kernel,
                "own_price",
                [block_shape, level_shape, block_shape],
                [head, rest, dual, price, level, unit_block, unit_lane, gain],
                sums,
            )
            (out,) = product(
                last_kernel,
                "last_price",
                [jax.ShapeDtypeStruct((hours * rows_out, width), jnp.bfloat16)],
                [other_half, other, before, base, inject, delta, level, line_dual, unit_block, unit_lane, gain],
                [
                    scratch(block_shape),
                    scratch(level_shape),
                    pltpu.VMEM((hours * rows_out, width), jnp.float32),
                ]
                + sums,
            )

    back = lax.all_to_all(
        out.reshape(devices, hour_rows * rows_out, width), "tm", split_axis=0, concat_axis=0, tiled=True
    )
    inject, own_dual, level = small(
        unpack_kernel,
        "unpack",
        [
            jax.ShapeDtypeStruct((hour_rows, bus_count // width, width), jnp.float32),
            jax.ShapeDtypeStruct((hour_rows, line_count // width, width), jnp.float32),
            jax.ShapeDtypeStruct((hour_rows, unit_rows, width), jnp.float32),
        ],
        [back],
    )
    inject = inject.reshape(hour_rows, bus_count)
    own_dual = own_dual.reshape(hour_rows, line_count)
    level = level.reshape(hour_rows, units)
    return (inject, own_dual, level)


def solution(mesh):
    in_specs = (
        P(("scen", "tm"), None),
        P(None, "tm", None, None),
        P(None, "tm"),
        P(),
        P(),
        P(),
        P(("scen", "tm"), None),
    )
    out_specs = (P(("scen", "tm"), None), P(("scen", "tm"), None), P(("scen", "tm"), None))
    return jax.shard_map(shards, mesh=mesh, in_specs=in_specs, out_specs=out_specs, check_vma=False)
```
